128 devices in a mesh: row: 8 (over x, z_hi), col: 8 (over y, z_lo), dp: 2 (over core).
Axes of the slice: x: 4, y: 4, z: 4 (z_hi: 2, z_lo: 2; z = z_hi * 2 + z_lo), core: 2. Of those that a mesh axis runs over, the one named last changes fastest.
Arguments:
- hid_query: bfloat16 [16384, 4096], P(('row', 'col', 'dp')), may hold values from -6 to 6
- hid_key: bfloat16 [16384, 4096], P(('row', 'col', 'dp')), may hold values from -6 to 6
- projection: bfloat16 [4096, 1024], replicated, may hold values from -0.09375 to 0.09375
- tile_rows: int32 [8, 8, 48], P('row', 'col'), may hold values from 0 to 7, as said below
- tile_cols: int32 [8, 8, 48], P('row', 'col'), may hold values from 0 to 7, as said below
- tile_count: int32 [8, 8], P('row', 'col'), may hold values from 1 to 48, as said below
- positive: int32 [16384], P(('row', 'col', 'dp')), may hold values from 0 to 16383, as said below
Outputs:
- grad_projection: float32 [4096, 1024], P(('row', 'col', 'dp'))
The draws below stay inside these ranges and needn't reach their ends.
Inputs may be any that keep to these rules, and one draw needn't show every extreme that they name: Entry s of cell (r, c) names tile (tile_rows, tile_cols); the 48 entries of one cell name distinct tiles. `tile_cols`: see tile_rows. `tile_count`: some cell of every draw uses all 48 entries. `positive`: maps each device's 128 documents one to one onto the same device's documents.
All inputs are finite; a program needn't handle non-finite values.
Results may differ from the reference program's by a relative error of at most 0.0095.
Values may be sent and summed in bfloat16 or wider, within the bound.
No kernel may reach another device: no remote copies, remote signals or barrier semaphores. Data moves between devices by JAX's collectives and lax.ppermute only.
A program may use at most 128 MiB of HBM per device.

```python
import jax
import jax.numpy as jnp
from jax import lax

D = 4096
P_SIZE = 1024
TILE = 256
DOC_DEV = 128
NDOC = 16384
ROWBLK = 2048
COLBLK = 2048
TROWS = 8
TCOLS = 8
SLOTS = 48
N_ROW = 8
N_COL = 8
N_DP = 2


def tile_layout(key):
    cell_keys = jax.random.split(key, N_ROW * N_COL)
    orders = jax.vmap(lambda one: jax.random.permutation(one, TROWS * TCOLS))(cell_keys)
    return orders[:, :SLOTS].reshape(N_ROW, N_COL, SLOTS).astype(jnp.int32)


def draw_tile_rows(key, part):
    layout = tile_layout(key)
    return (layout // TCOLS).astype(jnp.int32)


def draw_tile_cols(key, part):
    layout = tile_layout(key)
    return (layout % TCOLS).astype(jnp.int32)


def draw_tile_count(key, part):
    key = jax.random.fold_in(key, 5)
    count_key, full_key = jax.random.split(key)
    counts = jax.random.randint(count_key, (N_ROW * N_COL,), 1, SLOTS + 1)
    fullest = jax.random.randint(full_key, (), 0, N_ROW * N_COL)
    counts = counts.at[fullest].set(SLOTS)
    return counts.reshape(N_ROW, N_COL).astype(jnp.int32)


def draw_positive(key, part):
    key = jax.random.fold_in(key, 7)
    blocks = NDOC // DOC_DEV
    block_keys = jax.random.split(key, blocks)
    orders = jax.vmap(lambda one: jax.random.permutation(one, DOC_DEV))(block_keys)
    offsets = jnp.arange(blocks, dtype=jnp.int32)[:, None] * DOC_DEV
    return (orders.astype(jnp.int32) + offsets).reshape(NDOC).astype(jnp.int32)


def levels(stream_key, shape, cuts, smallest, top_value):
    loudness, own = 1.0, jax.random.fold_in(stream_key, 6)
    for dim, parts in cuts:
        steps = jnp.exp(jax.random.uniform(jax.random.fold_in(own, dim), (parts,), jnp.float32, smallest / len(cuts), top_value / len(cuts)))
        loudness = loudness * jnp.repeat(steps, shape[dim] // parts).reshape([-1 if axis == dim else 1 for axis in range(len(shape))])
    return loudness


def centred(rng, dims, spread, bound, cuts=(), kind=jnp.bfloat16):
    entries = jax.random.normal(rng, dims, jnp.float32) * spread
    if len(cuts) > 0:
        entries = levels(rng, dims, cuts, -0.22, 0.18) * entries
    return jnp.clip(entries, min=-bound, max=bound).astype(kind)


def setup_inputs(seed: int = 0) -> dict:
    seeds = jax.random.split(jax.random.key(seed), 8)
    return {
        "hid_query": centred(seeds[0], (NDOC, D), 1.0, 6.0, ((0, 128),)),
        "hid_key": centred(seeds[1], (NDOC, D), 1.0, 6.0, ((0, 128),)),
        "projection": centred(seeds[2], (D, P_SIZE), D ** -0.5, 0.09375),
        "tile_rows": draw_tile_rows(jax.random.fold_in(seeds[7], 71), 0),
        "tile_cols": draw_tile_cols(jax.random.fold_in(seeds[7], 71), 0),
        "tile_count": draw_tile_count(jax.random.fold_in(seeds[7], 71), 0),
        "positive": draw_positive(jax.random.fold_in(seeds[7], 71), 0),
    }


TAU_INV = 20.0
EPS = 1e-06

def unit_rows(raw):
    values = raw.astype(jnp.float32)
    scale = lax.rsqrt(lax.optimization_barrier(jnp.sum(values * values, axis=1, keepdims=True)) + EPS)
    return (values * scale, scale)

def to_columns(values):
    return values.reshape(N_ROW, N_COL, N_DP * DOC_DEV, -1).transpose(1, 0, 2, 3).reshape(N_COL, COLBLK, -1)

def from_columns(values):
    return values.reshape(N_COL, N_ROW, N_DP * DOC_DEV, -1).transpose(1, 0, 2, 3).reshape(NDOC, -1)

def reference(hid_query, hid_key, projection, tile_rows, tile_cols, tile_count, positive):
    query_raw = jnp.dot(hid_query, projection, preferred_element_type=jnp.float32).astype(jnp.bfloat16)
    key_raw = jnp.dot(hid_key, projection, preferred_element_type=jnp.float32).astype(jnp.bfloat16)
    query_exact, query_scale = unit_rows(query_raw)
    key_exact, key_scale = unit_rows(key_raw)
    query_unit = query_exact.astype(jnp.bfloat16)
    key_unit = key_exact.astype(jnp.bfloat16)
    paired = key_unit[positive]
    pos_score = lax.optimization_barrier(jnp.sum(query_unit.astype(jnp.float32) * paired.astype(jnp.float32), axis=1)) * TAU_INV
    query_grid = query_unit.reshape(N_ROW, ROWBLK, P_SIZE)
    key_grid = to_columns(key_unit)
    total_steps = N_ROW * N_COL * SLOTS
    zero = jnp.zeros((), jnp.int32)

    def locate(flat):
        flat = jnp.asarray(flat).astype(jnp.int32)
        cell = (flat // SLOTS).astype(jnp.int32)
        entry = (flat % SLOTS).astype(jnp.int32)
        grid_row = (cell // N_COL).astype(jnp.int32)
        grid_col = (cell % N_COL).astype(jnp.int32)
        tile_row = tile_rows[grid_row, grid_col, entry].astype(jnp.int32)
        tile_col = tile_cols[grid_row, grid_col, entry].astype(jnp.int32)
        valid = entry < tile_count[grid_row, grid_col]
        return (grid_row, grid_col, (tile_row * TILE).astype(jnp.int32), (tile_col * TILE).astype(jnp.int32), valid)

    def scores_of(grid_row, grid_col, row_start, col_start):
        query_tile = lax.dynamic_slice(query_grid, (grid_row, row_start, zero), (1, TILE, P_SIZE))[0]
        key_tile = lax.dynamic_slice(key_grid, (grid_col, col_start, zero), (1, TILE, P_SIZE))[0]
        score = jnp.dot(query_tile, key_tile.T, preferred_element_type=jnp.float32) * TAU_INV
        return (query_tile, key_tile, score)

    def first_pass(flat, carry):
        grid_row, grid_col, row_start, col_start, valid = locate(flat)

        def accumulate(sums):
            row_sum, col_sum = sums
            _, _, score = scores_of(grid_row, grid_col, row_start, col_start)
            expo = jnp.exp(score)
            row_old = lax.dynamic_slice(row_sum, (grid_row, row_start), (1, TILE))
            row_sum = lax.dynamic_update_slice(row_sum, row_old + lax.optimization_barrier(jnp.sum(expo, axis=1))[None], (grid_row, row_start))
            col_old = lax.dynamic_slice(col_sum, (grid_col, col_start), (1, TILE))
            col_sum = lax.dynamic_update_slice(col_sum, col_old + lax.optimization_barrier(jnp.sum(expo, axis=0))[None], (grid_col, col_start))
            return (row_sum, col_sum)
        return lax.cond(valid, accumulate, lambda sums: sums, carry)
    row_sum, col_sum = lax.fori_loop(0, total_steps, first_pass, (jnp.zeros((N_ROW, ROWBLK), jnp.float32), jnp.zeros((N_COL, COLBLK), jnp.float32)))
    pos_exp = jnp.exp(pos_score)
    row_log = jnp.log(row_sum.reshape(NDOC) + pos_exp)
    col_log = jnp.log(from_columns(col_sum[..., None])[:, 0] + jnp.zeros((NDOC,), jnp.float32).at[positive].add(pos_exp))
    row_grid = row_log.reshape(N_ROW, ROWBLK)
    col_grid = to_columns(col_log[:, None])[..., 0]

    def second_pass(flat, carry):
        grid_row, grid_col, row_start, col_start, valid = locate(flat)

        def accumulate(grads):
            query_acc, key_acc = grads
            query_tile, key_tile, score = scores_of(grid_row, grid_col, row_start, col_start)
            row_part = lax.dynamic_slice(row_grid, (grid_row, row_start), (1, TILE))[0]
            col_part = lax.dynamic_slice(col_grid, (grid_col, col_start), (1, TILE))[0]
            weight = (jnp.exp(score - row_part[:, None]) + jnp.exp(score - col_part[None, :])).astype(jnp.bfloat16)
            query_add = jnp.dot(weight, key_tile, preferred_element_type=jnp.float32) * TAU_INV
            key_add = jnp.dot(weight.T, query_tile, preferred_element_type=jnp.float32) * TAU_INV
            query_old = lax.dynamic_slice(query_acc, (grid_row, row_start, zero), (1, TILE, P_SIZE))
            query_acc = lax.dynamic_update_slice(query_acc, query_old + query_add[None], (grid_row, row_start, zero))
            key_old = lax.dynamic_slice(key_acc, (grid_col, col_start, zero), (1, TILE, P_SIZE))
            key_acc = lax.dynamic_update_slice(key_acc, key_old + key_add[None], (grid_col, col_start, zero))
            return (query_acc, key_acc)
        return lax.cond(valid, accumulate, lambda grads: grads, carry)
    query_acc, key_acc = lax.fori_loop(0, total_steps, second_pass, (jnp.zeros((N_ROW, ROWBLK, P_SIZE), jnp.float32), jnp.zeros((N_COL, COLBLK, P_SIZE), jnp.float32)))
    pos_weight = jnp.exp(pos_score - row_log) + jnp.exp(pos_score - col_log[positive]) - 2.0
    grad_query = query_acc.reshape(NDOC, P_SIZE) + pos_weight[:, None] * paired.astype(jnp.float32) * TAU_INV
    grad_key = from_columns(key_acc) + jnp.zeros((NDOC, P_SIZE), jnp.float32).at[positive].add(pos_weight[:, None] * query_unit.astype(jnp.float32) * TAU_INV)
    query_back = (query_scale * (grad_query - query_exact * lax.optimization_barrier(jnp.sum(query_exact * grad_query, axis=1, keepdims=True)))).astype(jnp.bfloat16)
    key_back = (key_scale * (grad_key - key_exact * lax.optimization_barrier(jnp.sum(key_exact * grad_key, axis=1, keepdims=True)))).astype(jnp.bfloat16)
    grad_projection = jnp.dot(hid_query.T, query_back, preferred_element_type=jnp.float32)
    grad_projection = grad_projection + jnp.dot(hid_key.T, key_back, preferred_element_type=jnp.float32)
    return grad_projection
```

```python
import jax
import jax.numpy as jnp
from jax import lax
from jax.experimental import pallas as pl
from jax.experimental.pallas import tpu as pltpu
from jax.sharding import PartitionSpec as P

TAU_INV = 20.0
EPS = 1e-06
DOCS = 128
EMB = 1024
HID = 4096
NX = 384
NY = 384
NZ = 256
NA = 640
NB = EMB - NA
BF = jnp.bfloat16
F32 = jnp.float32
VM = 56 * 1024 * 1024


def ring_pair(step, flip):
    return [(i, ((i // 2 + step) % 4) * 2 + ((i % 2) ^ flip)) for i in range(8)]


def move_query(value, step, flip):
    return lax.ppermute(value, "col", ring_pair(step, flip))


def move_key(value, step, flip):
    return lax.ppermute(value, "row", ring_pair(step, flip))


def move_x(value, step):
    return lax.ppermute(value, "row", ring_pair(step, 0))


def move_y(value, step):
    return lax.ppermute(value, "col", ring_pair(step, 0))


def move_z(value, step):
    pairs = []
    for r in range(8):
        for c in range(8):
            z = ((r % 2) * 2 + c % 2 + step) % 4
            pairs.append((r * 8 + c, ((r // 2) * 2 + z // 2) * 8 + (c // 2) * 2 + z % 2))
    return lax.ppermute(value, ("row", "col"), pairs)


def swap(value):
    return lax.ppermute(value, "dp", [(0, 1), (1, 0)])


def params():
    return pltpu.CompilerParams(vmem_limit_bytes=VM)


def sds(shape, dtype):
    return jax.ShapeDtypeStruct(shape, dtype)


ANY = pl.BlockSpec(memory_space=pl.ANY)
SMEM = pl.BlockSpec(memory_space=pltpu.SMEM)
VMEM = pl.BlockSpec(memory_space=pltpu.VMEM)


def dot(a, b):
    return lax.dot_general(a, b, (((1,), (0,)), ((), ())), preferred_element_type=F32)


def dot_t(a, b):
    return lax.dot_general(a, b, (((1,), (1,)), ((), ())), preferred_element_type=F32)


def t_dot(a, b):
    return lax.dot_general(a, b, (((0,), (0,)), ((), ())), preferred_element_type=F32)


def unit_of(raw):
    values = raw.astype(F32)
    scale = lax.rsqrt(jnp.sum(values * values, axis=1, keepdims=True) + EPS)
    return values * scale, scale


def project_body(hq, hk, proj, q_unit, k_unit, q_raw, k_raw, acc):
    step = pl.program_id(0)

    @pl.when(step == 0)
    def _():
        acc[...] = jnp.zeros_like(acc)

    acc[:DOCS, :] += dot(hq[...], proj[...])
    acc[DOCS:, :] += dot(hk[...], proj[...])

    @pl.when(step == pl.num_programs(0) - 1)
    def _():
        for raw_ref, unit_ref, start in ((q_raw, q_unit, 0), (k_raw, k_unit, DOCS)):
            raw = acc[start : start + DOCS, :].astype(BF)
            raw_ref[...] = raw
            unit_ref[...] = unit_of(raw)[0].astype(BF)


def project(hid_query, hid_key, projection):
    depth = 512
    whole = pl.BlockSpec((DOCS, EMB), lambda i: (0, 0))
    return pl.pallas_call(
        project_body,
        grid=(HID // depth,),
        in_specs=[
            pl.BlockSpec((DOCS, depth), lambda i: (0, i)),
            pl.BlockSpec((DOCS, depth), lambda i: (0, i)),
            pl.BlockSpec((depth, EMB), lambda i: (i, 0)),
        ],
        out_specs=[whole] * 4,
        out_shape=[sds((DOCS, EMB), BF)] * 4,
        scratch_shapes=[pltpu.VMEM((2 * DOCS, EMB), F32)],
        compiler_params=params(),
    )(hid_query, hid_key, projection)


def one_hot(pos):
    lane = lax.broadcasted_iota(jnp.int32, (DOCS, DOCS), 1)
    return (lane == pos).astype(F32)


def eye():
    lane = lax.broadcasted_iota(jnp.int32, (DOCS, DOCS), 1)
    row = lax.broadcasted_iota(jnp.int32, (DOCS, DOCS), 0)
    return (lane == row).astype(F32)


def pairs_body(q_unit, k_unit, pos, paired, q_perm, pos_rows):
    hot = one_hot(pos[...])
    hot_bf = hot.astype(BF)
    pair = dot(hot_bf, k_unit[...])
    paired[...] = pair.astype(BF)
    q_perm[...] = t_dot(hot_bf, q_unit[...]).astype(BF)
    score = jnp.sum(q_unit[...].astype(F32) * pair, axis=1, keepdims=True) * TAU_INV
    expo = jnp.exp(score)
    pos_rows[0:1, :] = jnp.sum(eye() * expo, axis=0, keepdims=True)
    pos_rows[1:2, :] = jnp.sum(hot * expo, axis=0, keepdims=True)
    pos_rows[2:8, :] = jnp.zeros((6, DOCS), F32)


def pair_up(q_unit, k_unit, pos):
    return pl.pallas_call(
        pairs_body,
        in_specs=[VMEM] * 3,
        out_specs=[VMEM] * 3,
        out_shape=[sds((DOCS, EMB), BF), sds((DOCS, EMB), BF), sds((8, DOCS), F32)],
        compiler_params=params(),
    )(q_unit, k_unit, pos)


def scores_body(*refs):
    q_in, k_own, k_oth = refs[0:8], refs[8:16], refs[16:24]
    mask, pos_rows = refs[24:26]
    e_own, e_oth, row_out, col_out = refs[26:30]
    q_s, k_s, acc, sems = refs[30:34]
    loads_q = [
        pltpu.make_async_copy(q_in[s], q_s.at[pl.ds(s * DOCS, DOCS)], sems.at[s]) for s in range(8)
    ]
    loads_k = []
    for s in range(8):
        for half, src in ((0, k_own), (1, k_oth)):
            loads_k.append(
                pltpu.make_async_copy(
                    src[s],
                    k_s.at[pl.ds(s * 256 + half * DOCS, DOCS)],
                    sems.at[8 + s * 2 + half],
                )
            )
    for load in loads_q + loads_k:
        load.start()
    for load in loads_q:
        load.wait()
    for b in range(8):
        loads_k[2 * b].wait()
        loads_k[2 * b + 1].wait()
        score = dot_t(q_s[...], k_s[b * 256 : (b + 1) * 256, :])
        total = None
        for a in range(8):
            rows = slice(a * DOCS, (a + 1) * DOCS)
            expo = jnp.exp(score[rows, :] * TAU_INV) * mask[a, b]
            own, oth = expo[:, :DOCS], expo[:, DOCS:]
            e_own[b, rows, :] = own.astype(BF)
            e_oth[b, rows, :] = oth.astype(BF)
            if b == 0:
                acc[rows, :] = own + oth
            else:
                acc[rows, :] += own + oth
            total = expo if total is None else total + expo
        col = jnp.sum(total, axis=0, keepdims=True)
        if b == 0:
            col_out[0:1, :] = col[:, :DOCS] + pos_rows[1:2, :]
        else:
            col_out[2 * b : 2 * b + 1, :] = col[:, :DOCS]
        col_out[2 * b + 1 : 2 * b + 2, :] = col[:, DOCS:]
    for a in range(8):
        part = jnp.sum(acc[a * DOCS : (a + 1) * DOCS, :].T, axis=0, keepdims=True)
        if a == 0:
            part = part + pos_rows[0:1, :]
        row_out[a : a + 1, :] = part


def scores(q_in, k_own, k_oth, mask, pos_rows):
    return pl.pallas_call(
        scores_body,
        in_specs=[ANY] * 24 + [SMEM, VMEM],
        out_specs=[VMEM] * 4,
        out_shape=[
            sds((8, 8 * DOCS, DOCS), BF),
            sds((8, 8 * DOCS, DOCS), BF),
            sds((8, DOCS), F32),
            sds((16, DOCS), F32),
        ],
        scratch_shapes=[
            pltpu.VMEM((8 * DOCS, EMB), BF),
            pltpu.VMEM((16 * DOCS, EMB), BF),
            pltpu.VMEM((8 * DOCS, DOCS), F32),
            pltpu.SemaphoreType.DMA((24,)),
        ],
        compiler_params=params(),
    )(*q_in, *k_own, *k_oth, mask, pos_rows)


def grads_body(*refs):
    q_own, q_oth, k_own, k_oth = refs[0:8], refs[8:16], refs[16:24], refs[24:32]
    e_own, e_oth, e_rcv, inv_row, inv_col = refs[32:37]
    outs = refs[37:49]
    q_s, k_s, wq, wk, sems = refs[49:54]
    loads = []
    for s in range(8):
        for half, src in ((0, k_own), (1, k_oth)):
            loads.append((src[s], k_s.at[pl.ds(s * 256 + half * DOCS, DOCS)]))
    for half, src in ((0, q_own), (1, q_oth)):
        for s in range(8):
            loads.append((src[s], q_s.at[pl.ds((half * 8 + s) * DOCS, DOCS)]))
    loads = [pltpu.make_async_copy(s, d, sems.at[i]) for i, (s, d) in enumerate(loads)]
    for load in loads:
        load.start()
    for a in range(8):
        rows = slice(a * DOCS, (a + 1) * DOCS)
        far = slice((8 + a) * DOCS, (9 + a) * DOCS)
        col_own = jnp.broadcast_to(inv_row[a : a + 1, :], (DOCS, DOCS)).T
        col_oth = jnp.broadcast_to(inv_row[8 + a : 9 + a, :], (DOCS, DOCS)).T
        for b in range(8):
            near_key = inv_col[2 * b : 2 * b + 1, :]
            far_key = inv_col[2 * b + 1 : 2 * b + 2, :]
            w1 = (e_own[b, rows, :].astype(F32) * (col_own + near_key)).astype(BF)
            w2 = (e_oth[b, rows, :].astype(F32) * (col_own + far_key)).astype(BF)
            w3 = (e_rcv[b, rows, :].astype(F32) * (col_oth + near_key)).astype(BF)
            wq[rows, b * 256 : b * 256 + DOCS] = w1
            wq[rows, b * 256 + DOCS : (b + 1) * 256] = w2
            wk[rows, b * DOCS : (b + 1) * DOCS] = w1
            wk[far, b * DOCS : (b + 1) * DOCS] = w3
    for load in loads[:16]:
        load.wait()

    def put(outs, m, grad):
        grad = grad.astype(BF)
        outs[m][...] = grad[:, :NA]
        outs[4][m * DOCS : (m + 1) * DOCS, :] = grad[:DOCS, NA:]
        outs[5][m * DOCS : (m + 1) * DOCS, :] = grad[DOCS:, NA:]

    for m in range(4):
        put(outs[:6], m, dot(wq[m * 256 : (m + 1) * 256, :], k_s[...]) * TAU_INV)
    for load in loads[16:]:
        load.wait()
    for m in range(4):
        put(outs[6:], m, t_dot(wk[:, m * 256 : (m + 1) * 256], q_s[...]) * TAU_INV)


def grads(q_own, q_oth, k_own, k_oth, e_own, e_oth, e_rcv, inv_row, inv_col):
    one = [sds((256, NA), BF)] * 4 + [sds((4 * DOCS, NB), BF)] * 2
    return pl.pallas_call(
        grads_body,
        in_specs=[ANY] * 32 + [VMEM] * 5,
        out_specs=[VMEM] * 12,
        out_shape=one + one,
        scratch_shapes=[
            pltpu.VMEM((16 * DOCS, EMB), BF),
            pltpu.VMEM((16 * DOCS, EMB), BF),
            pltpu.VMEM((8 * DOCS, 16 * DOCS), BF),
            pltpu.VMEM((16 * DOCS, 8 * DOCS), BF),
            pltpu.SemaphoreType.DMA((32,)),
        ],
        compiler_params=params(),
    )(*q_own, *q_oth, *k_own, *k_oth, e_own, e_oth, e_rcv, inv_row, inv_col)


def middle_body(*refs):
    for ins, outs in ((refs[0:6], refs[12:18]), (refs[6:12], refs[18:24])):
        total = sum(ref[...].astype(F32) for ref in ins[:4])
        outs[0][...] = total[:DOCS, :]
        outs[1][...] = total[DOCS:, :].astype(BF)
        for s in range(4):
            rows = slice(s * DOCS, (s + 1) * DOCS)
            part = ins[4][rows, :].astype(F32) + ins[5][rows, :].astype(F32)
            outs[2 + s][...] = part.astype(outs[2 + s].dtype)


def middle(query_in, key_in):
    one = [sds((DOCS, NA), F32), sds((DOCS, NA), BF), sds((DOCS, NB), F32)] + [
        sds((DOCS, NB), BF)
    ] * 3
    return pl.pallas_call(
        middle_body,
        in_specs=[VMEM] * 12,
        out_specs=[VMEM] * 12,
        out_shape=one + one,
        compiler_params=params(),
    )(*query_in, *key_in)


def back_body(*refs):
    q_parts, k_parts = refs[0:6], refs[6:12]
    q_raw, k_raw, q_unit, paired, q_perm, pos, inv_row, inv_col, out = refs[12:21]
    hot = one_hot(pos[...])
    same = eye()
    pair = paired[...].astype(F32)
    score = jnp.sum(q_unit[...].astype(F32) * pair, axis=1, keepdims=True) * TAU_INV
    expo = jnp.exp(score)
    inv_r = jnp.sum(same * inv_row[0:1, :], axis=1, keepdims=True)
    inv_c = jnp.sum(hot * inv_col[0:1, :], axis=1, keepdims=True)
    weight = expo * inv_r + expo * inv_c - 2.0
    weight_k = jnp.sum(same * jnp.sum(hot * weight, axis=0, keepdims=True), axis=1, keepdims=True)
    for parts, raw, w, pair_rows, start in (
        (q_parts, q_raw, weight, pair, 0),
        (k_parts, k_raw, weight_k, q_perm[...].astype(F32), DOCS),
    ):
        left = parts[0][...] + parts[1][...].astype(F32)
        right = parts[2][...] + sum(ref[...].astype(F32) for ref in parts[3:6])
        grad = jnp.concatenate([left, right], axis=1) + (w * TAU_INV) * pair_rows
        exact, scale = unit_of(raw[...])
        inner = jnp.sum(exact * grad, axis=1, keepdims=True)
        out[start : start + DOCS, :] = (scale * (grad - exact * inner)).astype(BF)


def back(*args):
    return pl.pallas_call(
        back_body,
        in_specs=[VMEM] * 20,
        out_specs=VMEM,
        out_shape=sds((2 * DOCS, EMB), BF),
        compiler_params=params(),
    )(*args)


def contract_body(h_own, h_oth, b_own, b_oth, where, *outs):
    for k in range(4):
        x = (where[0] + k) & 3
        y = (where[1] + k) & 3
        z = (where[2] + k) & 3
        picks = (
            [(x * 16, 16)],
            [((g * 4 + y) * 2, 2) for g in range(8)],
            [(g * 16 + (z >> 1) * 8 + i * 2 + (z & 1), 1) for g in range(4) for i in range(4)],
        )
        columns = ((0, NX), (NX, NX + NY), (NX + NY, EMB))
        for part in range(3):
            lo, hi = columns[part]
            total = None
            for h, b in ((h_own, b_own), (h_oth, b_oth)):
                left = jnp.concatenate([h[pl.ds(s, n)] for s, n in picks[part]], axis=0)
                left = left.reshape(512, 256)
                one = dot(left, b[:, lo:hi])
                total = one if total is None else total + one
            ref = outs[part * 4 + k]
            ref[...] = total.astype(ref.dtype)


def contract(h_own, h_oth, b_own, b_oth, where):
    shapes = []
    for n in (NX, NY, NZ):
        shapes += [sds((512, n), F32)] + [sds((512, n), BF)] * 3
    return pl.pallas_call(
        contract_body,
        in_specs=[VMEM] * 4 + [SMEM],
        out_specs=[VMEM] * 12,
        out_shape=shapes,
        compiler_params=params(),
    )(h_own, h_oth, b_own, b_oth, where)


def sum_first_body(*refs):
    ins, where, outs = refs[0:12], refs[12], refs[13:25]
    for k in range(4):
        x = (where[0] + k) & 3
        y = (where[1] + k) & 3
        z = (where[2] + k) & 3
        picks = (
            [((g * 4 + y) * 64, 64) for g in range(2)],
            [(g * 128 + z * 32, 32) for g in range(4)],
            [(x * 128, 128)],
        )
        for part in range(3):
            out = outs[part * 4 + k]
            at = 0
            for start, n in picks[part]:
                rows = pl.ds(pl.multiple_of(start, 32), n)
                total = sum(ref[rows, :].astype(F32) for ref in ins[part * 4 : part * 4 + 4])
                out[at : at + n, :] = total.astype(out.dtype)
                at += n


def sum_first(ins, where):
    shapes = []
    for n in (NX, NY, NZ):
        shapes += [sds((128, n), F32)] + [sds((128, n), BF)] * 3
    return pl.pallas_call(
        sum_first_body,
        in_specs=[VMEM] * 12 + [SMEM],
        out_specs=[VMEM] * 12,
        out_shape=shapes,
        compiler_params=params(),
    )(*ins, where)


def sum_second_body(*refs):
    ins, where, outs = refs[0:12], refs[12], refs[13:25]
    for k in range(4):
        for part, axis in ((0, 2), (1, 0), (2, 1)):
            at = (where[axis] + k) & 3
            rows = pl.ds(pl.multiple_of(at * 32, 32), 32)
            total = sum(ref[rows, :].astype(F32) for ref in ins[part * 4 : part * 4 + 4])
            out = outs[part * 4 + k]
            out[...] = total.astype(out.dtype)


def sum_second(ins, where):
    shapes = []
    for n in (NX, NY, NZ):
        shapes += [sds((32, n), F32)] + [sds((32, n), BF)] * 3
    return pl.pallas_call(
        sum_second_body,
        in_specs=[VMEM] * 12 + [SMEM],
        out_specs=[VMEM] * 12,
        out_shape=shapes,
        compiler_params=params(),
    )(*ins, where)


def sum_last_body(*refs):
    ins, out = refs[0:12], refs[12]
    for part, (lo, hi) in enumerate(((0, NX), (NX, NX + NY), (NX + NY, EMB))):
        out[:, lo:hi] = sum(ref[...].astype(F32) for ref in ins[part * 4 : part * 4 + 4])


def sum_last(ins):
    return pl.pallas_call(
        sum_last_body,
        in_specs=[VMEM] * 12,
        out_specs=VMEM,
        out_shape=sds((32, EMB), F32),
        compiler_params=params(),
    )(*ins)


def exchange(parts, moves):
    done = []
    for part, move in enumerate(moves):
        own = parts[part * 4]
        done += [own] + [move(parts[part * 4 + k], k) for k in (1, 2, 3)]
    return done


def gather(own, move):
    slots = [None] * 8
    slots[0] = own
    slots[1] = move(own, 0, 1)
    for step in (1, 3, 2):
        slots[2 * step] = move(own, step, 0)
    for step in (1, 3, 2):
        slots[2 * step + 1] = move(slots[1], step, 0)
    return slots


def add_up(own, move):
    total = own
    for step in range(4):
        for flip in range(2):
            if step or flip:
                got = move(own, step, flip)
                order = [((j // 2 - step) % 4) * 2 + ((j % 2) ^ flip) for j in range(8)]
                total = total + jnp.stack([got[j] for j in order])
    return total


def to_owners(parts, move):
    near = [parts[0]] + [move(parts[(4 - step) % 4], step, 0) for step in (1, 2, 3)]
    return near + [parts[4], move(parts[5], 0, 1)]


def local(hid_query, hid_key, projection, tile_rows, tile_cols, tile_count, positive):
    row_index = lax.axis_index("row")
    col_index = lax.axis_index("col")
    core_index = lax.axis_index("dp")
    x, z_hi = row_index // 2, row_index % 2
    y, z_lo = col_index // 2, col_index % 2
    where = jnp.stack([x, y, z_hi * 2 + z_lo, core_index]).astype(jnp.int32)

    q_unit, k_unit, q_raw, k_raw = project(hid_query, hid_key, projection)
    k_own = gather(k_unit, move_key)
    q_own = gather(q_unit, move_query)
    k_oth = [swap(one) for one in k_own]
    q_oth = [swap(one) for one in q_own]

    pos = (positive - ((row_index * 8 + col_index) * 2 + core_index) * DOCS).reshape(DOCS, 1)
    paired, q_perm, pos_rows = pair_up(q_unit, k_unit, pos)
    turned = jnp.concatenate([hid_query, hid_key], axis=0).T.reshape(64, 2, 32, 256)
    h_own = lax.dynamic_index_in_dim(turned, core_index, 1, keepdims=False)
    h_oth = swap(lax.dynamic_index_in_dim(turned, 1 - core_index, 1, keepdims=False))

    entry_rows = tile_rows[0, 0]
    entry_cols = tile_cols[0, 0]
    used = jnp.arange(entry_rows.shape[0], dtype=jnp.int32) < tile_count[0, 0]
    slot_rows = ((y - entry_rows // 2) % 4) * 2 + (z_lo ^ (entry_rows % 2))
    slot_cols = ((x - entry_cols // 2) % 4) * 2 + (z_hi ^ (entry_cols % 2))
    eight = jnp.arange(8, dtype=jnp.int32)
    hit = (
        (slot_rows[:, None, None] == eight[None, :, None])
        & (slot_cols[:, None, None] == eight[None, None, :])
        & used[:, None, None]
    )
    mask = jnp.any(hit, axis=0).astype(F32)

    e_own, e_oth, row_part, col_part = scores(q_own, k_own, k_oth, mask, pos_rows)
    e_rcv = swap(e_oth)
    row_total = add_up(row_part.reshape(8, 1, DOCS), move_query).reshape(8, DOCS)
    col_total = add_up(col_part.reshape(8, 2, DOCS), move_key)
    far = swap(jnp.concatenate([row_total, col_total.reshape(16, DOCS)], axis=0))
    col_total = (col_total + far[8:].reshape(8, 2, DOCS)[:, ::-1]).reshape(16, DOCS)
    inv_row = 1.0 / jnp.concatenate([row_total, far[:8]], axis=0)
    inv_col = 1.0 / col_total

    parts = grads(q_own, q_oth, k_own, k_oth, e_own, e_oth, e_rcv, inv_row, inv_col)
    sums = middle(to_owners(parts[:6], move_query), to_owners(parts[6:], move_key))

    def finish(one, move):
        got = [one[0], move(one[1], 0, 1), one[2]]
        return got + [move(one[2 + (4 - step) % 4], step, 0) for step in (1, 2, 3)]

    b_own = back(
        *finish(sums[:6], move_query),
        *finish(sums[6:], move_key),
        q_raw,
        k_raw,
        q_unit,
        paired,
        q_perm,
        pos,
        inv_row,
        inv_col,
    )
    b_oth = swap(b_own)
    out = contract(h_own, h_oth, b_own, b_oth, where)
    out = sum_first(exchange(out, (move_x, move_y, move_z)), where)
    out = sum_second(exchange(out, (move_y, move_z, move_x)), where)
    return sum_last(exchange(out, (move_z, move_x, move_y)))


def solution(mesh):
    return jax.shard_map(
        local,
        mesh=mesh,
        in_specs=(
            P(("row", "col", "dp"), None),
            P(("row", "col", "dp"), None),
            P(),
            P("row", "col", None),
            P("row", "col", None),
            P("row", "col"),
            P(("row", "col", "dp")),
        ),
        out_specs=P(("row", "col", "dp"), None),
        check_vma=False,
    )
```

```python
import jax
import jax.numpy as jnp
from jax import lax
from jax.experimental import pallas as pl
from jax.experimental.pallas import tpu as pltpu
from jax.sharding import PartitionSpec as P

TAU_INV = 20.0
EPS = 1e-06
LOG2E = 1.4426950408889634
DOCS = 128
EMB = 1024
HID = 4096
BF = jnp.bfloat16
F32 = jnp.float32
VM = 56 * 1024 * 1024


def ring_pair(step, flip):
    return [(i, ((i // 2 + step) % 4) * 2 + ((i % 2) ^ flip)) for i in range(8)]


def move_query(value, step, flip):
    return lax.ppermute(value, "col", ring_pair(step, flip))


def move_key(value, step, flip):
    return lax.ppermute(value, "row", ring_pair(step, flip))


def move_z(value, step):
    pairs = []
    for r in range(8):
        for c in range(8):
            z = ((r % 2) * 2 + c % 2 + step) % 4
            pairs.append((r * 8 + c, ((r // 2) * 2 + z // 2) * 8 + (c // 2) * 2 + z % 2))
    return lax.ppermute(value, ("row", "col"), pairs)


def chip(x, y, z):
    return (x * 2 + z // 2) * 8 + y * 2 + z % 2


Z_GROUPS = [
    [chip(x, y, z) * 2 + core for z in range(4) for core in range(2)]
    for x in range(4)
    for y in range(4)
]
XY_GROUPS = [[chip(x, y, z) for x in range(4) for y in range(4)] for z in range(4)]


def swap(value):
    return lax.ppermute(value, "dp", [(0, 1), (1, 0)])


def params():
    return pltpu.CompilerParams(vmem_limit_bytes=VM)


def sds(shape, dtype):
    return jax.ShapeDtypeStruct(shape, dtype)


ANY = pl.BlockSpec(memory_space=pl.ANY)
SMEM = pl.BlockSpec(memory_space=pltpu.SMEM)
VMEM = pl.BlockSpec(memory_space=pltpu.VMEM)


def dot(a, b):
    return lax.dot_general(a, b, (((1,), (0,)), ((), ())), preferred_element_type=F32)


def dot_t(a, b):
    return lax.dot_general(a, b, (((1,), (1,)), ((), ())), preferred_element_type=F32)


def t_dot(a, b):
    return lax.dot_general(a, b, (((0,), (0,)), ((), ())), preferred_element_type=F32)


def unit_of(raw):
    values = raw.astype(F32)
    scale = lax.rsqrt(jnp.sum(values * values, axis=1, keepdims=True) + EPS)
    return values * scale, scale


def project_body(hq, hk, proj, q_unit, k_unit, q_raw, k_raw, hid, acc):
    step = pl.program_id(0)
    hid[:DOCS, :] = hq[...]
    hid[DOCS:, :] = hk[...]
    part = dot(hid[...], proj[...])

    @pl.when(step == 0)
    def _():
        acc[...] = part

    @pl.when(step > 0)
    def _():
        acc[...] += part

    @pl.when(step == pl.num_programs(0) - 1)
    def _():
        for raw_ref, unit_ref, start in ((q_raw, q_unit, 0), (k_raw, k_unit, DOCS)):
            raw = acc[start : start + DOCS, :].astype(BF)
            raw_ref[...] = raw
            unit_ref[...] = unit_of(raw)[0].astype(BF)


def project(hid_query, hid_key, projection):
    depth = 1024
    whole = pl.BlockSpec((DOCS, EMB), lambda i: (0, 0))
    return pl.pallas_call(
        project_body,
        grid=(HID // depth,),
        in_specs=[
            pl.BlockSpec((DOCS, depth), lambda i: (0, i)),
            pl.BlockSpec((DOCS, depth), lambda i: (0, i)),
            pl.BlockSpec((depth, EMB), lambda i: (i, 0)),
        ],
        out_specs=[whole] * 4,
        out_shape=[sds((DOCS, EMB), BF)] * 4,
        scratch_shapes=[pltpu.VMEM((2 * DOCS, depth), BF), pltpu.VMEM((2 * DOCS, EMB), F32)],
        compiler_params=params(),
    )(hid_query, hid_key, projection)


def one_hot(pos):
    lane = lax.broadcasted_iota(jnp.int32, (DOCS, DOCS), 1)
    return (lane == pos).astype(F32)


def eye():
    lane = lax.broadcasted_iota(jnp.int32, (DOCS, DOCS), 1)
    row = lax.broadcasted_iota(jnp.int32, (DOCS, DOCS), 0)
    return (lane == row).astype(F32)


def pairs_body(q_unit, k_unit, pos, paired, q_perm, pos_rows):
    hot = one_hot(pos[...])
    hot_bf = hot.astype(BF)
    pair = dot(hot_bf, k_unit[...])
    paired[...] = pair.astype(BF)
    q_perm[...] = t_dot(hot_bf, q_unit[...]).astype(BF)
    score = jnp.sum(q_unit[...].astype(F32) * pair, axis=1, keepdims=True) * TAU_INV
    expo = jnp.exp(score)
    pos_rows[0:1, :] = jnp.sum(eye() * expo, axis=0, keepdims=True)
    pos_rows[1:2, :] = jnp.sum(hot * expo, axis=0, keepdims=True)
    pos_rows[2:8, :] = jnp.zeros((6, DOCS), F32)


def pair_up(q_unit, k_unit, pos):
    return pl.pallas_call(
        pairs_body,
        in_specs=[VMEM] * 3,
        out_specs=[VMEM] * 3,
        out_shape=[sds((DOCS, EMB), BF), sds((DOCS, EMB), BF), sds((8, DOCS), F32)],
        compiler_params=params(),
    )(q_unit, k_unit, pos)


def scores_body(*refs):
    q_in, k_in = refs[0:4], refs[4:12]
    mask, pos_rows = refs[12:14]
    e_own, e_oth, sums = refs[14:17]
    q_s, k_s, e_s, acc, in_sems, out_sems = refs[17:23]
    loads = [
        pltpu.make_async_copy(ref, q_s.at[pl.ds(s * 256, 256)], in_sems.at[s])
        for s, ref in enumerate(q_in)
    ] + [
        pltpu.make_async_copy(ref, k_s.at[pl.ds(s * 256, 256)], in_sems.at[4 + s])
        for s, ref in enumerate(k_in)
    ]
    order = [4, 0, 1, 2, 3] + list(range(5, 12))
    for i in order:
        loads[i].start()
    stores = []
    for b in range(8):
        loads[4 + b].wait()
        total = [None, None]
        for m in range(4):
            if b == 0:
                loads[m].wait()
            chunk = slice(m * 256, (m + 1) * 256)
            score = dot_t(q_s[chunk, :], k_s[b * 256 : (b + 1) * 256, :])
            for n in range(2):
                a = m * 2 + n
                rows = slice(a * DOCS, (a + 1) * DOCS)
                expo = jnp.exp2(score[n * DOCS : (n + 1) * DOCS, :] * (TAU_INV * LOG2E))
                both = None
                for half in range(2):
                    slot = (b % 4) * 2 + half
                    one = expo[:, half * DOCS : (half + 1) * DOCS] * mask[a, slot]
                    e_s[b, rows, half * DOCS : (half + 1) * DOCS] = one.astype(BF)
                    both = one if half == 0 else both + one
                    part = one.reshape(16, 8, DOCS).sum(axis=0)
                    total[half] = part if a == 0 else total[half] + part
                if b == 0:
                    acc[rows, :] = both
                else:
                    acc[rows, :] += both
        out = (e_own if b < 4 else e_oth).at[:, pl.ds((b % 4) * 256, 256)]
        stores.append(pltpu.make_async_copy(e_s.at[b], out, out_sems.at[b]))
        stores[-1].start()
        for half in range(2):
            col = jnp.sum(total[half], axis=0, keepdims=True)
            if b == 0 and half == 0:
                col = col + pos_rows[1:2, :]
            sums[8 + 2 * b + half : 9 + 2 * b + half, :] = col
    for a in range(8):
        part = jnp.sum(acc[a * DOCS : (a + 1) * DOCS, :].T, axis=0, keepdims=True)
        if a == 0:
            part = part + pos_rows[0:1, :]
        sums[a : a + 1, :] = part
    for store in stores:
        store.wait()


def scores(q_in, k_in, mask, pos_rows):
    return pl.pallas_call(
        scores_body,
        in_specs=[ANY] * 12 + [SMEM, VMEM],
        out_specs=[ANY, ANY, VMEM],
        out_shape=[
            sds((8 * DOCS, 8 * DOCS), BF),
            sds((8 * DOCS, 8 * DOCS), BF),
            sds((24, DOCS), F32),
        ],
        scratch_shapes=[
            pltpu.VMEM((8 * DOCS, EMB), BF),
            pltpu.VMEM((16 * DOCS, EMB), BF),
            pltpu.VMEM((8, 8 * DOCS, 256), BF),
            pltpu.VMEM((8 * DOCS, DOCS), F32),
            pltpu.SemaphoreType.DMA((12,)),
            pltpu.SemaphoreType.DMA((8,)),
        ],
        compiler_params=params(),
    )(*q_in, *k_in, mask, pos_rows)


def grads_body(*refs):
    q_in, k_in, e_in = refs[0:8], refs[8:16], refs[16:19]
    row_in, col_in = refs[19:23], refs[23:27]
    q_out, k_out, inv_out = refs[27:31], refs[31:35], refs[35]
    q_s, k_s, e_s, wq, wk, out_s, inv, sems, out_sems = refs[36:45]
    loads = []
    for m in range(4):
        for i in range(3):
            rows = pl.ds(m * 256, 256)
            loads.append((e_in[i].at[rows], e_s.at[i, rows]))
    loads += [(ref, k_s.at[pl.ds(s * 256, 256)]) for s, ref in enumerate(k_in)]
    loads += [(ref, q_s.at[pl.ds(s * 256, 256)]) for s, ref in enumerate(q_in)]
    loads = [pltpu.make_async_copy(s, d, sems.at[i]) for i, (s, d) in enumerate(loads)]
    for load in loads:
        load.start()
    for at, ins in ((0, row_in), (16, col_in)):
        for rel in range(2):
            for slot in range(8):
                total = ins[0][rel * 8 + slot : rel * 8 + slot + 1, :]
                for step in (1, 2, 3):
                    src = rel * 8 + (slot - 2 * step) % 8
                    total = total + ins[step][src : src + 1, :]
                dst = at + rel * 8 + slot
                inv[dst : dst + 1, :] = 1.0 / total
    inv_out[0:1, :] = inv[0:1, :]
    inv_out[1:2, :] = inv[16:17, :]
    inv_out[2:8, :] = jnp.zeros((6, DOCS), F32)
    stores = []

    def put(i, ref, grad):
        out_s[i] = grad.astype(BF)
        stores.append(pltpu.make_async_copy(out_s.at[i], ref, out_sems.at[i]))
        stores[-1].start()

    for m in range(4):
        for load in loads[3 * m : 3 * m + 3]:
            load.wait()
        for a in (2 * m, 2 * m + 1):
            rows = slice(a * DOCS, (a + 1) * DOCS)
            far = slice((8 + a) * DOCS, (9 + a) * DOCS)
            col_own = jnp.broadcast_to(inv[a : a + 1, :], (DOCS, DOCS)).T
            col_oth = jnp.broadcast_to(inv[8 + a : 9 + a, :], (DOCS, DOCS)).T
            for b in range(8):
                near_key = inv[16 + b : 17 + b, :]
                far_key = inv[24 + b : 25 + b, :]
                keys = slice(b * DOCS, (b + 1) * DOCS)
                keys_far = slice((8 + b) * DOCS, (9 + b) * DOCS)
                w1 = (e_s[0, rows, keys].astype(F32) * (col_own + near_key)).astype(BF)
                w2 = (e_s[1, rows, keys].astype(F32) * (col_own + far_key)).astype(BF)
                w3 = (e_s[2, rows, keys].astype(F32) * (col_oth + near_key)).astype(BF)
                wq[rows, keys] = w1
                wq[rows, keys_far] = w2
                wk[rows, keys] = w1
                wk[far, keys] = w3
    for load in loads[12:20]:
        load.wait()
    for m in range(4):
        put(m, q_out[m], dot(wq[m * 256 : (m + 1) * 256, :], k_s[...]) * TAU_INV)
    for load in loads[20:]:
        load.wait()
    for m in range(4):
        put(4 + m, k_out[m], t_dot(wk[:, m * 256 : (m + 1) * 256], q_s[...]) * TAU_INV)
    for store in stores:
        store.wait()


def grads(q_in, k_in, e_in, row_in, col_in):
    return pl.pallas_call(
        grads_body,
        in_specs=[ANY] * 19 + [VMEM] * 8,
        out_specs=[ANY] * 8 + [VMEM],
        out_shape=[sds((256, EMB), BF)] * 8 + [sds((8, DOCS), F32)],
        scratch_shapes=[
            pltpu.VMEM((16 * DOCS, EMB), BF),
            pltpu.VMEM((16 * DOCS, EMB), BF),
            pltpu.VMEM((3, 8 * DOCS, 8 * DOCS), BF),
            pltpu.VMEM((8 * DOCS, 16 * DOCS), BF),
            pltpu.VMEM((16 * DOCS, 8 * DOCS), BF),
            pltpu.VMEM((8, 256, EMB), BF),
            pltpu.VMEM((32, DOCS), F32),
            pltpu.SemaphoreType.DMA((28,)),
            pltpu.SemaphoreType.DMA((8,)),
        ],
        compiler_params=params(),
    )(*q_in, *k_in, *e_in, *row_in, *col_in)


def half_block(which):
    return pl.BlockSpec((DOCS, EMB), lambda i: (which, 0))


def pass_body(*refs):
    for ins, out in ((refs[0:4], refs[8]), (refs[4:8], refs[9])):
        out[...] = sum(ref[...].astype(F32) for ref in ins).astype(BF)


def pass_on(query_in, key_in):
    return pl.pallas_call(
        pass_body,
        grid=(1,),
        in_specs=[half_block(1)] * 8,
        out_specs=[half_block(0)] * 2,
        out_shape=[sds((DOCS, EMB), BF)] * 2,
        compiler_params=params(),
    )(*query_in, *key_in)


def keep_body(*refs):
    q_parts, k_parts = refs[0:4], refs[4:8]
    q_unit, paired, q_perm, pos, inv, q_out, k_out = refs[8:15]
    hot = one_hot(pos[...])
    same = eye()
    pair = paired[...].astype(F32)
    score = jnp.sum(q_unit[...].astype(F32) * pair, axis=1, keepdims=True) * TAU_INV
    expo = jnp.exp(score)
    inv_r = jnp.sum(same * inv[0:1, :], axis=1, keepdims=True)
    inv_c = jnp.sum(hot * inv[1:2, :], axis=1, keepdims=True)
    weight = expo * inv_r + expo * inv_c - 2.0
    weight_k = jnp.sum(same * jnp.sum(hot * weight, axis=0, keepdims=True), axis=1, keepdims=True)
    for parts, w, pair_rows, out in (
        (q_parts, weight, pair, q_out),
        (k_parts, weight_k, q_perm[...].astype(F32), k_out),
    ):
        out[...] = sum(ref[...].astype(F32) for ref in parts) + (w * TAU_INV) * pair_rows


def keep(query_in, key_in, q_unit, paired, q_perm, pos, inv):
    return pl.pallas_call(
        keep_body,
        grid=(1,),
        in_specs=[half_block(0)] * 11 + [VMEM] * 2,
        out_specs=[half_block(0)] * 2,
        out_shape=[sds((DOCS, EMB), F32)] * 2,
        compiler_params=params(),
    )(*query_in, *key_in, q_unit, paired, q_perm, pos, inv)


def back_body(q_keep, q_got, k_keep, k_got, q_raw, k_raw, out):
    for kept, got, raw, start in ((q_keep, q_got, q_raw, 0), (k_keep, k_got, k_raw, DOCS)):
        grad = kept[...] + got[...].astype(F32)
        exact, scale = unit_of(raw[...])
        inner = jnp.sum(exact * grad, axis=1, keepdims=True)
        out[start : start + DOCS, :] = (scale * (grad - exact * inner)).astype(BF)


def back(*args):
    return pl.pallas_call(
        back_body,
        in_specs=[VMEM] * 6,
        out_specs=VMEM,
        out_shape=sds((2 * DOCS, EMB), BF),
        compiler_params=params(),
    )(*args)


def contract_body(*refs):
    b_in, h_in, where, out = refs[0:8], refs[8], refs[9], refs[10]
    h_s, b_s, sems = refs[11:14]
    loads = []
    for i in range(8):
        step, far = i % 4, i // 4
        source = ((where[2] - step) & 3) * 2 + (where[3] ^ far)
        loads.append((b_in[i], b_s.at[pl.ds(i * 256, 256)]))
        loads.append((h_in.at[source], h_s.at[:, pl.ds(i * 256, 256)]))
    loads = [pltpu.make_async_copy(s, d, sems.at[i]) for i, (s, d) in enumerate(loads)]
    for load in loads:
        load.start()
    for load in loads[:8]:
        load.wait()
    near = dot(h_s[:, :1024], b_s[:1024, :])
    for load in loads[8:]:
        load.wait()
    out[...] = (near + dot(h_s[:, 1024:], b_s[1024:, :])).astype(BF)


def contract(b_in, h_in, where):
    return pl.pallas_call(
        contract_body,
        in_specs=[ANY] * 9 + [SMEM],
        out_specs=VMEM,
        out_shape=sds((512, EMB), BF),
        scratch_shapes=[
            pltpu.VMEM((512, 2048), BF),
            pltpu.VMEM((2048, EMB), BF),
            pltpu.SemaphoreType.DMA((16,)),
        ],
        compiler_params=params(),
    )(*b_in, h_in, where)


def flip_slots(value):
    return value[:, ::-1]


def to_owners(parts, move):
    return [parts[0]] + [move(parts[(4 - step) % 4], step, 0) for step in (1, 2, 3)]


def local(hid_query, hid_key, projection, tile_rows, tile_cols, tile_count, positive):
    row_index = lax.axis_index("row")
    col_index = lax.axis_index("col")
    core_index = lax.axis_index("dp")
    x, z_hi = row_index // 2, row_index % 2
    y, z_lo = col_index // 2, col_index % 2
    where = jnp.stack([x, y, z_hi * 2 + z_lo, core_index]).astype(jnp.int32)

    q_unit, k_unit, q_raw, k_raw = project(hid_query, hid_key, projection)
    k_flip = move_key(k_unit, 0, 1)
    q_flip = move_query(q_unit, 0, 1)

    pos = (positive - ((row_index * 8 + col_index) * 2 + core_index) * DOCS).reshape(DOCS, 1)
    paired, q_perm, pos_rows = pair_up(q_unit, k_unit, pos)
    turned = jnp.concatenate([hid_query, hid_key], axis=0).T.reshape(4, 2, 4, 2, 2, 32, 256)
    turned = turned.transpose(1, 3, 4, 0, 2, 5, 6).reshape(4096, 256)
    entry_rows = tile_rows[0, 0]
    entry_cols = tile_cols[0, 0]
    used = jnp.arange(entry_rows.shape[0], dtype=jnp.int32) < tile_count[0, 0]
    slot_rows = ((y - entry_rows // 2) % 4) * 2 + (z_lo ^ (entry_rows % 2))
    slot_cols = ((x - entry_cols // 2) % 4) * 2 + (z_hi ^ (entry_cols % 2))
    eight = jnp.arange(8, dtype=jnp.int32)
    hit = (
        (slot_rows[:, None, None] == eight[None, :, None])
        & (slot_cols[:, None, None] == eight[None, None, :])
        & used[:, None, None]
    )
    mask = jnp.any(hit, axis=0).astype(F32)

    k_flip, q_flip, pos, paired, q_perm, pos_rows, turned, mask = lax.optimization_barrier(
        (k_flip, q_flip, pos, paired, q_perm, pos_rows, turned, mask)
    )
    k_pair = jnp.concatenate([k_unit, k_flip], axis=0)
    q_pair = jnp.concatenate([q_unit, q_flip], axis=0)
    h_all = lax.all_to_all(
        turned, ("row", "col", "dp"), 0, 0, tiled=True, axis_index_groups=Z_GROUPS
    ).reshape(8, 512, 256)
    k_own = [k_pair] + [move_key(k_pair, step, 0) for step in (1, 2, 3)]
    q_own = [q_pair] + [move_query(q_pair, step, 0) for step in (1, 2, 3)]
    k_oth = [swap(one) for one in k_own]
    q_oth = [swap(one) for one in q_own]
    mask, h_all = lax.optimization_barrier((mask, h_all))

    e_own, e_oth, sums = scores(q_own, k_own + k_oth, mask, pos_rows)
    far = swap(sums)
    e_rcv = swap(e_oth)
    row_part = jnp.concatenate([sums[:8], far[:8]], axis=0).reshape(8, 2, DOCS)
    col_part = sums[8:] + jnp.concatenate([far[16:], far[8:16]], axis=0)
    col_part = col_part.reshape(8, 2, DOCS)
    row_part = row_part + flip_slots(move_query(row_part, 0, 1))
    col_part = col_part + flip_slots(move_key(col_part, 0, 1))
    row_part = row_part.reshape(16, DOCS)
    col_part = col_part.reshape(16, DOCS)
    row_got = [row_part] + [move_query(row_part, step, 0) for step in (1, 2, 3)]
    col_got = [col_part] + [move_key(col_part, step, 0) for step in (1, 2, 3)]

    parts = grads(q_own + q_oth, k_own + k_oth, [e_own, e_oth, e_rcv], row_got, col_got)
    inv = parts[8]
    query_in = to_owners(parts[:4], move_query)
    key_in = to_owners(parts[4:8], move_key)
    q_send, k_send = pass_on(query_in, key_in)
    q_got = move_query(q_send, 0, 1)
    k_got = move_key(k_send, 0, 1)
    q_keep, k_keep = keep(query_in, key_in, q_unit, paired, q_perm, pos, inv)
    b_own = back(q_keep, q_got, k_keep, k_got, q_raw, k_raw)
    b_near = [b_own] + [move_z(b_own, step) for step in (1, 2, 3)]
    out = contract(b_near + [swap(one) for one in b_near], h_all, where)
    out = lax.all_to_all(out, ("row", "col"), 0, 0, tiled=True, axis_index_groups=XY_GROUPS)
    return jnp.sum(out.reshape(16, 32, EMB).astype(F32), axis=0)


def solution(mesh):
    return jax.shard_map(
        local,
        mesh=mesh,
        in_specs=(
            P(("row", "col", "dp"), None),
            P(("row", "col", "dp"), None),
            P(),
            P("row", "col", None),
            P("row", "col", None),
            P("row", "col"),
            P(("row", "col", "dp")),
        ),
        out_specs=P(("row", "col", "dp"), None),
        check_vma=False,
    )
```

```python
import jax
import jax.numpy as jnp
from jax import lax
from jax.experimental import pallas as pl
from jax.experimental.pallas import tpu as pltpu
from jax.sharding import PartitionSpec as P

TAU_INV = 20.0
EPS = 1e-06
LOG2E = 1.4426950408889634
DOCS = 128
EMB = 1024
HID = 4096
BF = jnp.bfloat16
F32 = jnp.float32
VM = 56 * 1024 * 1024


def ring_pair(step, flip):
    return [(i, ((i // 2 + step) % 4) * 2 + ((i % 2) ^ flip)) for i in range(8)]


def move_query(value, step, flip):
    return lax.ppermute(value, "col", ring_pair(step, flip))


def move_key(value, step, flip):
    return lax.ppermute(value, "row", ring_pair(step, flip))


def move_z(value, step):
    pairs = []
    for r in range(8):
        for c in range(8):
            z = ((r % 2) * 2 + c % 2 + step) % 4
            pairs.append((r * 8 + c, ((r // 2) * 2 + z // 2) * 8 + (c // 2) * 2 + z % 2))
    return lax.ppermute(value, ("row", "col"), pairs)


def chip(x, y, z):
    return (x * 2 + z // 2) * 8 + y * 2 + z % 2


Z_GROUPS = [
    [chip(x, y, z) * 2 + core for z in range(4) for core in range(2)]
    for x in range(4)
    for y in range(4)
]
XY_GROUPS = [[chip(x, y, z) for x in range(4) for y in range(4)] for z in range(4)]


def swap(value):
    return lax.ppermute(value, "dp", [(0, 1), (1, 0)])


def params():
    return pltpu.CompilerParams(vmem_limit_bytes=VM)


def sds(shape, dtype):
    return jax.ShapeDtypeStruct(shape, dtype)


ANY = pl.BlockSpec(memory_space=pl.ANY)
SMEM = pl.BlockSpec(memory_space=pltpu.SMEM)
VMEM = pl.BlockSpec(memory_space=pltpu.VMEM)


def dot(a, b):
    return lax.dot_general(a, b, (((1,), (0,)), ((), ())), preferred_element_type=F32)


def dot_t(a, b):
    return lax.dot_general(a, b, (((1,), (1,)), ((), ())), preferred_element_type=F32)


def t_dot(a, b):
    return lax.dot_general(a, b, (((0,), (0,)), ((), ())), preferred_element_type=F32)


def unit_of(raw):
    values = raw.astype(F32)
    scale = lax.rsqrt(jnp.sum(values * values, axis=1, keepdims=True) + EPS)
    return values * scale, scale


def project_body(hq, hk, proj, q_unit, k_unit, q_raw, k_raw, hid, acc):
    step = pl.program_id(0)
    hid[:DOCS, :] = hq[...]
    hid[DOCS:, :] = hk[...]
    part = dot(hid[...], proj[...])

    @pl.when(step == 0)
    def _():
        acc[...] = part

    @pl.when(step > 0)
    def _():
        acc[...] += part

    @pl.when(step == pl.num_programs(0) - 1)
    def _():
        for raw_ref, unit_ref, start in ((q_raw, q_unit, 0), (k_raw, k_unit, DOCS)):
            raw = acc[start : start + DOCS, :].astype(BF)
            raw_ref[...] = raw
            unit_ref[...] = unit_of(raw)[0].astype(BF)


def project(hid_query, hid_key, projection):
    depth = 1024
    whole = pl.BlockSpec((DOCS, EMB), lambda i: (0, 0))
    return pl.pallas_call(
        project_body,
        grid=(HID // depth,),
        in_specs=[
            pl.BlockSpec((DOCS, depth), lambda i: (0, i)),
            pl.BlockSpec((DOCS, depth), lambda i: (0, i)),
            pl.BlockSpec((depth, EMB), lambda i: (i, 0)),
        ],
        out_specs=[whole] * 4,
        out_shape=[sds((DOCS, EMB), BF)] * 4,
        scratch_shapes=[pltpu.VMEM((2 * DOCS, depth), BF), pltpu.VMEM((2 * DOCS, EMB), F32)],
        compiler_params=params(),
    )(hid_query, hid_key, projection)


def one_hot(pos):
    lane = lax.broadcasted_iota(jnp.int32, (DOCS, DOCS), 1)
    return (lane == pos).astype(F32)


def eye():
    lane = lax.broadcasted_iota(jnp.int32, (DOCS, DOCS), 1)
    row = lax.broadcasted_iota(jnp.int32, (DOCS, DOCS), 0)
    return (lane == row).astype(F32)


def pairs_body(q_unit, k_unit, pos, paired, q_perm, pos_rows):
    hot = one_hot(pos[...])
    hot_bf = hot.astype(BF)
    pair = dot(hot_bf, k_unit[...])
    paired[...] = pair.astype(BF)
    q_perm[...] = t_dot(hot_bf, q_unit[...]).astype(BF)
    score = jnp.sum(q_unit[...].astype(F32) * pair, axis=1, keepdims=True) * TAU_INV
    expo = jnp.exp(score)
    pos_rows[0:1, :] = jnp.sum(eye() * expo, axis=0, keepdims=True)
    pos_rows[1:2, :] = jnp.sum(hot * expo, axis=0, keepdims=True)
    pos_rows[2:8, :] = jnp.zeros((6, DOCS), F32)


def pair_up(q_unit, k_unit, pos):
    return pl.pallas_call(
        pairs_body,
        in_specs=[VMEM] * 3,
        out_specs=[VMEM] * 3,
        out_shape=[sds((DOCS, EMB), BF), sds((DOCS, EMB), BF), sds((8, DOCS), F32)],
        compiler_params=params(),
    )(q_unit, k_unit, pos)


PARTS = ((0, 256), (256, 256), (512, 128), (640, 128), (768, 256))


def block_copies(ins, scratch, sems, first, row):
    copies = []
    for i, (start, rows) in enumerate(PARTS):
        target = scratch.at[pl.ds(row + start, rows)]
        copies.append(pltpu.make_async_copy(ins[i], target, sems.at[first + i]))
    return copies


def scores_body(*refs):
    q_in, k_near, k_far = refs[0:5], refs[5:10], refs[10:15]
    mask, pos_rows = refs[15:17]
    e_own, e_oth, sums = refs[17:20]
    q_s, k_s, e_s, acc, in_sems, out_sems = refs[20:26]
    q_loads = block_copies(q_in, q_s, in_sems, 0, 0)
    k_loads = block_copies(k_near, k_s, in_sems, 5, 0) + block_copies(k_far, k_s, in_sems, 10, 1024)
    for load in k_loads[:1] + q_loads + k_loads[1:]:
        load.start()
    waits = ((0,), (1,), (2, 3), (4,), (5,), (6,), (7, 8), (9,))
    stores = []
    for b in range(8):
        for i in waits[b]:
            k_loads[i].wait()
        total = [None, None]
        for m in range(4):
            if b == 0:
                for i in waits[m]:
                    q_loads[i].wait()
            chunk = slice(m * 256, (m + 1) * 256)
            score = dot_t(q_s[chunk, :], k_s[b * 256 : (b + 1) * 256, :])
            for n in range(2):
                a = m * 2 + n
                rows = slice(a * DOCS, (a + 1) * DOCS)
                expo = jnp.exp2(score[n * DOCS : (n + 1) * DOCS, :] * (TAU_INV * LOG2E))
                both = None
                for half in range(2):
                    slot = (b % 4) * 2 + half
                    one = expo[:, half * DOCS : (half + 1) * DOCS] * mask[a, slot]
                    e_s[b, rows, half * DOCS : (half + 1) * DOCS] = one.astype(BF)
                    both = one if half == 0 else both + one
                    part = one.reshape(16, 8, DOCS).sum(axis=0)
                    total[half] = part if a == 0 else total[half] + part
                if b == 0:
                    acc[rows, :] = both
                else:
                    acc[rows, :] += both
        out = (e_own if b < 4 else e_oth).at[:, pl.ds((b % 4) * 256, 256)]
        stores.append(pltpu.make_async_copy(e_s.at[b], out, out_sems.at[b]))
        stores[-1].start()
        for half in range(2):
            col = jnp.sum(total[half], axis=0, keepdims=True)
            if b == 0 and half == 0:
                col = col + pos_rows[1:2, :]
            sums[8 + 2 * b + half : 9 + 2 * b + half, :] = col
    for a in range(8):
        part = jnp.sum(acc[a * DOCS : (a + 1) * DOCS, :].T, axis=0, keepdims=True)
        if a == 0:
            part = part + pos_rows[0:1, :]
        sums[a : a + 1, :] = part
    for store in stores:
        store.wait()


def scores(q_in, k_near, k_far, mask, pos_rows):
    return pl.pallas_call(
        scores_body,
        in_specs=[ANY] * 15 + [SMEM, VMEM],
        out_specs=[ANY, ANY, VMEM],
        out_shape=[
            sds((8 * DOCS, 8 * DOCS), BF),
            sds((8 * DOCS, 8 * DOCS), BF),
            sds((24, DOCS), F32),
        ],
        scratch_shapes=[
            pltpu.VMEM((8 * DOCS, EMB), BF),
            pltpu.VMEM((16 * DOCS, EMB), BF),
            pltpu.VMEM((8, 8 * DOCS, 256), BF),
            pltpu.VMEM((8 * DOCS, DOCS), F32),
            pltpu.SemaphoreType.DMA((15,)),
            pltpu.SemaphoreType.DMA((8,)),
        ],
        compiler_params=params(),
    )(*q_in, *k_near, *k_far, mask, pos_rows)


def grads_body(*refs):
    q_near, q_far, k_near, k_far = refs[0:5], refs[5:10], refs[10:15], refs[15:20]
    e_in, row_in, col_in = refs[20:23], refs[23:27], refs[27:31]
    q_out, k_out, inv_out = refs[31:35], refs[35:39], refs[39]
    q_s, k_s, e_s, wq, wk, out_s, inv, sems, out_sems = refs[40:49]
    loads = []
    for m in range(4):
        for i in range(3):
            rows = pl.ds(m * 256, 256)
            one = (e_in[i].at[rows], e_s.at[i, rows], sems.at[3 * m + i])
            loads.append(pltpu.make_async_copy(*one))
    loads += block_copies(k_near, k_s, sems, 12, 0) + block_copies(k_far, k_s, sems, 17, 1024)
    loads += block_copies(q_near, q_s, sems, 22, 0) + block_copies(q_far, q_s, sems, 27, 1024)
    for load in loads:
        load.start()
    for at, ins in ((0, row_in), (16, col_in)):
        for rel in range(2):
            for slot in range(8):
                total = ins[0][rel * 8 + slot : rel * 8 + slot + 1, :]
                for step in (1, 2, 3):
                    src = rel * 8 + (slot - 2 * step) % 8
                    total = total + ins[step][src : src + 1, :]
                dst = at + rel * 8 + slot
                inv[dst : dst + 1, :] = 1.0 / total
    inv_out[0:1, :] = inv[0:1, :]
    inv_out[1:2, :] = inv[16:17, :]
    inv_out[2:8, :] = jnp.zeros((6, DOCS), F32)
    stores = []

    def put(i, ref, grad):
        out_s[i] = grad.astype(BF)
        stores.append(pltpu.make_async_copy(out_s.at[i], ref, out_sems.at[i]))
        stores[-1].start()

    for m in range(4):
        for load in loads[3 * m : 3 * m + 3]:
            load.wait()
        for a in (2 * m, 2 * m + 1):
            rows = slice(a * DOCS, (a + 1) * DOCS)
            far = slice((8 + a) * DOCS, (9 + a) * DOCS)
            col_own = jnp.broadcast_to(inv[a : a + 1, :], (DOCS, DOCS)).T
            col_oth = jnp.broadcast_to(inv[8 + a : 9 + a, :], (DOCS, DOCS)).T
            for b in range(8):
                near_key = inv[16 + b : 17 + b, :]
                far_key = inv[24 + b : 25 + b, :]
                keys = slice(b * DOCS, (b + 1) * DOCS)
                keys_far = slice((8 + b) * DOCS, (9 + b) * DOCS)
                w1 = (e_s[0, rows, keys].astype(F32) * (col_own + near_key)).astype(BF)
                w2 = (e_s[1, rows, keys].astype(F32) * (col_own + far_key)).astype(BF)
                w3 = (e_s[2, rows, keys].astype(F32) * (col_oth + near_key)).astype(BF)
                wq[rows, keys] = w1
                wq[rows, keys_far] = w2
                wk[rows, keys] = w1
                wk[far, keys] = w3
    for load in loads[12:22]:
        load.wait()
    for m in range(4):
        put(m, q_out[m], dot(wq[m * 256 : (m + 1) * 256, :], k_s[...]) * TAU_INV)
    for load in loads[22:]:
        load.wait()
    for m in range(4):
        put(4 + m, k_out[m], t_dot(wk[:, m * 256 : (m + 1) * 256], q_s[...]) * TAU_INV)
    for store in stores:
        store.wait()


def grads(q_near, q_far, k_near, k_far, e_in, row_in, col_in):
    return pl.pallas_call(
        grads_body,
        in_specs=[ANY] * 23 + [VMEM] * 8,
        out_specs=[ANY] * 8 + [VMEM],
        out_shape=[sds((256, EMB), BF)] * 8 + [sds((8, DOCS), F32)],
        scratch_shapes=[
            pltpu.VMEM((16 * DOCS, EMB), BF),
            pltpu.VMEM((16 * DOCS, EMB), BF),
            pltpu.VMEM((3, 8 * DOCS, 8 * DOCS), BF),
            pltpu.VMEM((8 * DOCS, 16 * DOCS), BF),
            pltpu.VMEM((16 * DOCS, 8 * DOCS), BF),
            pltpu.VMEM((8, 256, EMB), BF),
            pltpu.VMEM((32, DOCS), F32),
            pltpu.SemaphoreType.DMA((32,)),
            pltpu.SemaphoreType.DMA((8,)),
        ],
        compiler_params=params(),
    )(*q_near, *q_far, *k_near, *k_far, *e_in, *row_in, *col_in)


def half_block(which):
    return pl.BlockSpec((DOCS, EMB), lambda i: (which, 0))


def pass_body(*refs):
    for ins, out in ((refs[0:4], refs[8]), (refs[4:8], refs[9])):
        out[...] = sum(ref[...].astype(F32) for ref in ins).astype(BF)


def pass_on(query_in, key_in):
    return pl.pallas_call(
        pass_body,
        grid=(1,),
        in_specs=[half_block(1)] * 8,
        out_specs=[half_block(0)] * 2,
        out_shape=[sds((DOCS, EMB), BF)] * 2,
        compiler_params=params(),
    )(*query_in, *key_in)


def keep_body(*refs):
    q_parts, k_parts = refs[0:4], refs[4:8]
    q_unit, paired, q_perm, pos, inv, q_out, k_out = refs[8:15]
    hot = one_hot(pos[...])
    same = eye()
    pair = paired[...].astype(F32)
    score = jnp.sum(q_unit[...].astype(F32) * pair, axis=1, keepdims=True) * TAU_INV
    expo = jnp.exp(score)
    inv_r = jnp.sum(same * inv[0:1, :], axis=1, keepdims=True)
    inv_c = jnp.sum(hot * inv[1:2, :], axis=1, keepdims=True)
    weight = expo * inv_r + expo * inv_c - 2.0
    weight_k = jnp.sum(same * jnp.sum(hot * weight, axis=0, keepdims=True), axis=1, keepdims=True)
    for parts, w, pair_rows, out in (
        (q_parts, weight, pair, q_out),
        (k_parts, weight_k, q_perm[...].astype(F32), k_out),
    ):
        out[...] = sum(ref[...].astype(F32) for ref in parts) + (w * TAU_INV) * pair_rows


def keep(query_in, key_in, q_unit, paired, q_perm, pos, inv):
    return pl.pallas_call(
        keep_body,
        grid=(1,),
        in_specs=[half_block(0)] * 11 + [VMEM] * 2,
        out_specs=[half_block(0)] * 2,
        out_shape=[sds((DOCS, EMB), F32)] * 2,
        compiler_params=params(),
    )(*query_in, *key_in, q_unit, paired, q_perm, pos, inv)


def back_body(q_keep, q_got, k_keep, k_got, q_raw, k_raw, out):
    for kept, got, raw, start in ((q_keep, q_got, q_raw, 0), (k_keep, k_got, k_raw, DOCS)):
        grad = kept[...] + got[...].astype(F32)
        exact, scale = unit_of(raw[...])
        inner = jnp.sum(exact * grad, axis=1, keepdims=True)
        out[start : start + DOCS, :] = (scale * (grad - exact * inner)).astype(BF)


def back(*args):
    return pl.pallas_call(
        back_body,
        in_specs=[VMEM] * 6,
        out_specs=VMEM,
        out_shape=sds((2 * DOCS, EMB), BF),
        compiler_params=params(),
    )(*args)


FIRST = ((0, 0), (1, 0), (3, 0), (0, 1), (1, 1), (3, 1))


def contract_first_body(*refs):
    b_in, h_in, where, out = refs[0:6], refs[6], refs[7], refs[8]
    h_s, b_s, sems = refs[9:12]
    loads = []
    for i, (step, far) in enumerate(FIRST):
        source = ((where[2] - step) & 3) * 2 + (where[3] ^ far)
        loads.append((b_in[i], b_s.at[pl.ds(i * 256, 256)]))
        loads.append((h_in.at[source], h_s.at[:, pl.ds(i * 256, 256)]))
    loads = [pltpu.make_async_copy(s, d, sems.at[i]) for i, (s, d) in enumerate(loads)]
    for load in loads:
        load.start()
    for load in loads:
        load.wait()
    out[...] = dot(h_s[...], b_s[...])


def contract_first(b_in, h_in, where):
    return pl.pallas_call(
        contract_first_body,
        in_specs=[ANY] * 7 + [SMEM],
        out_specs=VMEM,
        out_shape=sds((512, EMB), F32),
        scratch_shapes=[
            pltpu.VMEM((512, 1536), BF),
            pltpu.VMEM((1536, EMB), BF),
            pltpu.SemaphoreType.DMA((12,)),
        ],
        compiler_params=params(),
    )(*b_in, h_in, where)


def contract_last_body(*refs):
    b_in, h_in, first, where, out = refs[0:4], refs[4], refs[5], refs[6], refs[7]
    h_s, b_s, t_s, sems = refs[8:12]
    loads = []
    for far in range(2):
        source = ((where[2] - 2) & 3) * 2 + (where[3] ^ far)
        loads.append((h_in.at[source], h_s.at[:, pl.ds(far * 256, 256)]))
        for part in range(2):
            i = far * 2 + part
            loads.append((b_in[i], b_s.at[pl.ds(i * DOCS, DOCS)]))
    loads.append((first, t_s))
    loads = [pltpu.make_async_copy(s, d, sems.at[i]) for i, (s, d) in enumerate(loads)]
    for load in loads:
        load.start()
    for load in loads:
        load.wait()
    out[...] = (t_s[...] + dot(h_s[...], b_s[...])).astype(BF)


def contract_last(b_in, h_in, first, where):
    return pl.pallas_call(
        contract_last_body,
        in_specs=[ANY] * 6 + [SMEM],
        out_specs=VMEM,
        out_shape=sds((512, EMB), BF),
        scratch_shapes=[
            pltpu.VMEM((512, 512), BF),
            pltpu.VMEM((512, EMB), BF),
            pltpu.VMEM((512, EMB), F32),
            pltpu.SemaphoreType.DMA((7,)),
        ],
        compiler_params=params(),
    )(*b_in, h_in, first, where)


def flip_slots(value):
    return value[:, ::-1]


def to_owners(parts, move):
    return [parts[0]] + [move(parts[(4 - step) % 4], step, 0) for step in (1, 2, 3)]


def local(hid_query, hid_key, projection, tile_rows, tile_cols, tile_count, positive):
    row_index = lax.axis_index("row")
    col_index = lax.axis_index("col")
    core_index = lax.axis_index("dp")
    x, z_hi = row_index // 2, row_index % 2
    y, z_lo = col_index // 2, col_index % 2
    where = jnp.stack([x, y, z_hi * 2 + z_lo, core_index]).astype(jnp.int32)

    q_unit, k_unit, q_raw, k_raw = project(hid_query, hid_key, projection)
    k_flip = move_key(k_unit, 0, 1)
    q_flip = move_query(q_unit, 0, 1)

    pos = (positive - ((row_index * 8 + col_index) * 2 + core_index) * DOCS).reshape(DOCS, 1)
    paired, q_perm, pos_rows = pair_up(q_unit, k_unit, pos)
    turned = jnp.concatenate([hid_query, hid_key], axis=0).T.reshape(4, 2, 4, 2, 2, 32, 256)
    turned = turned.transpose(1, 3, 4, 0, 2, 5, 6).reshape(4096, 256)
    entry_rows = tile_rows[0, 0]
    entry_cols = tile_cols[0, 0]
    used = jnp.arange(entry_rows.shape[0], dtype=jnp.int32) < tile_count[0, 0]
    slot_rows = ((y - entry_rows // 2) % 4) * 2 + (z_lo ^ (entry_rows % 2))
    slot_cols = ((x - entry_cols // 2) % 4) * 2 + (z_hi ^ (entry_cols % 2))
    eight = jnp.arange(8, dtype=jnp.int32)
    hit = (
        (slot_rows[:, None, None] == eight[None, :, None])
        & (slot_cols[:, None, None] == eight[None, None, :])
        & used[:, None, None]
    )
    mask = jnp.any(hit, axis=0).astype(F32)

    k_flip, q_flip, pos, paired, q_perm, pos_rows, turned, mask = lax.optimization_barrier(
        (k_flip, q_flip, pos, paired, q_perm, pos_rows, turned, mask)
    )
    k_pair = jnp.concatenate([k_unit, k_flip], axis=0)
    q_pair = jnp.concatenate([q_unit, q_flip], axis=0)
    k1 = move_key(k_pair, 1, 0)
    q1 = move_query(q_pair, 1, 0)
    k3 = move_key(k_pair, 3, 0)
    q3 = move_query(q_pair, 3, 0)
    k_far = swap(k_pair)
    k1, q1, k3, q3, k_far = lax.optimization_barrier((k1, q1, k3, q3, k_far))
    k_own = [
        k_pair,
        k1,
        move_key(k1[:DOCS], 1, 0),
        move_key(k3[DOCS:], 3, 0),
        k3,
    ]
    q_own = [
        q_pair,
        q1,
        move_query(q1[:DOCS], 1, 0),
        move_query(q3[DOCS:], 3, 0),
        q3,
    ]
    k1_far = swap(k1)
    k1_far, k3_late = lax.optimization_barrier((k1_far, k3))
    k3_far = swap(k3_late)
    k_oth = [k_far, k1_far, swap(k_own[2]), swap(k_own[3]), k3_far]

    e_own, e_oth, sums = scores(q_own, k_own, k_oth, mask, pos_rows)
    far = swap(sums)
    far, e_late, *q_late = lax.optimization_barrier((far, e_oth, *q_own))
    e_rcv = swap(e_late)
    q_oth = [swap(one) for one in q_late]
    row_part = jnp.concatenate([sums[:8], far[:8]], axis=0).reshape(8, 2, DOCS)
    col_part = sums[8:] + jnp.concatenate([far[16:], far[8:16]], axis=0)
    col_part = col_part.reshape(8, 2, DOCS)
    row_part = row_part + flip_slots(move_query(row_part, 0, 1))
    col_part = col_part + flip_slots(move_key(col_part, 0, 1))
    row_part = row_part.reshape(16, DOCS)
    col_part = col_part.reshape(16, DOCS)
    row_got = [row_part] + [move_query(row_part, step, 0) for step in (1, 2, 3)]
    col_got = [col_part] + [move_key(col_part, step, 0) for step in (1, 2, 3)]

    parts = grads(q_own, q_oth, k_own, k_oth, [e_own, e_oth, e_rcv], row_got, col_got)
    *parts, turned = lax.optimization_barrier((*parts, turned))
    h_all = lax.all_to_all(
        turned, ("row", "col", "dp"), 0, 0, tiled=True, axis_index_groups=Z_GROUPS
    ).reshape(8, 512, 256)
    inv = parts[8]
    query_in = to_owners(parts[:4], move_query)
    key_in = to_owners(parts[4:8], move_key)
    q_send, k_send = pass_on(query_in, key_in)
    q_got = move_query(q_send, 0, 1)
    k_got = move_key(k_send, 0, 1)
    q_keep, k_keep = keep(query_in, key_in, q_unit, paired, q_perm, pos, inv)
    b_own = back(q_keep, q_got, k_keep, k_got, q_raw, k_raw)
    b1 = move_z(b_own, 1)
    b3 = move_z(b_own, 3)
    b1, b3 = lax.optimization_barrier((b1, b3))
    b_last = [move_z(b1[:DOCS], 1), move_z(b3[DOCS:], 3)]
    b_first = [b_own, b1, b3]
    first = contract_first(b_first + [swap(one) for one in b_first], h_all, where)
    first, *b_last = lax.optimization_barrier((first, *b_last))
    out = contract_last(b_last + [swap(one) for one in b_last], h_all, first, where)
    out = lax.all_to_all(out, ("row", "col"), 0, 0, tiled=True, axis_index_groups=XY_GROUPS)
    return jnp.sum(out.reshape(16, 32, EMB).astype(F32), axis=0)


def solution(mesh):
    return jax.shard_map(
        local,
        mesh=mesh,
        in_specs=(
            P(("row", "col", "dp"), None),
            P(("row", "col", "dp"), None),
            P(),
            P("row", "col", None),
            P("row", "col", None),
            P("row", "col"),
            P(("row", "col", "dp")),
        ),
        out_specs=P(("row", "col", "dp"), None),
        check_vma=False,
    )
```

```python
import jax
import jax.numpy as jnp
from jax import lax
from jax.experimental import pallas as pl
from jax.experimental.pallas import tpu as pltpu
from jax.sharding import PartitionSpec as P

TAU_INV = 20.0
EPS = 1e-06
LOG2E = 1.4426950408889634
DOCS = 128
EMB = 1024
HID = 4096
BF = jnp.bfloat16
F32 = jnp.float32
VM = 56 * 1024 * 1024


def ring_pair(step, flip):
    return [(i, ((i // 2 + step) % 4) * 2 + ((i % 2) ^ flip)) for i in range(8)]


def move_query(value, step, flip):
    return lax.ppermute(value, "col", ring_pair(step, flip))


def move_key(value, step, flip):
    return lax.ppermute(value, "row", ring_pair(step, flip))


def chip(x, y, z):
    return (x * 2 + z // 2) * 8 + y * 2 + z % 2


PLANES = [
    [chip(x, y, z_hi * 2 + z_lo) for x in range(4) for z_hi in range(2) for y in range(4)]
    for z_lo in range(2)
]


def swap(value):
    return lax.ppermute(value, "dp", [(0, 1), (1, 0)])


def params():
    return pltpu.CompilerParams(vmem_limit_bytes=VM)


def sds(shape, dtype):
    return jax.ShapeDtypeStruct(shape, dtype)


ANY = pl.BlockSpec(memory_space=pl.ANY)
SMEM = pl.BlockSpec(memory_space=pltpu.SMEM)
VMEM = pl.BlockSpec(memory_space=pltpu.VMEM)


def dot(a, b):
    return lax.dot_general(a, b, (((1,), (0,)), ((), ())), preferred_element_type=F32)


def dot_t(a, b):
    return lax.dot_general(a, b, (((1,), (1,)), ((), ())), preferred_element_type=F32)


def t_dot(a, b):
    return lax.dot_general(a, b, (((0,), (0,)), ((), ())), preferred_element_type=F32)


def unit_of(raw):
    values = raw.astype(F32)
    scale = lax.rsqrt(jnp.sum(values * values, axis=1, keepdims=True) + EPS)
    return values * scale, scale


def project_body(hq, hk, proj, q_unit, k_unit, q_raw, k_raw, hid, acc):
    step = pl.program_id(0)
    hid[:DOCS, :] = hq[...]
    hid[DOCS:, :] = hk[...]
    part = dot(hid[...], proj[...])

    @pl.when(step == 0)
    def _():
        acc[...] = part

    @pl.when(step > 0)
    def _():
        acc[...] += part

    @pl.when(step == pl.num_programs(0) - 1)
    def _():
        for raw_ref, unit_ref, start in ((q_raw, q_unit, 0), (k_raw, k_unit, DOCS)):
            raw = acc[start : start + DOCS, :].astype(BF)
            raw_ref[...] = raw
            unit_ref[...] = unit_of(raw)[0].astype(BF)


def project(hid_query, hid_key, projection):
    depth = 1024
    whole = pl.BlockSpec((DOCS, EMB), lambda i: (0, 0))
    return pl.pallas_call(
        project_body,
        grid=(HID // depth,),
        in_specs=[
            pl.BlockSpec((DOCS, depth), lambda i: (0, i)),
            pl.BlockSpec((DOCS, depth), lambda i: (0, i)),
            pl.BlockSpec((depth, EMB), lambda i: (i, 0)),
        ],
        out_specs=[whole] * 4,
        out_shape=[sds((DOCS, EMB), BF)] * 4,
        scratch_shapes=[pltpu.VMEM((2 * DOCS, depth), BF), pltpu.VMEM((2 * DOCS, EMB), F32)],
        compiler_params=params(),
    )(hid_query, hid_key, projection)


def one_hot(pos):
    lane = lax.broadcasted_iota(jnp.int32, (DOCS, DOCS), 1)
    return (lane == pos).astype(F32)


def eye():
    lane = lax.broadcasted_iota(jnp.int32, (DOCS, DOCS), 1)
    row = lax.broadcasted_iota(jnp.int32, (DOCS, DOCS), 0)
    return (lane == row).astype(F32)


def pairs_body(q_unit, k_unit, pos, paired, q_perm, pos_rows):
    hot = one_hot(pos[...])
    hot_bf = hot.astype(BF)
    pair = dot(hot_bf, k_unit[...])
    paired[...] = pair.astype(BF)
    q_perm[...] = t_dot(hot_bf, q_unit[...]).astype(BF)
    score = jnp.sum(q_unit[...].astype(F32) * pair, axis=1, keepdims=True) * TAU_INV
    expo = jnp.exp(score)
    pos_rows[0:1, :] = jnp.sum(eye() * expo, axis=0, keepdims=True)
    pos_rows[1:2, :] = jnp.sum(hot * expo, axis=0, keepdims=True)
    pos_rows[2:8, :] = jnp.zeros((6, DOCS), F32)


def pair_up(q_unit, k_unit, pos):
    return pl.pallas_call(
        pairs_body,
        in_specs=[VMEM] * 3,
        out_specs=[VMEM] * 3,
        out_shape=[sds((DOCS, EMB), BF), sds((DOCS, EMB), BF), sds((8, DOCS), F32)],
        compiler_params=params(),
    )(q_unit, k_unit, pos)


PARTS = ((0, 256), (256, 256), (512, 128), (640, 128), (768, 256))


def block_copies(ins, scratch, sems, first, row):
    copies = []
    for i, (start, rows) in enumerate(PARTS):
        target = scratch.at[pl.ds(row + start, rows)]
        copies.append(pltpu.make_async_copy(ins[i], target, sems.at[first + i]))
    return copies


def scores_body(*refs):
    q_in, k_near, k_far = refs[0:5], refs[5:10], refs[10:15]
    mask, pos_rows = refs[15:17]
    e_own, mix, sums = refs[17:20]
    q_s, k_s, e_s, acc, in_sems, out_sems = refs[20:26]
    q_loads = block_copies(q_in, q_s, in_sems, 0, 0)
    k_loads = block_copies(k_near, k_s, in_sems, 5, 0) + block_copies(k_far, k_s, in_sems, 10, 1024)
    for load in k_loads[:1] + q_loads:
        load.start()
    waits = ((0,), (1,), (2, 3), (4,), (5,), (6,), (7, 8), (9,))
    stores = []
    for b in range(8):
        for i in waits[b]:
            k_loads[i].wait()
        total = [None, None]
        for m in range(4):
            if b == 0:
                for i in waits[m]:
                    q_loads[i].wait()
                if m == 3:
                    for load in k_loads[1:]:
                        load.start()
            chunk = slice(m * 256, (m + 1) * 256)
            score = dot_t(q_s[chunk, :], k_s[b * 256 : (b + 1) * 256, :])
            for n in range(2):
                a = m * 2 + n
                rows = slice(a * DOCS, (a + 1) * DOCS)
                expo = jnp.exp2(score[n * DOCS : (n + 1) * DOCS, :] * (TAU_INV * LOG2E))
                both = None
                for half in range(2):
                    slot = (b % 4) * 2 + half
                    one = expo[:, half * DOCS : (half + 1) * DOCS] * mask[a, slot]
                    e_s[b, rows, half * DOCS : (half + 1) * DOCS] = one.astype(BF)
                    both = one if half == 0 else both + one
                    part = one.reshape(16, 8, DOCS).sum(axis=0)
                    total[half] = part if a == 0 else total[half] + part
                if b == 0:
                    acc[rows, :] = both
                else:
                    acc[rows, :] += both
        out = (e_own if b < 4 else mix).at[pl.ds(0, 1024), pl.ds((b % 4) * 256, 256)]
        stores.append(pltpu.make_async_copy(e_s.at[b], out, out_sems.at[b]))
        stores[-1].start()
        if b == 0:
            stores.append(pltpu.make_async_copy(q_s, mix.at[pl.ds(1024, 1024)], out_sems.at[8]))
            stores[-1].start()
        for half in range(2):
            col = jnp.sum(total[half], axis=0, keepdims=True)
            if b == 0 and half == 0:
                col = col + pos_rows[1:2, :]
            sums[8 + 2 * b + half : 9 + 2 * b + half, :] = col
    for a in range(8):
        part = jnp.sum(acc[a * DOCS : (a + 1) * DOCS, :].T, axis=0, keepdims=True)
        if a == 0:
            part = part + pos_rows[0:1, :]
        sums[a : a + 1, :] = part
    for store in stores:
        store.wait()


def scores(q_in, k_near, k_far, mask, pos_rows):
    return pl.pallas_call(
        scores_body,
        in_specs=[ANY] * 15 + [SMEM, VMEM],
        out_specs=[ANY, ANY, VMEM],
        out_shape=[
            sds((8 * DOCS, 8 * DOCS), BF),
            sds((16 * DOCS, 8 * DOCS), BF),
            sds((24, DOCS), F32),
        ],
        scratch_shapes=[
            pltpu.VMEM((8 * DOCS, EMB), BF),
            pltpu.VMEM((16 * DOCS, EMB), BF),
            pltpu.VMEM((8, 8 * DOCS, 256), BF),
            pltpu.VMEM((8 * DOCS, DOCS), F32),
            pltpu.SemaphoreType.DMA((15,)),
            pltpu.SemaphoreType.DMA((9,)),
        ],
        compiler_params=params(),
    )(*q_in, *k_near, *k_far, mask, pos_rows)


def grads_body(*refs):
    k_near, k_far = refs[0:5], refs[5:10]
    e_own, mix, mix_far, row_in, col_in = refs[10], refs[11], refs[12], refs[13:17], refs[17:21]
    q_out, k_out, inv_out = refs[21:25], refs[25:29], refs[29]
    q_s, k_s, e_s, wq, wk, out_s, inv, sems, out_sems = refs[30:39]
    e_loads = []
    for m in range(4):
        rows = pl.ds(m * 256, 256)
        for i, ref in enumerate((e_own, mix, mix_far)):
            one = (ref.at[rows], e_s.at[i, rows], sems.at[3 * m + i])
            e_loads.append(pltpu.make_async_copy(*one))
    k_loads = block_copies(k_near, k_s, sems, 12, 0) + block_copies(k_far, k_s, sems, 17, 1024)
    q_loads = []
    for i, ref in enumerate((mix, mix_far)):
        one = (ref.at[pl.ds(1024, 1024)], q_s.at[pl.ds(i * 1024, 1024)], sems.at[22 + i])
        q_loads.append(pltpu.make_async_copy(*one))
    for load in e_loads[:3] + k_loads:
        load.start()
    for at, ins in ((0, row_in), (16, col_in)):
        for rel in range(2):
            for slot in range(8):
                total = ins[0][rel * 8 + slot : rel * 8 + slot + 1, :]
                for step in (1, 2, 3):
                    src = rel * 8 + (slot - 2 * step) % 8
                    total = total + ins[step][src : src + 1, :]
                dst = at + rel * 8 + slot
                inv[dst : dst + 1, :] = 1.0 / total
    inv_out[0:1, :] = inv[0:1, :]
    inv_out[1:2, :] = inv[16:17, :]
    inv_out[2:8, :] = jnp.zeros((6, DOCS), F32)
    stores = []

    def put(i, ref, grad):
        out_s[i] = grad.astype(BF)
        stores.append(pltpu.make_async_copy(out_s.at[i], ref, out_sems.at[i]))
        stores[-1].start()

    for m in range(4):
        for load in e_loads[3 * m : 3 * m + 3]:
            load.wait()
        for a in (2 * m, 2 * m + 1):
            rows = slice(a * DOCS, (a + 1) * DOCS)
            far = slice((8 + a) * DOCS, (9 + a) * DOCS)
            col_own = jnp.broadcast_to(inv[a : a + 1, :], (DOCS, DOCS)).T
            col_oth = jnp.broadcast_to(inv[8 + a : 9 + a, :], (DOCS, DOCS)).T
            for b in range(8):
                near_key = inv[16 + b : 17 + b, :]
                far_key = inv[24 + b : 25 + b, :]
                keys = slice(b * DOCS, (b + 1) * DOCS)
                keys_far = slice((8 + b) * DOCS, (9 + b) * DOCS)
                w1 = (e_s[0, rows, keys].astype(F32) * (col_own + near_key)).astype(BF)
                w2 = (e_s[1, rows, keys].astype(F32) * (col_own + far_key)).astype(BF)
                w3 = (e_s[2, rows, keys].astype(F32) * (col_oth + near_key)).astype(BF)
                wq[rows, keys] = w1
                wq[rows, keys_far] = w2
                wk[rows, keys] = w1
                wk[far, keys] = w3
        if m == 0:
            for load in k_loads:
                load.wait()
            for load in e_loads[3:] + q_loads:
                load.start()
        put(m, q_out[m], dot(wq[m * 256 : (m + 1) * 256, :], k_s[...]) * TAU_INV)
    for load in q_loads:
        load.wait()
    for m in range(4):
        put(4 + m, k_out[m], t_dot(wk[:, m * 256 : (m + 1) * 256], q_s[...]) * TAU_INV)
    for store in stores:
        store.wait()


def grads(k_near, k_far, e_own, mix, mix_far, row_in, col_in):
    return pl.pallas_call(
        grads_body,
        in_specs=[ANY] * 13 + [VMEM] * 8,
        out_specs=[ANY] * 8 + [VMEM],
        out_shape=[sds((256, EMB), BF)] * 8 + [sds((8, DOCS), F32)],
        scratch_shapes=[
            pltpu.VMEM((16 * DOCS, EMB), BF),
            pltpu.VMEM((16 * DOCS, EMB), BF),
            pltpu.VMEM((3, 8 * DOCS, 8 * DOCS), BF),
            pltpu.VMEM((8 * DOCS, 16 * DOCS), BF),
            pltpu.VMEM((16 * DOCS, 8 * DOCS), BF),
            pltpu.VMEM((8, 256, EMB), BF),
            pltpu.VMEM((32, DOCS), F32),
            pltpu.SemaphoreType.DMA((24,)),
            pltpu.SemaphoreType.DMA((8,)),
        ],
        compiler_params=params(),
    )(*k_near, *k_far, e_own, mix, mix_far, *row_in, *col_in)


def half_block(which):
    return pl.BlockSpec((DOCS, EMB), lambda i: (which, 0))


def pass_body(*refs):
    for ins, out in ((refs[0:4], refs[8]), (refs[4:8], refs[9])):
        out[...] = sum(ref[...].astype(F32) for ref in ins).astype(BF)


def pass_on(query_in, key_in):
    return pl.pallas_call(
        pass_body,
        grid=(1,),
        in_specs=[half_block(1)] * 8,
        out_specs=[half_block(0)] * 2,
        out_shape=[sds((DOCS, EMB), BF)] * 2,
        compiler_params=params(),
    )(*query_in, *key_in)


def keep_body(*refs):
    q_parts, k_parts = refs[0:4], refs[4:8]
    q_unit, paired, q_perm, pos, inv, q_out, k_out = refs[8:15]
    hot = one_hot(pos[...])
    same = eye()
    pair = paired[...].astype(F32)
    score = jnp.sum(q_unit[...].astype(F32) * pair, axis=1, keepdims=True) * TAU_INV
    expo = jnp.exp(score)
    inv_r = jnp.sum(same * inv[0:1, :], axis=1, keepdims=True)
    inv_c = jnp.sum(hot * inv[1:2, :], axis=1, keepdims=True)
    weight = expo * inv_r + expo * inv_c - 2.0
    weight_k = jnp.sum(same * jnp.sum(hot * weight, axis=0, keepdims=True), axis=1, keepdims=True)
    for parts, w, pair_rows, out in (
        (q_parts, weight, pair, q_out),
        (k_parts, weight_k, q_perm[...].astype(F32), k_out),
    ):
        out[...] = sum(ref[...].astype(F32) for ref in parts) + (w * TAU_INV) * pair_rows


def keep(query_in, key_in, q_unit, paired, q_perm, pos, inv):
    return pl.pallas_call(
        keep_body,
        grid=(1,),
        in_specs=[half_block(0)] * 11 + [VMEM] * 2,
        out_specs=[half_block(0)] * 2,
        out_shape=[sds((DOCS, EMB), F32)] * 2,
        compiler_params=params(),
    )(*query_in, *key_in, q_unit, paired, q_perm, pos, inv)


def back_body(q_keep, q_got, k_keep, k_got, q_raw, k_raw, out):
    for kept, got, raw, start in ((q_keep, q_got, q_raw, 0), (k_keep, k_got, k_raw, DOCS)):
        grad = kept[...] + got[...].astype(F32)
        exact, scale = unit_of(raw[...])
        inner = jnp.sum(exact * grad, axis=1, keepdims=True)
        out[start : start + DOCS, :] = (scale * (grad - exact * inner)).astype(BF)


def back(*args):
    return pl.pallas_call(
        back_body,
        in_specs=[VMEM] * 6,
        out_specs=VMEM,
        out_shape=sds((2 * DOCS, EMB), BF),
        compiler_params=params(),
    )(*args)


def contract_body(*refs):
    b_in, h_all, h_in, where, out = refs[0:4], refs[4], refs[5:8], refs[8], refs[9]
    h_s, b_s, o_s, sems, out_sems = refs[10:15]
    sources = (h_all.at[where[0]],) + tuple(h_in)
    loads = []
    for i in range(4):
        loads.append((b_in[i], b_s.at[pl.ds(i * 256, 256)]))
        loads.append((sources[i], h_s.at[:, pl.ds(i * 256, 256)]))
    loads = [pltpu.make_async_copy(s, d, sems.at[i]) for i, (s, d) in enumerate(loads)]
    for load in loads:
        load.start()
    for load in loads:
        load.wait()
    stores = []
    for m in range(4):
        rows = pl.ds(m * 256, 256)
        o_s[rows, :] = dot(h_s[rows, :], b_s[...]).astype(BF)
        stores.append(pltpu.make_async_copy(o_s.at[rows], out.at[rows], out_sems.at[m]))
        stores[-1].start()
    for store in stores:
        store.wait()


def contract(b_in, h_all, h_in, where):
    return pl.pallas_call(
        contract_body,
        in_specs=[ANY] * 8 + [SMEM],
        out_specs=ANY,
        out_shape=sds((1024, EMB), BF),
        scratch_shapes=[
            pltpu.VMEM((1024, 1024), BF),
            pltpu.VMEM((1024, EMB), BF),
            pltpu.VMEM((1024, EMB), BF),
            pltpu.SemaphoreType.DMA((8,)),
            pltpu.SemaphoreType.DMA((4,)),
        ],
        compiler_params=params(),
    )(*b_in, h_all, *h_in, where)


def flip_slots(value):
    return value[:, ::-1]


def to_owners(parts, move):
    return [parts[0]] + [move(parts[(4 - step) % 4], step, 0) for step in (1, 2, 3)]


def local(hid_query, hid_key, projection, tile_rows, tile_cols, tile_count, positive):
    row_index = lax.axis_index("row")
    col_index = lax.axis_index("col")
    core_index = lax.axis_index("dp")
    x, z_hi = row_index // 2, row_index % 2
    y, z_lo = col_index // 2, col_index % 2
    quarter = z_lo * 2 + core_index

    q_unit, k_unit, q_raw, k_raw = project(hid_query, hid_key, projection)
    k_flip = move_key(k_unit, 0, 1)
    q_flip = move_query(q_unit, 0, 1)

    pos = (positive - ((row_index * 8 + col_index) * 2 + core_index) * DOCS).reshape(DOCS, 1)
    paired, q_perm, pos_rows = pair_up(q_unit, k_unit, pos)
    turned = jnp.concatenate([hid_query, hid_key], axis=0).T.reshape(4, 2, 4, 2, 2, 32, 256)
    turned = turned.transpose(3, 4, 0, 1, 2, 5, 6).reshape(4, 1024, 256)
    h_flip = lax.dynamic_index_in_dim(turned, quarter ^ 2, 0, keepdims=False)
    h_both = lax.dynamic_index_in_dim(turned, quarter ^ 3, 0, keepdims=False)
    h_core = lax.dynamic_index_in_dim(turned, quarter ^ 1, 0, keepdims=False)
    entry_rows = tile_rows[0, 0]
    entry_cols = tile_cols[0, 0]
    used = jnp.arange(entry_rows.shape[0], dtype=jnp.int32) < tile_count[0, 0]
    slot_rows = ((y - entry_rows // 2) % 4) * 2 + (z_lo ^ (entry_rows % 2))
    slot_cols = ((x - entry_cols // 2) % 4) * 2 + (z_hi ^ (entry_cols % 2))
    eight = jnp.arange(8, dtype=jnp.int32)
    hit = (
        (slot_rows[:, None, None] == eight[None, :, None])
        & (slot_cols[:, None, None] == eight[None, None, :])
        & used[:, None, None]
    )
    mask = jnp.any(hit, axis=0).astype(F32)

    k_flip, q_flip, pos, paired, q_perm, pos_rows, turned, h_flip, h_both, h_core, mask = (
        lax.optimization_barrier(
            (k_flip, q_flip, pos, paired, q_perm, pos_rows, turned, h_flip, h_both, h_core, mask)
        )
    )
    k_pair = jnp.concatenate([k_unit, k_flip], axis=0)
    q_pair = jnp.concatenate([q_unit, q_flip], axis=0)
    k1 = move_key(k_pair, 1, 0)
    q1 = move_query(q_pair, 1, 0)
    k3 = move_key(k_pair, 3, 0)
    q3 = move_query(q_pair, 3, 0)
    k_far = swap(k_pair)
    k1, q1, k3, q3, k_far = lax.optimization_barrier((k1, q1, k3, q3, k_far))
    k_own = [
        k_pair,
        k1,
        move_key(k1[:DOCS], 1, 0),
        move_key(k3[DOCS:], 3, 0),
        k3,
    ]
    q_own = [
        q_pair,
        q1,
        move_query(q1[:DOCS], 1, 0),
        move_query(q3[DOCS:], 3, 0),
        q3,
    ]
    k1_far = swap(k1)
    k1_far, k3_late = lax.optimization_barrier((k1_far, k3))
    k3_far = swap(k3_late)
    k_oth = [k_far, k1_far, swap(k_own[2]), swap(k_own[3]), k3_far]

    h_flip, *blocks = lax.optimization_barrier((h_flip, *q_own, *k_oth))
    q_own, k_oth = blocks[:5], blocks[5:]
    h_flip = move_query(h_flip, 0, 1)
    e_own, mix, sums = scores(q_own, k_own, k_oth, mask, pos_rows)
    sums, mix, h_flip = lax.optimization_barrier((sums, mix, h_flip))
    far = swap(sums)
    far, mix = lax.optimization_barrier((far, mix))
    mix_far = swap(mix)
    row_part = jnp.concatenate([sums[:8], far[:8]], axis=0).reshape(8, 2, DOCS)
    col_part = sums[8:] + jnp.concatenate([far[16:], far[8:16]], axis=0)
    col_part = col_part.reshape(8, 2, DOCS)
    row_part = row_part + flip_slots(move_query(row_part, 0, 1))
    col_part = col_part + flip_slots(move_key(col_part, 0, 1))
    row_part = row_part.reshape(16, DOCS)
    col_part = col_part.reshape(16, DOCS)
    row_got = [row_part] + [move_query(row_part, step, 0) for step in (1, 2, 3)]
    col_got = [col_part] + [move_key(col_part, step, 0) for step in (1, 2, 3)]

    h_both, h_core, *got = lax.optimization_barrier((h_both, h_core, *row_got, *col_got))
    h_both = move_query(h_both, 0, 1)
    parts = grads(k_own, k_oth, e_own, mix, mix_far, got[:4], got[4:])
    h_both, *parts = lax.optimization_barrier((h_both, *parts))
    inv = parts[8]
    query_in = to_owners(parts[:4], move_query)
    key_in = to_owners(parts[4:8], move_key)
    q_send, k_send = pass_on(query_in, key_in)
    q_got = move_query(q_send, 0, 1)
    k_got = move_key(k_send, 0, 1)
    q_keep, k_keep = keep(query_in, key_in, q_unit, paired, q_perm, pos, inv)
    b_own = back(q_keep, q_got, k_keep, k_got, q_raw, k_raw)
    b_flip = move_query(b_own, 0, 1)
    out = contract(
        [b_own, swap(b_own), b_flip, swap(b_flip)],
        turned,
        [swap(h_core), h_flip, swap(h_both)],
        quarter.reshape(1).astype(jnp.int32),
    )
    out = lax.all_to_all(out, ("row", "col"), 0, 0, tiled=True, axis_index_groups=PLANES)
    return jnp.sum(out.reshape(32, 32, EMB).astype(F32), axis=0)


def solution(mesh):
    return jax.shard_map(
        local,
        mesh=mesh,
        in_specs=(
            P(("row", "col", "dp"), None),
            P(("row", "col", "dp"), None),
            P(),
            P("row", "col", None),
            P("row", "col", None),
            P("row", "col"),
            P(("row", "col", "dp")),
        ),
        out_specs=P(("row", "col", "dp"), None),
        check_vma=False,
    )
```

```python
import jax
import jax.numpy as jnp
from jax import lax
from jax.experimental import pallas as pl
from jax.experimental.pallas import tpu as pltpu
from jax.sharding import PartitionSpec as P

TAU_INV = 20.0
EPS = 1e-06
LOG2E = 1.4426950408889634
DOCS = 128
EMB = 1024
HID = 4096
BF = jnp.bfloat16
F32 = jnp.float32
VM = 56 * 1024 * 1024


def ring_pair(step, flip):
    return [(i, ((i // 2 + step) % 4) * 2 + ((i % 2) ^ flip)) for i in range(8)]


def move_query(value, step, flip):
    return lax.ppermute(value, "col", ring_pair(step, flip))


def move_key(value, step, flip):
    return lax.ppermute(value, "row", ring_pair(step, flip))


def chip(x, y, z):
    return (x * 2 + z // 2) * 8 + y * 2 + z % 2


PLANES = [
    [chip(x, y, z_hi * 2 + z_lo) for x in range(4) for z_hi in range(2) for y in range(4)]
    for z_lo in range(2)
]


def swap(value):
    return lax.ppermute(value, "dp", [(0, 1), (1, 0)])


def params():
    return pltpu.CompilerParams(vmem_limit_bytes=VM)


def sds(shape, dtype):
    return jax.ShapeDtypeStruct(shape, dtype)


ANY = pl.BlockSpec(memory_space=pl.ANY)
SMEM = pl.BlockSpec(memory_space=pltpu.SMEM)
VMEM = pl.BlockSpec(memory_space=pltpu.VMEM)


def dot(a, b):
    return lax.dot_general(a, b, (((1,), (0,)), ((), ())), preferred_element_type=F32)


def dot_t(a, b):
    return lax.dot_general(a, b, (((1,), (1,)), ((), ())), preferred_element_type=F32)


def t_dot(a, b):
    return lax.dot_general(a, b, (((0,), (0,)), ((), ())), preferred_element_type=F32)


def unit_of(raw):
    values = raw.astype(F32)
    scale = lax.rsqrt(jnp.sum(values * values, axis=1, keepdims=True) + EPS)
    return values * scale, scale


def project_body(hq, hk, proj, q_unit, k_unit, q_raw, k_raw, hid, acc):
    step = pl.program_id(0)
    hid[:DOCS, :] = hq[...]
    hid[DOCS:, :] = hk[...]
    part = dot(hid[...], proj[...])

    @pl.when(step == 0)
    def _():
        acc[...] = part

    @pl.when(step > 0)
    def _():
        acc[...] += part

    @pl.when(step == pl.num_programs(0) - 1)
    def _():
        for raw_ref, unit_ref, start in ((q_raw, q_unit, 0), (k_raw, k_unit, DOCS)):
            raw = acc[start : start + DOCS, :].astype(BF)
            raw_ref[...] = raw
            unit_ref[...] = unit_of(raw)[0].astype(BF)


def project(hid_query, hid_key, projection):
    depth = 1024
    whole = pl.BlockSpec((DOCS, EMB), lambda i: (0, 0))
    return pl.pallas_call(
        project_body,
        grid=(HID // depth,),
        in_specs=[
            pl.BlockSpec((DOCS, depth), lambda i: (0, i)),
            pl.BlockSpec((DOCS, depth), lambda i: (0, i)),
            pl.BlockSpec((depth, EMB), lambda i: (i, 0)),
        ],
        out_specs=[whole] * 4,
        out_shape=[sds((DOCS, EMB), BF)] * 4,
        scratch_shapes=[pltpu.VMEM((2 * DOCS, depth), BF), pltpu.VMEM((2 * DOCS, EMB), F32)],
        compiler_params=params(),
    )(hid_query, hid_key, projection)


def one_hot(pos):
    lane = lax.broadcasted_iota(jnp.int32, (DOCS, DOCS), 1)
    return (lane == pos).astype(F32)


def eye():
    lane = lax.broadcasted_iota(jnp.int32, (DOCS, DOCS), 1)
    row = lax.broadcasted_iota(jnp.int32, (DOCS, DOCS), 0)
    return (lane == row).astype(F32)


def pairs_body(q_unit, k_unit, pos, paired, q_perm, pos_rows):
    hot = one_hot(pos[...])
    hot_bf = hot.astype(BF)
    pair = dot(hot_bf, k_unit[...])
    paired[...] = pair.astype(BF)
    q_perm[...] = t_dot(hot_bf, q_unit[...]).astype(BF)
    score = jnp.sum(q_unit[...].astype(F32) * pair, axis=1, keepdims=True) * TAU_INV
    expo = jnp.exp(score)
    pos_rows[0:1, :] = jnp.sum(eye() * expo, axis=0, keepdims=True)
    pos_rows[1:2, :] = jnp.sum(hot * expo, axis=0, keepdims=True)
    pos_rows[2:8, :] = jnp.zeros((6, DOCS), F32)


def pair_up(q_unit, k_unit, pos):
    return pl.pallas_call(
        pairs_body,
        in_specs=[VMEM] * 3,
        out_specs=[VMEM] * 3,
        out_shape=[sds((DOCS, EMB), BF), sds((DOCS, EMB), BF), sds((8, DOCS), F32)],
        compiler_params=params(),
    )(q_unit, k_unit, pos)


PARTS = ((0, 256), (256, 256), (512, 128), (640, 128), (768, 256))


def block_copies(ins, scratch, sems, first, row):
    copies = []
    for i, (start, rows) in enumerate(PARTS):
        target = scratch.at[pl.ds(row + start, rows)]
        copies.append(pltpu.make_async_copy(ins[i], target, sems.at[first + i]))
    return copies


def scores_body(*refs):
    q_in, k_near, k_far = refs[0:5], refs[5:10], refs[10:15]
    mask, pos_rows = refs[15:17]
    e_own, mix, sums = refs[17:20]
    q_s, k_s, e_s, acc, in_sems, out_sems = refs[20:26]
    q_loads = block_copies(q_in, q_s, in_sems, 0, 0)
    k_loads = block_copies(k_near, k_s, in_sems, 5, 0) + block_copies(k_far, k_s, in_sems, 10, 1024)
    for load in k_loads[:1] + q_loads + k_loads[1:]:
        load.start()
    waits = ((0,), (1,), (2, 3), (4,), (5,), (6,), (7, 8), (9,))

    def score_of(b, m):
        if m == 0:
            for i in waits[b]:
                k_loads[i].wait()
        if b == 0:
            for i in waits[m]:
                q_loads[i].wait()
        return dot_t(q_s[m * 256 : (m + 1) * 256, :], k_s[b * 256 : (b + 1) * 256, :])

    stores = []
    following = score_of(0, 0)
    for b in range(8):
        total = [None, None]
        for m in range(4):
            score = following
            if m < 3 or b < 7:
                following = score_of(b + (m + 1) // 4, (m + 1) % 4)
            for n in range(2):
                a = m * 2 + n
                rows = slice(a * DOCS, (a + 1) * DOCS)
                expo = jnp.exp2(score[n * DOCS : (n + 1) * DOCS, :] * (TAU_INV * LOG2E))
                both = None
                for half in range(2):
                    slot = (b % 4) * 2 + half
                    one = expo[:, half * DOCS : (half + 1) * DOCS] * mask[a, slot]
                    e_s[b, rows, half * DOCS : (half + 1) * DOCS] = one.astype(BF)
                    both = one if half == 0 else both + one
                    part = one.reshape(16, 8, DOCS).sum(axis=0)
                    total[half] = part if a == 0 else total[half] + part
                if b == 0:
                    acc[rows, :] = both
                else:
                    acc[rows, :] += both
        out = (e_own if b < 4 else mix).at[pl.ds(0, 1024), pl.ds((b % 4) * 256, 256)]
        stores.append(pltpu.make_async_copy(e_s.at[b], out, out_sems.at[b]))
        stores[-1].start()
        if b == 0:
            stores.append(pltpu.make_async_copy(q_s, mix.at[pl.ds(1024, 1024)], out_sems.at[8]))
            stores[-1].start()
        for half in range(2):
            col = jnp.sum(total[half], axis=0, keepdims=True)
            if b == 0 and half == 0:
                col = col + pos_rows[1:2, :]
            sums[8 + 2 * b + half : 9 + 2 * b + half, :] = col
    for a in range(8):
        part = jnp.sum(acc[a * DOCS : (a + 1) * DOCS, :].T, axis=0, keepdims=True)
        if a == 0:
            part = part + pos_rows[0:1, :]
        sums[a : a + 1, :] = part
    for store in stores:
        store.wait()


def scores(q_in, k_near, k_far, mask, pos_rows):
    return pl.pallas_call(
        scores_body,
        in_specs=[ANY] * 15 + [SMEM, VMEM],
        out_specs=[ANY, ANY, VMEM],
        out_shape=[
            sds((8 * DOCS, 8 * DOCS), BF),
            sds((16 * DOCS, 8 * DOCS), BF),
            sds((24, DOCS), F32),
        ],
        scratch_shapes=[
            pltpu.VMEM((8 * DOCS, EMB), BF),
            pltpu.VMEM((16 * DOCS, EMB), BF),
            pltpu.VMEM((8, 8 * DOCS, 256), BF),
            pltpu.VMEM((8 * DOCS, DOCS), F32),
            pltpu.SemaphoreType.DMA((15,)),
            pltpu.SemaphoreType.DMA((9,)),
        ],
        compiler_params=params(),
    )(*q_in, *k_near, *k_far, mask, pos_rows)


def grads_body(*refs):
    k_near, k_far = refs[0:5], refs[5:10]
    e_own, mix, mix_far, row_in, col_in = refs[10], refs[11], refs[12], refs[13:17], refs[17:21]
    q_out, k_out, inv_out = refs[21:25], refs[25:29], refs[29]
    q_s, k_s, e_s, wq, wk, out_s, inv, sems, out_sems = refs[30:39]
    e_loads = []
    for m in range(4):
        rows = pl.ds(m * 256, 256)
        for i, ref in enumerate((e_own, mix, mix_far)):
            one = (ref.at[rows], e_s.at[i, rows], sems.at[3 * m + i])
            e_loads.append(pltpu.make_async_copy(*one))
    k_loads = block_copies(k_near, k_s, sems, 12, 0) + block_copies(k_far, k_s, sems, 17, 1024)
    q_loads = []
    for i, ref in enumerate((mix, mix_far)):
        one = (ref.at[pl.ds(1024, 1024)], q_s.at[pl.ds(i * 1024, 1024)], sems.at[22 + i])
        q_loads.append(pltpu.make_async_copy(*one))
    for load in e_loads[:3] + k_loads:
        load.start()
    for at, ins in ((0, row_in), (16, col_in)):
        for rel in range(2):
            for slot in range(8):
                total = ins[0][rel * 8 + slot : rel * 8 + slot + 1, :]
                for step in (1, 2, 3):
                    src = rel * 8 + (slot - 2 * step) % 8
                    total = total + ins[step][src : src + 1, :]
                dst = at + rel * 8 + slot
                inv[dst : dst + 1, :] = 1.0 / total
    inv_out[0:1, :] = inv[0:1, :]
    inv_out[1:2, :] = inv[16:17, :]
    inv_out[2:8, :] = jnp.zeros((6, DOCS), F32)
    stores = []

    def put(i, ref, grad):
        out_s[i] = grad.astype(BF)
        stores.append(pltpu.make_async_copy(out_s.at[i], ref, out_sems.at[i]))
        stores[-1].start()

    for m in range(4):
        for load in e_loads[3 * m : 3 * m + 3]:
            load.wait()
        for a in (2 * m, 2 * m + 1):
            rows = slice(a * DOCS, (a + 1) * DOCS)
            far = slice((8 + a) * DOCS, (9 + a) * DOCS)
            col_own = jnp.broadcast_to(inv[a : a + 1, :], (DOCS, DOCS)).T
            col_oth = jnp.broadcast_to(inv[8 + a : 9 + a, :], (DOCS, DOCS)).T
            for b in range(8):
                near_key = inv[16 + b : 17 + b, :]
                far_key = inv[24 + b : 25 + b, :]
                keys = slice(b * DOCS, (b + 1) * DOCS)
                keys_far = slice((8 + b) * DOCS, (9 + b) * DOCS)
                w1 = (e_s[0, rows, keys].astype(F32) * (col_own + near_key)).astype(BF)
                w2 = (e_s[1, rows, keys].astype(F32) * (col_own + far_key)).astype(BF)
                w3 = (e_s[2, rows, keys].astype(F32) * (col_oth + near_key)).astype(BF)
                wq[rows, keys] = w1
                wq[rows, keys_far] = w2
                wk[rows, keys] = w1
                wk[far, keys] = w3
        if m == 0:
            for load in k_loads:
                load.wait()
            for load in e_loads[3:] + q_loads:
                load.start()
        put(m, q_out[m], dot(wq[m * 256 : (m + 1) * 256, :], k_s[...]) * TAU_INV)
    for load in q_loads:
        load.wait()
    for m in range(4):
        put(4 + m, k_out[m], t_dot(wk[:, m * 256 : (m + 1) * 256], q_s[...]) * TAU_INV)
    for store in stores:
        store.wait()


def grads(k_near, k_far, e_own, mix, mix_far, row_in, col_in):
    return pl.pallas_call(
        grads_body,
        in_specs=[ANY] * 13 + [VMEM] * 8,
        out_specs=[ANY] * 8 + [VMEM],
        out_shape=[sds((256, EMB), BF)] * 8 + [sds((8, DOCS), F32)],
        scratch_shapes=[
            pltpu.VMEM((16 * DOCS, EMB), BF),
            pltpu.VMEM((16 * DOCS, EMB), BF),
            pltpu.VMEM((3, 8 * DOCS, 8 * DOCS), BF),
            pltpu.VMEM((8 * DOCS, 16 * DOCS), BF),
            pltpu.VMEM((16 * DOCS, 8 * DOCS), BF),
            pltpu.VMEM((8, 256, EMB), BF),
            pltpu.VMEM((32, DOCS), F32),
            pltpu.SemaphoreType.DMA((24,)),
            pltpu.SemaphoreType.DMA((8,)),
        ],
        compiler_params=params(),
    )(*k_near, *k_far, e_own, mix, mix_far, *row_in, *col_in)


def half_block(which):
    return pl.BlockSpec((DOCS, EMB), lambda i: (which, 0))


def pass_body(*refs):
    for ins, out in ((refs[0:4], refs[8]), (refs[4:8], refs[9])):
        out[...] = sum(ref[...].astype(F32) for ref in ins).astype(BF)


def pass_on(query_in, key_in):
    return pl.pallas_call(
        pass_body,
        grid=(1,),
        in_specs=[half_block(1)] * 8,
        out_specs=[half_block(0)] * 2,
        out_shape=[sds((DOCS, EMB), BF)] * 2,
        compiler_params=params(),
    )(*query_in, *key_in)


def keep_body(*refs):
    q_parts, k_parts = refs[0:4], refs[4:8]
    q_unit, paired, q_perm, pos, inv, q_out, k_out = refs[8:15]
    hot = one_hot(pos[...])
    same = eye()
    pair = paired[...].astype(F32)
    score = jnp.sum(q_unit[...].astype(F32) * pair, axis=1, keepdims=True) * TAU_INV
    expo = jnp.exp(score)
    inv_r = jnp.sum(same * inv[0:1, :], axis=1, keepdims=True)
    inv_c = jnp.sum(hot * inv[1:2, :], axis=1, keepdims=True)
    weight = expo * inv_r + expo * inv_c - 2.0
    weight_k = jnp.sum(same * jnp.sum(hot * weight, axis=0, keepdims=True), axis=1, keepdims=True)
    for parts, w, pair_rows, out in (
        (q_parts, weight, pair, q_out),
        (k_parts, weight_k, q_perm[...].astype(F32), k_out),
    ):
        out[...] = sum(ref[...].astype(F32) for ref in parts) + (w * TAU_INV) * pair_rows


def keep(query_in, key_in, q_unit, paired, q_perm, pos, inv):
    return pl.pallas_call(
        keep_body,
        grid=(1,),
        in_specs=[half_block(0)] * 11 + [VMEM] * 2,
        out_specs=[half_block(0)] * 2,
        out_shape=[sds((DOCS, EMB), F32)] * 2,
        compiler_params=params(),
    )(*query_in, *key_in, q_unit, paired, q_perm, pos, inv)


def back_body(q_keep, q_got, k_keep, k_got, q_raw, k_raw, out):
    for kept, got, raw, start in ((q_keep, q_got, q_raw, 0), (k_keep, k_got, k_raw, DOCS)):
        grad = kept[...] + got[...].astype(F32)
        exact, scale = unit_of(raw[...])
        inner = jnp.sum(exact * grad, axis=1, keepdims=True)
        out[start : start + DOCS, :] = (scale * (grad - exact * inner)).astype(BF)


def back(*args):
    return pl.pallas_call(
        back_body,
        in_specs=[VMEM] * 6,
        out_specs=VMEM,
        out_shape=sds((2 * DOCS, EMB), BF),
        compiler_params=params(),
    )(*args)


def contract_body(*refs):
    b_in, h_all, h_in, where, out = refs[0:4], refs[4], refs[5:8], refs[8], refs[9]
    h_s, b_s, o_s, sems, out_sems = refs[10:15]
    sources = (h_all.at[where[0]],) + tuple(h_in)
    loads = []
    for i in range(4):
        loads.append((b_in[i], b_s.at[pl.ds(i * 256, 256)]))
        loads.append((sources[i], h_s.at[:, pl.ds(i * 256, 256)]))
    loads = [pltpu.make_async_copy(s, d, sems.at[i]) for i, (s, d) in enumerate(loads)]
    for load in loads:
        load.start()
    for load in loads:
        load.wait()
    stores = []
    for m in range(4):
        rows = pl.ds(m * 256, 256)
        o_s[rows, :] = dot(h_s[rows, :], b_s[...]).astype(BF)
        stores.append(pltpu.make_async_copy(o_s.at[rows], out.at[rows], out_sems.at[m]))
        stores[-1].start()
    for store in stores:
        store.wait()


def contract(b_in, h_all, h_in, where):
    return pl.pallas_call(
        contract_body,
        in_specs=[ANY] * 8 + [SMEM],
        out_specs=ANY,
        out_shape=sds((1024, EMB), BF),
        scratch_shapes=[
            pltpu.VMEM((1024, 1024), BF),
            pltpu.VMEM((1024, EMB), BF),
            pltpu.VMEM((1024, EMB), BF),
            pltpu.SemaphoreType.DMA((8,)),
            pltpu.SemaphoreType.DMA((4,)),
        ],
        compiler_params=params(),
    )(*b_in, h_all, *h_in, where)


def flip_slots(value):
    return value[:, ::-1]


def to_owners(parts, move):
    return [parts[0]] + [move(parts[(4 - step) % 4], step, 0) for step in (1, 2, 3)]


def local(hid_query, hid_key, projection, tile_rows, tile_cols, tile_count, positive):
    row_index = lax.axis_index("row")
    col_index = lax.axis_index("col")
    core_index = lax.axis_index("dp")
    x, z_hi = row_index // 2, row_index % 2
    y, z_lo = col_index // 2, col_index % 2
    quarter = z_lo * 2 + core_index

    q_unit, k_unit, q_raw, k_raw = project(hid_query, hid_key, projection)
    k_flip = move_key(k_unit, 0, 1)
    q_flip = move_query(q_unit, 0, 1)

    pos = (positive - ((row_index * 8 + col_index) * 2 + core_index) * DOCS).reshape(DOCS, 1)
    paired, q_perm, pos_rows = pair_up(q_unit, k_unit, pos)
    turned = jnp.concatenate([hid_query, hid_key], axis=0).T.reshape(4, 2, 4, 2, 2, 32, 256)
    turned = turned.transpose(3, 4, 0, 1, 2, 5, 6).reshape(4, 1024, 256)
    h_flip = lax.dynamic_index_in_dim(turned, quarter ^ 2, 0, keepdims=False)
    h_both = lax.dynamic_index_in_dim(turned, quarter ^ 3, 0, keepdims=False)
    h_core = lax.dynamic_index_in_dim(turned, quarter ^ 1, 0, keepdims=False)
    entry_rows = tile_rows[0, 0]
    entry_cols = tile_cols[0, 0]
    used = jnp.arange(entry_rows.shape[0], dtype=jnp.int32) < tile_count[0, 0]
    slot_rows = ((y - entry_rows // 2) % 4) * 2 + (z_lo ^ (entry_rows % 2))
    slot_cols = ((x - entry_cols // 2) % 4) * 2 + (z_hi ^ (entry_cols % 2))
    eight = jnp.arange(8, dtype=jnp.int32)
    hit = (
        (slot_rows[:, None, None] == eight[None, :, None])
        & (slot_cols[:, None, None] == eight[None, None, :])
        & used[:, None, None]
    )
    mask = jnp.any(hit, axis=0).astype(F32)

    k_flip, q_flip, pos, paired, q_perm, pos_rows, turned, h_flip, h_both, h_core, mask = (
        lax.optimization_barrier(
            (k_flip, q_flip, pos, paired, q_perm, pos_rows, turned, h_flip, h_both, h_core, mask)
        )
    )
    k_pair = jnp.concatenate([k_unit, k_flip], axis=0)
    q_pair = jnp.concatenate([q_unit, q_flip], axis=0)
    k_pair, q_pair = lax.optimization_barrier((k_pair, q_pair))
    k1 = move_key(k_pair, 1, 0)
    q1 = move_query(q_pair, 1, 0)
    k3 = move_key(k_pair, 3, 0)
    q3 = move_query(q_pair, 3, 0)
    k_far = swap(k_pair)
    k1, q1, k3, q3, k_far = lax.optimization_barrier((k1, q1, k3, q3, k_far))
    k_own = [
        k_pair,
        k1,
        move_key(k1[:DOCS], 1, 0),
        move_key(k3[DOCS:], 3, 0),
        k3,
    ]
    q_own = [
        q_pair,
        q1,
        move_query(q1[:DOCS], 1, 0),
        move_query(q3[DOCS:], 3, 0),
        q3,
    ]
    k1_far = swap(k1)
    k1_far, k3_late = lax.optimization_barrier((k1_far, k3))
    k3_far = swap(k3_late)
    k_oth = [k_far, k1_far, swap(k_own[2]), swap(k_own[3]), k3_far]

    h_flip, *blocks = lax.optimization_barrier((h_flip, *q_own, *k_oth))
    q_own, k_oth = blocks[:5], blocks[5:]
    h_flip = move_query(h_flip, 0, 1)
    e_own, mix, sums = scores(q_own, k_own, k_oth, mask, pos_rows)
    sums, mix, h_flip = lax.optimization_barrier((sums, mix, h_flip))
    far = swap(sums)
    far, mix = lax.optimization_barrier((far, mix))
    mix_far = swap(mix)
    row_part = jnp.concatenate([sums[:8], far[:8]], axis=0).reshape(8, 2, DOCS)
    col_part = sums[8:] + jnp.concatenate([far[16:], far[8:16]], axis=0)
    col_part = col_part.reshape(8, 2, DOCS)
    row_part = row_part + flip_slots(move_query(row_part, 0, 1))
    col_part = col_part + flip_slots(move_key(col_part, 0, 1))
    row_part = row_part.reshape(16, DOCS)
    col_part = col_part.reshape(16, DOCS)
    row_got = [row_part] + [move_query(row_part, step, 0) for step in (1, 2, 3)]
    col_got = [col_part] + [move_key(col_part, step, 0) for step in (1, 2, 3)]

    h_both, h_core, *got = lax.optimization_barrier((h_both, h_core, *row_got, *col_got))
    h_both = move_query(h_both, 0, 1)
    parts = grads(k_own, k_oth, e_own, mix, mix_far, got[:4], got[4:])
    h_both, *parts = lax.optimization_barrier((h_both, *parts))
    inv = parts[8]
    query_in = to_owners(parts[:4], move_query)
    key_in = to_owners(parts[4:8], move_key)
    q_send, k_send = pass_on(query_in, key_in)
    q_got = move_query(q_send, 0, 1)
    k_got = move_key(k_send, 0, 1)
    q_keep, k_keep = keep(query_in, key_in, q_unit, paired, q_perm, pos, inv)
    b_own = back(q_keep, q_got, k_keep, k_got, q_raw, k_raw)
    b_flip = move_query(b_own, 0, 1)
    out = contract(
        [b_own, swap(b_own), b_flip, swap(b_flip)],
        turned,
        [swap(h_core), h_flip, swap(h_both)],
        quarter.reshape(1).astype(jnp.int32),
    )
    out = lax.all_to_all(out, ("row", "col"), 0, 0, tiled=True, axis_index_groups=PLANES)
    return jnp.sum(out.reshape(32, 32, EMB).astype(F32), axis=0)


def solution(mesh):
    return jax.shard_map(
        local,
        mesh=mesh,
        in_specs=(
            P(("row", "col", "dp"), None),
            P(("row", "col", "dp"), None),
            P(),
            P("row", "col", None),
            P("row", "col", None),
            P("row", "col"),
            P(("row", "col", "dp")),
        ),
        out_specs=P(("row", "col", "dp"), None),
        check_vma=False,
    )
```

```python
import jax
import jax.numpy as jnp
from jax import lax
from jax.experimental import pallas as pl
from jax.experimental.pallas import tpu as pltpu
from jax.sharding import PartitionSpec as P

TAU_INV = 20.0
EPS = 1e-06
LOG2E = 1.4426950408889634
DOCS = 128
EMB = 1024
HID = 4096
BF = jnp.bfloat16
F32 = jnp.float32
VM = 56 * 1024 * 1024


def ring_pair(step, flip):
    return [(i, ((i // 2 + step) % 4) * 2 + ((i % 2) ^ flip)) for i in range(8)]


def move_query(value, step, flip):
    return lax.ppermute(value, "col", ring_pair(step, flip))


def move_key(value, step, flip):
    return lax.ppermute(value, "row", ring_pair(step, flip))


def chip(x, y, z):
    return (x * 2 + z // 2) * 8 + y * 2 + z % 2


PLANES = [
    [chip(x, y, z_hi * 2 + z_lo) for x in range(4) for z_hi in range(2) for y in range(4)]
    for z_lo in range(2)
]


def swap(value):
    return lax.ppermute(value, "dp", [(0, 1), (1, 0)])


def params():
    return pltpu.CompilerParams(vmem_limit_bytes=VM)


def sds(shape, dtype):
    return jax.ShapeDtypeStruct(shape, dtype)


ANY = pl.BlockSpec(memory_space=pl.ANY)
SMEM = pl.BlockSpec(memory_space=pltpu.SMEM)
VMEM = pl.BlockSpec(memory_space=pltpu.VMEM)


def dot(a, b):
    return lax.dot_general(a, b, (((1,), (0,)), ((), ())), preferred_element_type=F32)


def dot_t(a, b):
    return lax.dot_general(a, b, (((1,), (1,)), ((), ())), preferred_element_type=F32)


def t_dot(a, b):
    return lax.dot_general(a, b, (((0,), (0,)), ((), ())), preferred_element_type=F32)


def unit_of(raw):
    values = raw.astype(F32)
    scale = lax.rsqrt(jnp.sum(values * values, axis=1, keepdims=True) + EPS)
    return values * scale, scale


def project_body(hq, hk, proj, q_unit, k_unit, q_raw, k_raw, hid, proj_s, acc, sems):
    depth = 512
    loads = [
        pltpu.make_async_copy(hq, hid.at[pl.ds(0, DOCS)], sems.at[0]),
        pltpu.make_async_copy(hk, hid.at[pl.ds(DOCS, DOCS)], sems.at[1]),
    ]
    for c in range(HID // depth):
        rows = pl.ds(c * depth, depth)
        loads.append(pltpu.make_async_copy(proj.at[rows], proj_s.at[rows], sems.at[2 + c]))
    for load in loads:
        load.start()
    loads[0].wait()
    loads[1].wait()
    for c in range(HID // depth):
        loads[2 + c].wait()
        chunk = slice(c * depth, (c + 1) * depth)
        part = dot(hid[:, chunk], proj_s[chunk, :])
        if c == 0:
            acc[...] = part
        else:
            acc[...] += part
    for raw_ref, unit_ref, start in ((k_raw, k_unit, DOCS), (q_raw, q_unit, 0)):
        raw = acc[start : start + DOCS, :].astype(BF)
        raw_ref[...] = raw
        unit_ref[...] = unit_of(raw)[0].astype(BF)


def project(hid_query, hid_key, projection):
    return pl.pallas_call(
        project_body,
        in_specs=[ANY] * 3,
        out_specs=[VMEM] * 4,
        out_shape=[sds((DOCS, EMB), BF)] * 4,
        scratch_shapes=[
            pltpu.VMEM((2 * DOCS, HID), BF),
            pltpu.VMEM((HID, EMB), BF),
            pltpu.VMEM((2 * DOCS, EMB), F32),
            pltpu.SemaphoreType.DMA((2 + HID // 512,)),
        ],
        compiler_params=params(),
    )(hid_query, hid_key, projection)


def one_hot(pos):
    lane = lax.broadcasted_iota(jnp.int32, (DOCS, DOCS), 1)
    return (lane == pos).astype(F32)


def eye():
    lane = lax.broadcasted_iota(jnp.int32, (DOCS, DOCS), 1)
    row = lax.broadcasted_iota(jnp.int32, (DOCS, DOCS), 0)
    return (lane == row).astype(F32)


def pairs_body(q_unit, k_unit, pos, paired, q_perm, pos_rows):
    hot = one_hot(pos[...])
    hot_bf = hot.astype(BF)
    pair = dot(hot_bf, k_unit[...])
    paired[...] = pair.astype(BF)
    q_perm[...] = t_dot(hot_bf, q_unit[...]).astype(BF)
    score = jnp.sum(q_unit[...].astype(F32) * pair, axis=1, keepdims=True) * TAU_INV
    expo = jnp.exp(score)
    pos_rows[0:1, :] = jnp.sum(eye() * expo, axis=0, keepdims=True)
    pos_rows[1:2, :] = jnp.sum(hot * expo, axis=0, keepdims=True)
    pos_rows[2:8, :] = jnp.zeros((6, DOCS), F32)


def pair_up(q_unit, k_unit, pos):
    return pl.pallas_call(
        pairs_body,
        in_specs=[VMEM] * 3,
        out_specs=[VMEM] * 3,
        out_shape=[sds((DOCS, EMB), BF), sds((DOCS, EMB), BF), sds((8, DOCS), F32)],
        compiler_params=params(),
    )(q_unit, k_unit, pos)


PARTS = ((0, 256), (256, 256), (512, 128), (640, 128), (768, 256))


def block_copies(ins, scratch, sems, first, row):
    copies = []
    for i, (start, rows) in enumerate(PARTS):
        target = scratch.at[pl.ds(row + start, rows)]
        copies.append(pltpu.make_async_copy(ins[i], target, sems.at[first + i]))
    return copies


def scores_body(*refs):
    q_in, k_near, k_far = refs[0:5], refs[5:10], refs[10:15]
    mask, pos_rows = refs[15:17]
    e_own, mix, sums = refs[17:20]
    q_s, k_s, e_s, acc, in_sems, out_sems = refs[20:26]
    q_loads = block_copies(q_in, q_s, in_sems, 0, 0)
    k_loads = block_copies(k_near, k_s, in_sems, 5, 0) + block_copies(k_far, k_s, in_sems, 10, 1024)
    for load in k_loads[:1] + q_loads + k_loads[1:]:
        load.start()
    waits = ((0,), (1,), (2, 3), (4,), (5,), (6,), (7, 8), (9,))

    def score_of(b, m):
        if m == 0:
            for i in waits[b]:
                k_loads[i].wait()
        if b == 0:
            for i in waits[m]:
                q_loads[i].wait()
        return dot_t(q_s[m * 256 : (m + 1) * 256, :], k_s[b * 256 : (b + 1) * 256, :])

    stores = []
    following = score_of(0, 0)
    for b in range(8):
        total = [None, None]
        for m in range(4):
            score = following
            if m < 3 or b < 7:
                following = score_of(b + (m + 1) // 4, (m + 1) % 4)
            for n in range(2):
                a = m * 2 + n
                rows = slice(a * DOCS, (a + 1) * DOCS)
                expo = jnp.exp2(score[n * DOCS : (n + 1) * DOCS, :] * (TAU_INV * LOG2E))
                both = None
                for half in range(2):
                    slot = (b % 4) * 2 + half
                    one = expo[:, half * DOCS : (half + 1) * DOCS] * mask[a, slot]
                    e_s[b, rows, half * DOCS : (half + 1) * DOCS] = one.astype(BF)
                    both = one if half == 0 else both + one
                    part = one.reshape(16, 8, DOCS).sum(axis=0)
                    total[half] = part if a == 0 else total[half] + part
                if b == 0:
                    acc[rows, :] = both
                else:
                    acc[rows, :] += both
        out = (e_own if b < 4 else mix).at[pl.ds(0, 1024), pl.ds((b % 4) * 256, 256)]
        stores.append(pltpu.make_async_copy(e_s.at[b], out, out_sems.at[b]))
        stores[-1].start()
        if b == 0:
            stores.append(pltpu.make_async_copy(q_s, mix.at[pl.ds(1024, 1024)], out_sems.at[8]))
            stores[-1].start()
        for half in range(2):
            col = jnp.sum(total[half], axis=0, keepdims=True)
            if b == 0 and half == 0:
                col = col + pos_rows[1:2, :]
            sums[8 + 2 * b + half : 9 + 2 * b + half, :] = col
    for a in range(8):
        part = jnp.sum(acc[a * DOCS : (a + 1) * DOCS, :].T, axis=0, keepdims=True)
        if a == 0:
            part = part + pos_rows[0:1, :]
        sums[a : a + 1, :] = part
    for store in stores:
        store.wait()


def scores(q_in, k_near, k_far, mask, pos_rows):
    return pl.pallas_call(
        scores_body,
        in_specs=[ANY] * 15 + [SMEM, VMEM],
        out_specs=[ANY, ANY, VMEM],
        out_shape=[
            sds((8 * DOCS, 8 * DOCS), BF),
            sds((16 * DOCS, 8 * DOCS), BF),
            sds((24, DOCS), F32),
        ],
        scratch_shapes=[
            pltpu.VMEM((8 * DOCS, EMB), BF),
            pltpu.VMEM((16 * DOCS, EMB), BF),
            pltpu.VMEM((8, 8 * DOCS, 256), BF),
            pltpu.VMEM((8 * DOCS, DOCS), F32),
            pltpu.SemaphoreType.DMA((15,)),
            pltpu.SemaphoreType.DMA((9,)),
        ],
        compiler_params=params(),
    )(*q_in, *k_near, *k_far, mask, pos_rows)


def grads_body(*refs):
    k_near, k_far = refs[0:5], refs[5:10]
    e_own, mix, mix_far, row_in, col_in = refs[10], refs[11], refs[12], refs[13:17], refs[17:21]
    q_out, k_out, inv_out = refs[21:25], refs[25:29], refs[29]
    q_s, k_s, e_s, wq, wk, out_s, inv, sems, out_sems = refs[30:39]
    e_loads = []
    for m in range(4):
        rows = pl.ds(m * 256, 256)
        for i, ref in enumerate((e_own, mix, mix_far)):
            one = (ref.at[rows], e_s.at[i, rows], sems.at[3 * m + i])
            e_loads.append(pltpu.make_async_copy(*one))
    k_loads = block_copies(k_near, k_s, sems, 12, 0) + block_copies(k_far, k_s, sems, 17, 1024)
    q_loads = []
    for i, ref in enumerate((mix, mix_far)):
        one = (ref.at[pl.ds(1024, 1024)], q_s.at[pl.ds(i * 1024, 1024)], sems.at[22 + i])
        q_loads.append(pltpu.make_async_copy(*one))
    for load in e_loads[:3] + k_loads:
        load.start()
    for at, ins in ((0, row_in), (16, col_in)):
        for rel in range(2):
            for slot in range(8):
                total = ins[0][rel * 8 + slot : rel * 8 + slot + 1, :]
                for step in (1, 2, 3):
                    src = rel * 8 + (slot - 2 * step) % 8
                    total = total + ins[step][src : src + 1, :]
                dst = at + rel * 8 + slot
                inv[dst : dst + 1, :] = 1.0 / total
    inv_out[0:1, :] = inv[0:1, :]
    inv_out[1:2, :] = inv[16:17, :]
    inv_out[2:8, :] = jnp.zeros((6, DOCS), F32)
    stores = []

    def put(i, ref, grad):
        out_s[i] = grad.astype(BF)
        stores.append(pltpu.make_async_copy(out_s.at[i], ref, out_sems.at[i]))
        stores[-1].start()

    for m in range(4):
        for load in e_loads[3 * m : 3 * m + 3]:
            load.wait()
        for a in (2 * m, 2 * m + 1):
            rows = slice(a * DOCS, (a + 1) * DOCS)
            far = slice((8 + a) * DOCS, (9 + a) * DOCS)
            col_own = jnp.broadcast_to(inv[a : a + 1, :], (DOCS, DOCS)).T
            col_oth = jnp.broadcast_to(inv[8 + a : 9 + a, :], (DOCS, DOCS)).T
            for b in range(8):
                near_key = inv[16 + b : 17 + b, :]
                far_key = inv[24 + b : 25 + b, :]
                keys = slice(b * DOCS, (b + 1) * DOCS)
                keys_far = slice((8 + b) * DOCS, (9 + b) * DOCS)
                w1 = (e_s[0, rows, keys].astype(F32) * (col_own + near_key)).astype(BF)
                w2 = (e_s[1, rows, keys].astype(F32) * (col_own + far_key)).astype(BF)
                w3 = (e_s[2, rows, keys].astype(F32) * (col_oth + near_key)).astype(BF)
                wq[rows, keys] = w1
                wq[rows, keys_far] = w2
                wk[rows, keys] = w1
                wk[far, keys] = w3
        if m == 0:
            for load in k_loads:
                load.wait()
            for load in e_loads[3:] + q_loads:
                load.start()
        put(m, q_out[m], dot(wq[m * 256 : (m + 1) * 256, :], k_s[...]) * TAU_INV)
    for load in q_loads:
        load.wait()
    for m in range(4):
        put(4 + m, k_out[m], t_dot(wk[:, m * 256 : (m + 1) * 256], q_s[...]) * TAU_INV)
    for store in stores:
        store.wait()


def grads(k_near, k_far, e_own, mix, mix_far, row_in, col_in):
    return pl.pallas_call(
        grads_body,
        in_specs=[ANY] * 13 + [VMEM] * 8,
        out_specs=[ANY] * 8 + [VMEM],
        out_shape=[sds((256, EMB), BF)] * 8 + [sds((8, DOCS), F32)],
        scratch_shapes=[
            pltpu.VMEM((16 * DOCS, EMB), BF),
            pltpu.VMEM((16 * DOCS, EMB), BF),
            pltpu.VMEM((3, 8 * DOCS, 8 * DOCS), BF),
            pltpu.VMEM((8 * DOCS, 16 * DOCS), BF),
            pltpu.VMEM((16 * DOCS, 8 * DOCS), BF),
            pltpu.VMEM((8, 256, EMB), BF),
            pltpu.VMEM((32, DOCS), F32),
            pltpu.SemaphoreType.DMA((24,)),
            pltpu.SemaphoreType.DMA((8,)),
        ],
        compiler_params=params(),
    )(*k_near, *k_far, e_own, mix, mix_far, *row_in, *col_in)


def half_block(which):
    return pl.BlockSpec((DOCS, EMB), lambda i: (which, 0))


def pass_body(*refs):
    for ins, out in ((refs[0:4], refs[8]), (refs[4:8], refs[9])):
        out[...] = sum(ref[...].astype(F32) for ref in ins).astype(BF)


def pass_on(query_in, key_in):
    return pl.pallas_call(
        pass_body,
        grid=(1,),
        in_specs=[half_block(1)] * 8,
        out_specs=[half_block(0)] * 2,
        out_shape=[sds((DOCS, EMB), BF)] * 2,
        compiler_params=params(),
    )(*query_in, *key_in)


def keep_body(*refs):
    q_parts, k_parts = refs[0:4], refs[4:8]
    q_unit, paired, q_perm, pos, inv, q_out, k_out = refs[8:15]
    hot = one_hot(pos[...])
    same = eye()
    pair = paired[...].astype(F32)
    score = jnp.sum(q_unit[...].astype(F32) * pair, axis=1, keepdims=True) * TAU_INV
    expo = jnp.exp(score)
    inv_r = jnp.sum(same * inv[0:1, :], axis=1, keepdims=True)
    inv_c = jnp.sum(hot * inv[1:2, :], axis=1, keepdims=True)
    weight = expo * inv_r + expo * inv_c - 2.0
    weight_k = jnp.sum(same * jnp.sum(hot * weight, axis=0, keepdims=True), axis=1, keepdims=True)
    for parts, w, pair_rows, out in (
        (q_parts, weight, pair, q_out),
        (k_parts, weight_k, q_perm[...].astype(F32), k_out),
    ):
        out[...] = sum(ref[...].astype(F32) for ref in parts) + (w * TAU_INV) * pair_rows


def keep(query_in, key_in, q_unit, paired, q_perm, pos, inv):
    return pl.pallas_call(
        keep_body,
        grid=(1,),
        in_specs=[half_block(0)] * 11 + [VMEM] * 2,
        out_specs=[half_block(0)] * 2,
        out_shape=[sds((DOCS, EMB), F32)] * 2,
        compiler_params=params(),
    )(*query_in, *key_in, q_unit, paired, q_perm, pos, inv)


def back_body(q_keep, q_got, k_keep, k_got, q_raw, k_raw, out):
    for kept, got, raw, start in ((q_keep, q_got, q_raw, 0), (k_keep, k_got, k_raw, DOCS)):
        grad = kept[...] + got[...].astype(F32)
        exact, scale = unit_of(raw[...])
        inner = jnp.sum(exact * grad, axis=1, keepdims=True)
        out[start : start + DOCS, :] = (scale * (grad - exact * inner)).astype(BF)


def back(*args):
    return pl.pallas_call(
        back_body,
        in_specs=[VMEM] * 6,
        out_specs=VMEM,
        out_shape=sds((2 * DOCS, EMB), BF),
        compiler_params=params(),
    )(*args)


def contract_body(*refs):
    b_in, h_all, h_in, where, out = refs[0:4], refs[4], refs[5:8], refs[8], refs[9]
    h_s, b_s, o_s, sems, out_sems = refs[10:15]
    sources = (h_all.at[where[0]],) + tuple(h_in)
    loads = []
    for i in range(4):
        loads.append((b_in[i], b_s.at[pl.ds(i * 256, 256)]))
        loads.append((sources[i], h_s.at[:, pl.ds(i * 256, 256)]))
    loads = [pltpu.make_async_copy(s, d, sems.at[i]) for i, (s, d) in enumerate(loads)]
    for load in loads:
        load.start()
    for load in loads:
        load.wait()
    stores = []
    for m in range(4):
        rows = pl.ds(m * 256, 256)
        o_s[rows, :] = dot(h_s[rows, :], b_s[...]).astype(BF)
        stores.append(pltpu.make_async_copy(o_s.at[rows], out.at[rows], out_sems.at[m]))
        stores[-1].start()
    for store in stores:
        store.wait()


def contract(b_in, h_all, h_in, where):
    return pl.pallas_call(
        contract_body,
        in_specs=[ANY] * 8 + [SMEM],
        out_specs=ANY,
        out_shape=sds((1024, EMB), BF),
        scratch_shapes=[
            pltpu.VMEM((1024, 1024), BF),
            pltpu.VMEM((1024, EMB), BF),
            pltpu.VMEM((1024, EMB), BF),
            pltpu.SemaphoreType.DMA((8,)),
            pltpu.SemaphoreType.DMA((4,)),
        ],
        compiler_params=params(),
    )(*b_in, h_all, *h_in, where)


def flip_slots(value):
    return value[:, ::-1]


def to_owners(parts, move):
    return [parts[0]] + [move(parts[(4 - step) % 4], step, 0) for step in (1, 2, 3)]


def local(hid_query, hid_key, projection, tile_rows, tile_cols, tile_count, positive):
    row_index = lax.axis_index("row")
    col_index = lax.axis_index("col")
    core_index = lax.axis_index("dp")
    x, z_hi = row_index // 2, row_index % 2
    y, z_lo = col_index // 2, col_index % 2
    quarter = z_lo * 2 + core_index

    q_unit, k_unit, q_raw, k_raw = project(hid_query, hid_key, projection)
    k_flip = move_key(k_unit, 0, 1)
    q_flip = move_query(q_unit, 0, 1)

    pos = (positive - ((row_index * 8 + col_index) * 2 + core_index) * DOCS).reshape(DOCS, 1)
    paired, q_perm, pos_rows = pair_up(q_unit, k_unit, pos)
    turned = jnp.concatenate([hid_query, hid_key], axis=0).T.reshape(4, 2, 4, 2, 2, 32, 256)
    turned = turned.transpose(3, 4, 0, 1, 2, 5, 6).reshape(4, 1024, 256)
    h_flip = lax.dynamic_index_in_dim(turned, quarter ^ 2, 0, keepdims=False)
    h_both = lax.dynamic_index_in_dim(turned, quarter ^ 3, 0, keepdims=False)
    h_core = lax.dynamic_index_in_dim(turned, quarter ^ 1, 0, keepdims=False)
    entry_rows = tile_rows[0, 0]
    entry_cols = tile_cols[0, 0]
    used = jnp.arange(entry_rows.shape[0], dtype=jnp.int32) < tile_count[0, 0]
    slot_rows = ((y - entry_rows // 2) % 4) * 2 + (z_lo ^ (entry_rows % 2))
    slot_cols = ((x - entry_cols // 2) % 4) * 2 + (z_hi ^ (entry_cols % 2))
    eight = jnp.arange(8, dtype=jnp.int32)
    hit = (
        (slot_rows[:, None, None] == eight[None, :, None])
        & (slot_cols[:, None, None] == eight[None, None, :])
        & used[:, None, None]
    )
    mask = jnp.any(hit, axis=0).astype(F32)

    k_flip, q_flip, pos, paired, q_perm, pos_rows, turned, h_flip, h_both, h_core, mask = (
        lax.optimization_barrier(
            (k_flip, q_flip, pos, paired, q_perm, pos_rows, turned, h_flip, h_both, h_core, mask)
        )
    )
    k_pair = jnp.concatenate([k_unit, k_flip], axis=0)
    q_pair = jnp.concatenate([q_unit, q_flip], axis=0)
    k_pair, q_pair = lax.optimization_barrier((k_pair, q_pair))
    k1 = move_key(k_pair, 1, 0)
    q1 = move_query(q_pair, 1, 0)
    k3 = move_key(k_pair, 3, 0)
    q3 = move_query(q_pair, 3, 0)
    k_far = swap(k_pair)
    k1, q1, k3, q3, k_far = lax.optimization_barrier((k1, q1, k3, q3, k_far))
    k_own = [
        k_pair,
        k1,
        move_key(k1[:DOCS], 1, 0),
        move_key(k3[DOCS:], 3, 0),
        k3,
    ]
    q_own = [
        q_pair,
        q1,
        move_query(q1[:DOCS], 1, 0),
        move_query(q3[DOCS:], 3, 0),
        q3,
    ]
    k1_far = swap(k1)
    k1_far, k3_late = lax.optimization_barrier((k1_far, k3))
    k3_far = swap(k3_late)
    k_oth = [k_far, k1_far, swap(k_own[2]), swap(k_own[3]), k3_far]

    h_flip, *blocks = lax.optimization_barrier((h_flip, *q_own, *k_oth))
    q_own, k_oth = blocks[:5], blocks[5:]
    h_flip = move_query(h_flip, 0, 1)
    e_own, mix, sums = scores(q_own, k_own, k_oth, mask, pos_rows)
    far = swap(sums)
    far, mix, h_flip = lax.optimization_barrier((far, mix, h_flip))
    mix_far = swap(mix)
    row_part = jnp.concatenate([sums[:8], far[:8]], axis=0).reshape(8, 2, DOCS)
    col_part = sums[8:] + jnp.concatenate([far[16:], far[8:16]], axis=0)
    col_part = col_part.reshape(8, 2, DOCS)
    row_part = row_part + flip_slots(move_query(row_part, 0, 1))
    col_part = col_part + flip_slots(move_key(col_part, 0, 1))
    row_part = row_part.reshape(16, DOCS)
    col_part = col_part.reshape(16, DOCS)
    row_got = [row_part] + [move_query(row_part, step, 0) for step in (1, 2, 3)]
    col_got = [col_part] + [move_key(col_part, step, 0) for step in (1, 2, 3)]

    h_both, h_core, *got = lax.optimization_barrier((h_both, h_core, *row_got, *col_got))
    h_both = move_query(h_both, 0, 1)
    parts = grads(k_own, k_oth, e_own, mix, mix_far, got[:4], got[4:])
    h_both, *parts = lax.optimization_barrier((h_both, *parts))
    inv = parts[8]
    query_in = to_owners(parts[:4], move_query)
    key_in = to_owners(parts[4:8], move_key)
    q_send, k_send = pass_on(query_in, key_in)
    q_got = move_query(q_send, 0, 1)
    k_got = move_key(k_send, 0, 1)
    q_keep, k_keep = keep(query_in, key_in, q_unit, paired, q_perm, pos, inv)
    b_own = back(q_keep, q_got, k_keep, k_got, q_raw, k_raw)
    b_flip = move_query(b_own, 0, 1)
    out = contract(
        [b_own, swap(b_own), b_flip, swap(b_flip)],
        turned,
        [swap(h_core), h_flip, swap(h_both)],
        quarter.reshape(1).astype(jnp.int32),
    )
    out = lax.all_to_all(out, ("row", "col"), 0, 0, tiled=True, axis_index_groups=PLANES)
    return jnp.sum(out.reshape(32, 32, EMB).astype(F32), axis=0)


def solution(mesh):
    return jax.shard_map(
        local,
        mesh=mesh,
        in_specs=(
            P(("row", "col", "dp"), None),
            P(("row", "col", "dp"), None),
            P(),
            P("row", "col", None),
            P("row", "col", None),
            P("row", "col"),
            P(("row", "col", "dp")),
        ),
        out_specs=P(("row", "col", "dp"), None),
        check_vma=False,
    )
```

```python
import jax
import jax.numpy as jnp
from jax import lax
from jax.experimental import pallas as pl
from jax.experimental.pallas import tpu as pltpu
from jax.sharding import PartitionSpec as P

TAU_INV = 20.0
EPS = 1e-06
LOG2E = 1.4426950408889634
DOCS = 128
EMB = 1024
HID = 4096
BF = jnp.bfloat16
F32 = jnp.float32
VM = 56 * 1024 * 1024


def ring_pair(step, flip):
    return [(i, ((i // 2 + step) % 4) * 2 + ((i % 2) ^ flip)) for i in range(8)]


def move_query(value, step, flip):
    return lax.ppermute(value, "col", ring_pair(step, flip))


def move_key(value, step, flip):
    return lax.ppermute(value, "row", ring_pair(step, flip))


def chip(x, y, z):
    return (x * 2 + z // 2) * 8 + y * 2 + z % 2


PLANES = [
    [chip(x, y, z_hi * 2 + z_lo) for x in range(4) for z_hi in range(2) for y in range(4)]
    for z_lo in range(2)
]


def swap(value):
    return lax.ppermute(value, "dp", [(0, 1), (1, 0)])


def params():
    return pltpu.CompilerParams(vmem_limit_bytes=VM)


def sds(shape, dtype):
    return jax.ShapeDtypeStruct(shape, dtype)


ANY = pl.BlockSpec(memory_space=pl.ANY)
SMEM = pl.BlockSpec(memory_space=pltpu.SMEM)
VMEM = pl.BlockSpec(memory_space=pltpu.VMEM)


def dot(a, b):
    return lax.dot_general(a, b, (((1,), (0,)), ((), ())), preferred_element_type=F32)


def dot_t(a, b):
    return lax.dot_general(a, b, (((1,), (1,)), ((), ())), preferred_element_type=F32)


def t_dot(a, b):
    return lax.dot_general(a, b, (((0,), (0,)), ((), ())), preferred_element_type=F32)


def unit_of(raw):
    values = raw.astype(F32)
    scale = lax.rsqrt(jnp.sum(values * values, axis=1, keepdims=True) + EPS)
    return values * scale, scale


def project_body(hq, hk, proj, q_unit, k_unit, q_raw, k_raw, hid, proj_s, acc, sems):
    depth = 512
    loads = [
        pltpu.make_async_copy(hq, hid.at[pl.ds(0, DOCS)], sems.at[0]),
        pltpu.make_async_copy(hk, hid.at[pl.ds(DOCS, DOCS)], sems.at[1]),
    ]
    for c in range(HID // depth):
        rows = pl.ds(c * depth, depth)
        loads.append(pltpu.make_async_copy(proj.at[rows], proj_s.at[rows], sems.at[2 + c]))
    for load in loads:
        load.start()
    loads[0].wait()
    loads[1].wait()
    for c in range(HID // depth):
        loads[2 + c].wait()
        chunk = slice(c * depth, (c + 1) * depth)
        part = dot(hid[:, chunk], proj_s[chunk, :])
        if c == 0:
            acc[...] = part
        else:
            acc[...] += part
    for raw_ref, unit_ref, start in ((k_raw, k_unit, DOCS), (q_raw, q_unit, 0)):
        raw = acc[start : start + DOCS, :].astype(BF)
        raw_ref[...] = raw
        unit_ref[...] = unit_of(raw)[0].astype(BF)


def project(hid_query, hid_key, projection):
    return pl.pallas_call(
        project_body,
        in_specs=[ANY] * 3,
        out_specs=[VMEM] * 4,
        out_shape=[sds((DOCS, EMB), BF)] * 4,
        scratch_shapes=[
            pltpu.VMEM((2 * DOCS, HID), BF),
            pltpu.VMEM((HID, EMB), BF),
            pltpu.VMEM((2 * DOCS, EMB), F32),
            pltpu.SemaphoreType.DMA((2 + HID // 512,)),
        ],
        compiler_params=params(),
    )(hid_query, hid_key, projection)


def one_hot(pos):
    lane = lax.broadcasted_iota(jnp.int32, (DOCS, DOCS), 1)
    return (lane == pos).astype(F32)


def eye():
    lane = lax.broadcasted_iota(jnp.int32, (DOCS, DOCS), 1)
    row = lax.broadcasted_iota(jnp.int32, (DOCS, DOCS), 0)
    return (lane == row).astype(F32)


def pairs_body(q_unit, k_unit, pos, paired, q_perm, pos_rows):
    hot = one_hot(pos[...])
    hot_bf = hot.astype(BF)
    pair = dot(hot_bf, k_unit[...])
    paired[...] = pair.astype(BF)
    q_perm[...] = t_dot(hot_bf, q_unit[...]).astype(BF)
    score = jnp.sum(q_unit[...].astype(F32) * pair, axis=1, keepdims=True) * TAU_INV
    expo = jnp.exp(score)
    pos_rows[0:1, :] = jnp.sum(eye() * expo, axis=0, keepdims=True)
    pos_rows[1:2, :] = jnp.sum(hot * expo, axis=0, keepdims=True)
    pos_rows[2:8, :] = jnp.zeros((6, DOCS), F32)


def pair_up(q_unit, k_unit, pos):
    return pl.pallas_call(
        pairs_body,
        in_specs=[VMEM] * 3,
        out_specs=[VMEM] * 3,
        out_shape=[sds((DOCS, EMB), BF), sds((DOCS, EMB), BF), sds((8, DOCS), F32)],
        compiler_params=params(),
    )(q_unit, k_unit, pos)


PARTS = ((0, 256), (256, 256), (512, 128), (640, 128), (768, 256))


def block_copies(ins, scratch, sems, first, row):
    copies = []
    for i, (start, rows) in enumerate(PARTS):
        target = scratch.at[pl.ds(row + start, rows)]
        copies.append(pltpu.make_async_copy(ins[i], target, sems.at[first + i]))
    return copies


def scores_body(*refs):
    q_in, k_near, k_far = refs[0:5], refs[5:10], refs[10:15]
    mask, pos_rows = refs[15:17]
    e_own, mix, sums = refs[17:20]
    q_s, k_s, e_s, acc, in_sems, out_sems = refs[20:26]
    q_loads = block_copies(q_in, q_s, in_sems, 0, 0)
    k_loads = block_copies(k_near, k_s, in_sems, 5, 0) + block_copies(k_far, k_s, in_sems, 10, 1024)
    for load in k_loads[:1] + q_loads + k_loads[1:]:
        load.start()
    waits = ((0,), (1,), (2, 3), (4,), (5,), (6,), (7, 8), (9,))

    def score_of(b, m):
        if m == 0:
            for i in waits[b]:
                k_loads[i].wait()
        if b == 0:
            for i in waits[m]:
                q_loads[i].wait()
        return dot_t(q_s[m * 256 : (m + 1) * 256, :], k_s[b * 256 : (b + 1) * 256, :])

    stores = []
    following = score_of(0, 0)
    for b in range(8):
        total = [None, None]
        for m in range(4):
            score = following
            if m < 3 or b < 7:
                following = score_of(b + (m + 1) // 4, (m + 1) % 4)
            for n in range(2):
                a = m * 2 + n
                rows = slice(a * DOCS, (a + 1) * DOCS)
                expo = jnp.exp2(score[n * DOCS : (n + 1) * DOCS, :] * (TAU_INV * LOG2E))
                both = None
                for half in range(2):
                    slot = (b % 4) * 2 + half
                    one = expo[:, half * DOCS : (half + 1) * DOCS] * mask[a, slot]
                    e_s[b, rows, half * DOCS : (half + 1) * DOCS] = one.astype(BF)
                    both = one if half == 0 else both + one
                    part = one.reshape(16, 8, DOCS).sum(axis=0)
                    total[half] = part if a == 0 else total[half] + part
                if b == 0:
                    acc[rows, :] = both
                else:
                    acc[rows, :] += both
        out = (e_own if b < 4 else mix).at[pl.ds(0, 1024), pl.ds((b % 4) * 256, 256)]
        stores.append(pltpu.make_async_copy(e_s.at[b], out, out_sems.at[b]))
        stores[-1].start()
        if b == 0:
            stores.append(pltpu.make_async_copy(q_s, mix.at[pl.ds(1024, 1024)], out_sems.at[8]))
            stores[-1].start()
        for half in range(2):
            col = jnp.sum(total[half], axis=0, keepdims=True)
            if b == 0 and half == 0:
                col = col + pos_rows[1:2, :]
            sums[8 + 2 * b + half : 9 + 2 * b + half, :] = col
    for a in range(8):
        part = jnp.sum(acc[a * DOCS : (a + 1) * DOCS, :].T, axis=0, keepdims=True)
        if a == 0:
            part = part + pos_rows[0:1, :]
        sums[a : a + 1, :] = part
    for store in stores:
        store.wait()


def scores(q_in, k_near, k_far, mask, pos_rows):
    return pl.pallas_call(
        scores_body,
        in_specs=[ANY] * 15 + [SMEM, VMEM],
        out_specs=[ANY, ANY, VMEM],
        out_shape=[
            sds((8 * DOCS, 8 * DOCS), BF),
            sds((16 * DOCS, 8 * DOCS), BF),
            sds((24, DOCS), F32),
        ],
        scratch_shapes=[
            pltpu.VMEM((8 * DOCS, EMB), BF),
            pltpu.VMEM((16 * DOCS, EMB), BF),
            pltpu.VMEM((8, 8 * DOCS, 256), BF),
            pltpu.VMEM((8 * DOCS, DOCS), F32),
            pltpu.SemaphoreType.DMA((15,)),
            pltpu.SemaphoreType.DMA((9,)),
        ],
        compiler_params=params(),
    )(*q_in, *k_near, *k_far, mask, pos_rows)


def grads_body(*refs):
    k_near, k_far = refs[0:5], refs[5:10]
    e_own, mix, mix_far, row_in, col_in = refs[10], refs[11], refs[12], refs[13:17], refs[17:21]
    q_out, k_out, inv_out = refs[21:25], refs[25:29], refs[29]
    q_s, k_s, e_s, wq, wk, out_s, inv, sems, out_sems = refs[30:39]
    e_loads = []
    for m in range(4):
        rows = pl.ds(m * 256, 256)
        for i, ref in enumerate((e_own, mix, mix_far)):
            one = (ref.at[rows], e_s.at[i, rows], sems.at[3 * m + i])
            e_loads.append(pltpu.make_async_copy(*one))
    k_loads = block_copies(k_near, k_s, sems, 12, 0) + block_copies(k_far, k_s, sems, 17, 1024)
    q_loads = []
    for i, ref in enumerate((mix, mix_far)):
        one = (ref.at[pl.ds(1024, 1024)], q_s.at[pl.ds(i * 1024, 1024)], sems.at[22 + i])
        q_loads.append(pltpu.make_async_copy(*one))
    for load in e_loads[:3] + k_loads:
        load.start()
    for at, ins in ((0, row_in), (16, col_in)):
        for rel in range(2):
            for slot in range(8):
                total = ins[0][rel * 8 + slot : rel * 8 + slot + 1, :]
                for step in (1, 2, 3):
                    src = rel * 8 + (slot - 2 * step) % 8
                    total = total + ins[step][src : src + 1, :]
                dst = at + rel * 8 + slot
                inv[dst : dst + 1, :] = 1.0 / total
    inv_out[0:1, :] = inv[0:1, :]
    inv_out[1:2, :] = inv[16:17, :]
    inv_out[2:8, :] = jnp.zeros((6, DOCS), F32)
    stores = []

    def put(i, ref, grad):
        out_s[i] = grad.astype(BF)
        stores.append(pltpu.make_async_copy(out_s.at[i], ref, out_sems.at[i]))
        stores[-1].start()

    for m in range(4):
        for load in e_loads[3 * m : 3 * m + 3]:
            load.wait()
        for a in (2 * m, 2 * m + 1):
            rows = slice(a * DOCS, (a + 1) * DOCS)
            far = slice((8 + a) * DOCS, (9 + a) * DOCS)
            col_own = jnp.broadcast_to(inv[a : a + 1, :], (DOCS, DOCS)).T
            col_oth = jnp.broadcast_to(inv[8 + a : 9 + a, :], (DOCS, DOCS)).T
            for b in range(8):
                near_key = inv[16 + b : 17 + b, :]
                far_key = inv[24 + b : 25 + b, :]
                keys = slice(b * DOCS, (b + 1) * DOCS)
                keys_far = slice((8 + b) * DOCS, (9 + b) * DOCS)
                w1 = (e_s[0, rows, keys].astype(F32) * (col_own + near_key)).astype(BF)
                w2 = (e_s[1, rows, keys].astype(F32) * (col_own + far_key)).astype(BF)
                w3 = (e_s[2, rows, keys].astype(F32) * (col_oth + near_key)).astype(BF)
                wq[rows, keys] = w1
                wq[rows, keys_far] = w2
                wk[rows, keys] = w1
                wk[far, keys] = w3
        if m == 0:
            for load in k_loads:
                load.wait()
            for load in e_loads[3:] + q_loads:
                load.start()
        put(m, q_out[m], dot(wq[m * 256 : (m + 1) * 256, :], k_s[...]) * TAU_INV)
    for load in q_loads:
        load.wait()
    for m in range(4):
        put(4 + m, k_out[m], t_dot(wk[:, m * 256 : (m + 1) * 256], q_s[...]) * TAU_INV)
    for store in stores:
        store.wait()


def grads(k_near, k_far, e_own, mix, mix_far, row_in, col_in):
    return pl.pallas_call(
        grads_body,
        in_specs=[ANY] * 13 + [VMEM] * 8,
        out_specs=[ANY] * 8 + [VMEM],
        out_shape=[sds((256, EMB), BF)] * 8 + [sds((8, DOCS), F32)],
        scratch_shapes=[
            pltpu.VMEM((16 * DOCS, EMB), BF),
            pltpu.VMEM((16 * DOCS, EMB), BF),
            pltpu.VMEM((3, 8 * DOCS, 8 * DOCS), BF),
            pltpu.VMEM((8 * DOCS, 16 * DOCS), BF),
            pltpu.VMEM((16 * DOCS, 8 * DOCS), BF),
            pltpu.VMEM((8, 256, EMB), BF),
            pltpu.VMEM((32, DOCS), F32),
            pltpu.SemaphoreType.DMA((24,)),
            pltpu.SemaphoreType.DMA((8,)),
        ],
        compiler_params=params(),
    )(*k_near, *k_far, e_own, mix, mix_far, *row_in, *col_in)


def half_block(which):
    return pl.BlockSpec((DOCS, EMB), lambda i: (which, 0))


def pass_body(*refs):
    for ins, out in ((refs[0:4], refs[8]), (refs[4:8], refs[9])):
        out[...] = sum(ref[...].astype(F32) for ref in ins).astype(BF)


def pass_on(query_in, key_in):
    return pl.pallas_call(
        pass_body,
        grid=(1,),
        in_specs=[half_block(1)] * 8,
        out_specs=[half_block(0)] * 2,
        out_shape=[sds((DOCS, EMB), BF)] * 2,
        compiler_params=params(),
    )(*query_in, *key_in)


def keep_body(*refs):
    q_parts, k_parts = refs[0:4], refs[4:8]
    q_unit, paired, q_perm, pos, inv, q_out, k_out = refs[8:15]
    hot = one_hot(pos[...])
    same = eye()
    pair = paired[...].astype(F32)
    score = jnp.sum(q_unit[...].astype(F32) * pair, axis=1, keepdims=True) * TAU_INV
    expo = jnp.exp(score)
    inv_r = jnp.sum(same * inv[0:1, :], axis=1, keepdims=True)
    inv_c = jnp.sum(hot * inv[1:2, :], axis=1, keepdims=True)
    weight = expo * inv_r + expo * inv_c - 2.0
    weight_k = jnp.sum(same * jnp.sum(hot * weight, axis=0, keepdims=True), axis=1, keepdims=True)
    for parts, w, pair_rows, out in (
        (q_parts, weight, pair, q_out),
        (k_parts, weight_k, q_perm[...].astype(F32), k_out),
    ):
        out[...] = sum(ref[...].astype(F32) for ref in parts) + (w * TAU_INV) * pair_rows


def keep(query_in, key_in, q_unit, paired, q_perm, pos, inv):
    return pl.pallas_call(
        keep_body,
        grid=(1,),
        in_specs=[half_block(0)] * 11 + [VMEM] * 2,
        out_specs=[half_block(0)] * 2,
        out_shape=[sds((DOCS, EMB), F32)] * 2,
        compiler_params=params(),
    )(*query_in, *key_in, q_unit, paired, q_perm, pos, inv)


def back_body(q_keep, q_got, k_keep, k_got, q_raw, k_raw, out):
    for kept, got, raw, start in ((q_keep, q_got, q_raw, 0), (k_keep, k_got, k_raw, DOCS)):
        grad = kept[...] + got[...].astype(F32)
        exact, scale = unit_of(raw[...])
        inner = jnp.sum(exact * grad, axis=1, keepdims=True)
        out[start : start + DOCS, :] = (scale * (grad - exact * inner)).astype(BF)


def back(*args):
    return pl.pallas_call(
        back_body,
        in_specs=[VMEM] * 6,
        out_specs=VMEM,
        out_shape=sds((2 * DOCS, EMB), BF),
        compiler_params=params(),
    )(*args)


def contract_body(*refs):
    b_in, h_all, h_in, where, out = refs[0:4], refs[4], refs[5:8], refs[8], refs[9]
    h_s, b_s, o_s, sems, out_sems = refs[10:15]
    b_loads = [
        pltpu.make_async_copy(b_in[i], b_s.at[pl.ds(i * 256, 256)], sems.at[i]) for i in range(4)
    ]
    h_loads = []
    for m in range(4):
        rows = pl.ds(m * 256, 256)
        sources = [h_all.at[where[0], rows]] + [ref.at[rows] for ref in h_in]
        for i in range(4):
            target = h_s.at[rows, pl.ds(i * 256, 256)]
            h_loads.append(pltpu.make_async_copy(sources[i], target, sems.at[4 + m * 4 + i]))
    for load in h_loads[:4] + b_loads + h_loads[4:]:
        load.start()
    for load in b_loads:
        load.wait()
    stores = []
    for m in range(4):
        rows = pl.ds(m * 256, 256)
        for load in h_loads[m * 4 : m * 4 + 4]:
            load.wait()
        o_s[rows, :] = dot(h_s[rows, :], b_s[...]).astype(BF)
        stores.append(pltpu.make_async_copy(o_s.at[rows], out.at[rows], out_sems.at[m]))
        stores[-1].start()
    for store in stores:
        store.wait()


def contract(b_in, h_all, h_in, where):
    return pl.pallas_call(
        contract_body,
        in_specs=[ANY] * 8 + [SMEM],
        out_specs=ANY,
        out_shape=sds((1024, EMB), BF),
        scratch_shapes=[
            pltpu.VMEM((1024, 1024), BF),
            pltpu.VMEM((1024, EMB), BF),
            pltpu.VMEM((1024, EMB), BF),
            pltpu.SemaphoreType.DMA((20,)),
            pltpu.SemaphoreType.DMA((4,)),
        ],
        compiler_params=params(),
    )(*b_in, h_all, *h_in, where)


def flip_slots(value):
    return value[:, ::-1]


def to_owners(parts, move):
    return [parts[0]] + [move(parts[(4 - step) % 4], step, 0) for step in (1, 2, 3)]


def local(hid_query, hid_key, projection, tile_rows, tile_cols, tile_count, positive):
    row_index = lax.axis_index("row")
    col_index = lax.axis_index("col")
    core_index = lax.axis_index("dp")
    x, z_hi = row_index // 2, row_index % 2
    y, z_lo = col_index // 2, col_index % 2
    quarter = z_lo * 2 + core_index

    q_unit, k_unit, q_raw, k_raw = project(hid_query, hid_key, projection)
    k_flip = move_key(k_unit, 0, 1)
    q_flip = move_query(q_unit, 0, 1)

    pos = (positive - ((row_index * 8 + col_index) * 2 + core_index) * DOCS).reshape(DOCS, 1)
    paired, q_perm, pos_rows = pair_up(q_unit, k_unit, pos)
    turned = jnp.concatenate([hid_query, hid_key], axis=0).T.reshape(4, 2, 4, 2, 2, 32, 256)
    turned = turned.transpose(3, 4, 0, 1, 2, 5, 6).reshape(4, 1024, 256)
    h_flip = lax.dynamic_index_in_dim(turned, quarter ^ 2, 0, keepdims=False)
    h_both = lax.dynamic_index_in_dim(turned, quarter ^ 3, 0, keepdims=False)
    h_core = lax.dynamic_index_in_dim(turned, quarter ^ 1, 0, keepdims=False)
    entry_rows = tile_rows[0, 0]
    entry_cols = tile_cols[0, 0]
    used = jnp.arange(entry_rows.shape[0], dtype=jnp.int32) < tile_count[0, 0]
    slot_rows = ((y - entry_rows // 2) % 4) * 2 + (z_lo ^ (entry_rows % 2))
    slot_cols = ((x - entry_cols // 2) % 4) * 2 + (z_hi ^ (entry_cols % 2))
    eight = jnp.arange(8, dtype=jnp.int32)
    hit = (
        (slot_rows[:, None, None] == eight[None, :, None])
        & (slot_cols[:, None, None] == eight[None, None, :])
        & used[:, None, None]
    )
    mask = jnp.any(hit, axis=0).astype(F32)

    k_flip, q_flip, pos, paired, q_perm, pos_rows, turned, h_flip, h_both, h_core, mask = (
        lax.optimization_barrier(
            (k_flip, q_flip, pos, paired, q_perm, pos_rows, turned, h_flip, h_both, h_core, mask)
        )
    )
    k_pair = jnp.concatenate([k_unit, k_flip], axis=0)
    q_pair = jnp.concatenate([q_unit, q_flip], axis=0)
    k_pair, q_pair = lax.optimization_barrier((k_pair, q_pair))
    k1 = move_key(k_pair, 1, 0)
    q1 = move_query(q_pair, 1, 0)
    k3 = move_key(k_pair, 3, 0)
    q3 = move_query(q_pair, 3, 0)
    k_far = swap(k_pair)
    k1, q1, k3, q3, k_far = lax.optimization_barrier((k1, q1, k3, q3, k_far))
    k_own = [
        k_pair,
        k1,
        move_key(k1[:DOCS], 1, 0),
        move_key(k3[DOCS:], 3, 0),
        k3,
    ]
    q_own = [
        q_pair,
        q1,
        move_query(q1[:DOCS], 1, 0),
        move_query(q3[DOCS:], 3, 0),
        q3,
    ]
    k1_far = swap(k1)
    k1_far, k3_late = lax.optimization_barrier((k1_far, k3))
    k3_far = swap(k3_late)
    k_oth = [k_far, k1_far, swap(k_own[2]), swap(k_own[3]), k3_far]

    h_flip, *blocks = lax.optimization_barrier((h_flip, *q_own, *k_oth))
    q_own, k_oth = blocks[:5], blocks[5:]
    h_flip = move_query(h_flip, 0, 1)
    e_own, mix, sums = scores(q_own, k_own, k_oth, mask, pos_rows)
    far = swap(sums)
    far, mix, h_flip = lax.optimization_barrier((far, mix, h_flip))
    mix_far = swap(mix)
    row_part = jnp.concatenate([sums[:8], far[:8]], axis=0).reshape(8, 2, DOCS)
    col_part = sums[8:] + jnp.concatenate([far[16:], far[8:16]], axis=0)
    col_part = col_part.reshape(8, 2, DOCS)
    row_part = row_part + flip_slots(move_query(row_part, 0, 1))
    col_part = col_part + flip_slots(move_key(col_part, 0, 1))
    row_part = row_part.reshape(16, DOCS)
    col_part = col_part.reshape(16, DOCS)
    row_got = [row_part] + [move_query(row_part, step, 0) for step in (1, 2, 3)]
    col_got = [col_part] + [move_key(col_part, step, 0) for step in (1, 2, 3)]

    h_both, h_core, *got = lax.optimization_barrier((h_both, h_core, *row_got, *col_got))
    h_both = move_query(h_both, 0, 1)
    parts = grads(k_own, k_oth, e_own, mix, mix_far, got[:4], got[4:])
    inv = parts[8]
    query_in = to_owners(parts[:4], move_query)
    key_in = to_owners(parts[4:8], move_key)
    h_both, *query_in = lax.optimization_barrier((h_both, *query_in))
    q_send, k_send = pass_on(query_in, key_in)
    q_got = move_query(q_send, 0, 1)
    k_got = move_key(k_send, 0, 1)
    q_keep, k_keep = keep(query_in, key_in, q_unit, paired, q_perm, pos, inv)
    b_own = back(q_keep, q_got, k_keep, k_got, q_raw, k_raw)
    b_flip = move_query(b_own, 0, 1)
    out = contract(
        [b_own, swap(b_own), b_flip, swap(b_flip)],
        turned,
        [swap(h_core), h_flip, swap(h_both)],
        quarter.reshape(1).astype(jnp.int32),
    )
    out = lax.all_to_all(out, ("row", "col"), 0, 0, tiled=True, axis_index_groups=PLANES)
    return jnp.sum(out.reshape(32, 32, EMB).astype(F32), axis=0)


def solution(mesh):
    return jax.shard_map(
        local,
        mesh=mesh,
        in_specs=(
            P(("row", "col", "dp"), None),
            P(("row", "col", "dp"), None),
            P(),
            P("row", "col", None),
            P("row", "col", None),
            P("row", "col"),
            P(("row", "col", "dp")),
        ),
        out_specs=P(("row", "col", "dp"), None),
        check_vma=False,
    )
```

```python
import jax
import jax.numpy as jnp
from jax import lax
from jax.experimental import pallas as pl
from jax.experimental.pallas import tpu as pltpu
from jax.sharding import PartitionSpec as P

TAU_INV = 20.0
EPS = 1e-06
LOG2E = 1.4426950408889634
DOCS = 128
EMB = 1024
HID = 4096
BF = jnp.bfloat16
F32 = jnp.float32
VM = 56 * 1024 * 1024


def ring_pair(step, flip):
    return [(i, ((i // 2 + step) % 4) * 2 + ((i % 2) ^ flip)) for i in range(8)]


def move_query(value, step, flip):
    return lax.ppermute(value, "col", ring_pair(step, flip))


def move_key(value, step, flip):
    return lax.ppermute(value, "row", ring_pair(step, flip))


def chip(x, y, z):
    return (x * 2 + z // 2) * 8 + y * 2 + z % 2


PLANES = [
    [chip(x, y, z_hi * 2 + z_lo) for x in range(4) for z_hi in range(2) for y in range(4)]
    for z_lo in range(2)
]


def swap(value):
    return lax.ppermute(value, "dp", [(0, 1), (1, 0)])


def params():
    return pltpu.CompilerParams(vmem_limit_bytes=VM)


def sds(shape, dtype):
    return jax.ShapeDtypeStruct(shape, dtype)


ANY = pl.BlockSpec(memory_space=pl.ANY)
SMEM = pl.BlockSpec(memory_space=pltpu.SMEM)
VMEM = pl.BlockSpec(memory_space=pltpu.VMEM)


def dot(a, b):
    return lax.dot_general(a, b, (((1,), (0,)), ((), ())), preferred_element_type=F32)


def dot_t(a, b):
    return lax.dot_general(a, b, (((1,), (1,)), ((), ())), preferred_element_type=F32)


def t_dot(a, b):
    return lax.dot_general(a, b, (((0,), (0,)), ((), ())), preferred_element_type=F32)


def unit_of(raw):
    values = raw.astype(F32)
    scale = lax.rsqrt(jnp.sum(values * values, axis=1, keepdims=True) + EPS)
    return values * scale, scale


def project_body(hq, hk, proj, q_unit, k_unit, q_raw, k_raw, hid, proj_s, acc, sems):
    depth = 512
    loads = [
        pltpu.make_async_copy(hq, hid.at[pl.ds(0, DOCS)], sems.at[0]),
        pltpu.make_async_copy(hk, hid.at[pl.ds(DOCS, DOCS)], sems.at[1]),
    ]
    for c in range(HID // depth):
        rows = pl.ds(c * depth, depth)
        loads.append(pltpu.make_async_copy(proj.at[rows], proj_s.at[rows], sems.at[2 + c]))
    for load in loads:
        load.start()
    loads[0].wait()
    loads[1].wait()
    for c in range(HID // depth):
        loads[2 + c].wait()
        chunk = slice(c * depth, (c + 1) * depth)
        part = dot(hid[:, chunk], proj_s[chunk, :])
        if c == 0:
            acc[...] = part
        else:
            acc[...] += part
    for raw_ref, unit_ref, start in ((k_raw, k_unit, DOCS), (q_raw, q_unit, 0)):
        raw = acc[start : start + DOCS, :].astype(BF)
        raw_ref[...] = raw
        unit_ref[...] = unit_of(raw)[0].astype(BF)


def project(hid_query, hid_key, projection):
    return pl.pallas_call(
        project_body,
        in_specs=[ANY] * 3,
        out_specs=[VMEM] * 4,
        out_shape=[sds((DOCS, EMB), BF)] * 4,
        scratch_shapes=[
            pltpu.VMEM((2 * DOCS, HID), BF),
            pltpu.VMEM((HID, EMB), BF),
            pltpu.VMEM((2 * DOCS, EMB), F32),
            pltpu.SemaphoreType.DMA((2 + HID // 512,)),
        ],
        compiler_params=params(),
    )(hid_query, hid_key, projection)


def one_hot(pos):
    lane = lax.broadcasted_iota(jnp.int32, (DOCS, DOCS), 1)
    return (lane == pos).astype(F32)


def eye():
    lane = lax.broadcasted_iota(jnp.int32, (DOCS, DOCS), 1)
    row = lax.broadcasted_iota(jnp.int32, (DOCS, DOCS), 0)
    return (lane == row).astype(F32)


def pairs_body(q_unit, k_unit, pos, paired, q_perm, pos_rows):
    hot = one_hot(pos[...])
    hot_bf = hot.astype(BF)
    pair = dot(hot_bf, k_unit[...])
    paired[...] = pair.astype(BF)
    q_perm[...] = t_dot(hot_bf, q_unit[...]).astype(BF)
    score = jnp.sum(q_unit[...].astype(F32) * pair, axis=1, keepdims=True) * TAU_INV
    expo = jnp.exp(score)
    pos_rows[0:1, :] = jnp.sum(eye() * expo, axis=0, keepdims=True)
    pos_rows[1:2, :] = jnp.sum(hot * expo, axis=0, keepdims=True)
    pos_rows[2:8, :] = jnp.zeros((6, DOCS), F32)


def pair_up(q_unit, k_unit, pos):
    return pl.pallas_call(
        pairs_body,
        in_specs=[VMEM] * 3,
        out_specs=[VMEM] * 3,
        out_shape=[sds((DOCS, EMB), BF), sds((DOCS, EMB), BF), sds((8, DOCS), F32)],
        compiler_params=params(),
    )(q_unit, k_unit, pos)


PARTS = ((0, 256), (256, 256), (512, 128), (640, 128), (768, 256))


def block_copies(ins, scratch, sems, first, row):
    copies = []
    for i, (start, rows) in enumerate(PARTS):
        target = scratch.at[pl.ds(row + start, rows)]
        copies.append(pltpu.make_async_copy(ins[i], target, sems.at[first + i]))
    return copies


def scores_body(*refs):
    q_in, k_near, k_far = refs[0:5], refs[5:10], refs[10:15]
    mask, pos_rows = refs[15:17]
    e_own, mix, sums = refs[17:20]
    q_s, k_s, e_s, acc, in_sems, out_sems = refs[20:26]
    q_loads = block_copies(q_in, q_s, in_sems, 0, 0)
    k_loads = block_copies(k_near, k_s, in_sems, 5, 0) + block_copies(k_far, k_s, in_sems, 10, 1024)
    for load in k_loads[:1] + q_loads + k_loads[1:]:
        load.start()
    waits = ((0,), (1,), (2, 3), (4,), (5,), (6,), (7, 8), (9,))

    def score_of(b, m):
        if m == 0:
            for i in waits[b]:
                k_loads[i].wait()
        if b == 0:
            for i in waits[m]:
                q_loads[i].wait()
        return dot_t(q_s[m * 256 : (m + 1) * 256, :], k_s[b * 256 : (b + 1) * 256, :])

    stores = []
    following = score_of(0, 0)
    for b in range(8):
        total = [None, None]
        for m in range(4):
            score = following
            if m < 3 or b < 7:
                following = score_of(b + (m + 1) // 4, (m + 1) % 4)
            for n in range(2):
                a = m * 2 + n
                rows = slice(a * DOCS, (a + 1) * DOCS)
                expo = jnp.exp2(score[n * DOCS : (n + 1) * DOCS, :] * (TAU_INV * LOG2E))
                both = None
                for half in range(2):
                    slot = (b % 4) * 2 + half
                    one = expo[:, half * DOCS : (half + 1) * DOCS] * mask[a, slot]
                    e_s[b, rows, half * DOCS : (half + 1) * DOCS] = one.astype(BF)
                    both = one if half == 0 else both + one
                    part = one.reshape(16, 8, DOCS).sum(axis=0)
                    total[half] = part if a == 0 else total[half] + part
                if b == 0:
                    acc[rows, :] = both
                else:
                    acc[rows, :] += both
        out = (e_own if b < 4 else mix).at[pl.ds(0, 1024), pl.ds((b % 4) * 256, 256)]
        stores.append(pltpu.make_async_copy(e_s.at[b], out, out_sems.at[b]))
        stores[-1].start()
        if b == 0:
            stores.append(pltpu.make_async_copy(q_s, mix.at[pl.ds(1024, 1024)], out_sems.at[8]))
            stores[-1].start()
        for half in range(2):
            col = jnp.sum(total[half], axis=0, keepdims=True)
            if b == 0 and half == 0:
                col = col + pos_rows[1:2, :]
            sums[8 + 2 * b + half : 9 + 2 * b + half, :] = col
    for a in range(8):
        part = jnp.sum(acc[a * DOCS : (a + 1) * DOCS, :].T, axis=0, keepdims=True)
        if a == 0:
            part = part + pos_rows[0:1, :]
        sums[a : a + 1, :] = part
    for store in stores:
        store.wait()


def scores(q_in, k_near, k_far, mask, pos_rows):
    return pl.pallas_call(
        scores_body,
        in_specs=[ANY] * 15 + [SMEM, VMEM],
        out_specs=[ANY, ANY, VMEM],
        out_shape=[
            sds((8 * DOCS, 8 * DOCS), BF),
            sds((16 * DOCS, 8 * DOCS), BF),
            sds((24, DOCS), F32),
        ],
        scratch_shapes=[
            pltpu.VMEM((8 * DOCS, EMB), BF),
            pltpu.VMEM((16 * DOCS, EMB), BF),
            pltpu.VMEM((8, 8 * DOCS, 256), BF),
            pltpu.VMEM((8 * DOCS, DOCS), F32),
            pltpu.SemaphoreType.DMA((15,)),
            pltpu.SemaphoreType.DMA((9,)),
        ],
        compiler_params=params(),
    )(*q_in, *k_near, *k_far, mask, pos_rows)


def grads_body(*refs):
    k_near, k_far = refs[0:5], refs[5:10]
    e_own, mix, mix_far, row_in, col_in = refs[10], refs[11], refs[12], refs[13:17], refs[17:21]
    q_out, k_out, inv_out = refs[21:25], refs[25:29], refs[29]
    q_s, k_s, e_s, wq, wk, out_s, inv, sems, out_sems = refs[30:39]
    e_loads = []
    for m in range(4):
        rows = pl.ds(m * 256, 256)
        for i, ref in enumerate((e_own, mix, mix_far)):
            one = (ref.at[rows], e_s.at[i, rows], sems.at[3 * m + i])
            e_loads.append(pltpu.make_async_copy(*one))
    k_loads = block_copies(k_near, k_s, sems, 12, 0) + block_copies(k_far, k_s, sems, 17, 1024)
    q_loads = []
    for i, ref in enumerate((mix, mix_far)):
        one = (ref.at[pl.ds(1024, 1024)], q_s.at[pl.ds(i * 1024, 1024)], sems.at[22 + i])
        q_loads.append(pltpu.make_async_copy(*one))
    for load in e_loads[:3] + k_loads:
        load.start()
    for at, ins in ((0, row_in), (16, col_in)):
        for rel in range(2):
            for slot in range(8):
                total = ins[0][rel * 8 + slot : rel * 8 + slot + 1, :]
                for step in (1, 2, 3):
                    src = rel * 8 + (slot - 2 * step) % 8
                    total = total + ins[step][src : src + 1, :]
                dst = at + rel * 8 + slot
                inv[dst : dst + 1, :] = 1.0 / total
    inv_out[0:1, :] = inv[0:1, :]
    inv_out[1:2, :] = inv[16:17, :]
    inv_out[2:8, :] = jnp.zeros((6, DOCS), F32)
    stores = []

    def put(i, ref, grad):
        out_s[i] = grad.astype(BF)
        stores.append(pltpu.make_async_copy(out_s.at[i], ref, out_sems.at[i]))
        stores[-1].start()

    for m in range(4):
        for load in e_loads[3 * m : 3 * m + 3]:
            load.wait()
        for a in (2 * m, 2 * m + 1):
            rows = slice(a * DOCS, (a + 1) * DOCS)
            far = slice((8 + a) * DOCS, (9 + a) * DOCS)
            col_own = jnp.broadcast_to(inv[a : a + 1, :], (DOCS, DOCS)).T
            col_oth = jnp.broadcast_to(inv[8 + a : 9 + a, :], (DOCS, DOCS)).T
            for b in range(8):
                near_key = inv[16 + b : 17 + b, :]
                far_key = inv[24 + b : 25 + b, :]
                keys = slice(b * DOCS, (b + 1) * DOCS)
                keys_far = slice((8 + b) * DOCS, (9 + b) * DOCS)
                w1 = (e_s[0, rows, keys].astype(F32) * (col_own + near_key)).astype(BF)
                w2 = (e_s[1, rows, keys].astype(F32) * (col_own + far_key)).astype(BF)
                w3 = (e_s[2, rows, keys].astype(F32) * (col_oth + near_key)).astype(BF)
                wq[rows, keys] = w1
                wq[rows, keys_far] = w2
                wk[rows, keys] = w1
                wk[far, keys] = w3
        if m == 0:
            for load in k_loads:
                load.wait()
            for load in e_loads[3:] + q_loads:
                load.start()
        put(m, q_out[m], dot(wq[m * 256 : (m + 1) * 256, :], k_s[...]) * TAU_INV)
    for load in q_loads:
        load.wait()
    for m in range(4):
        put(4 + m, k_out[m], t_dot(wk[:, m * 256 : (m + 1) * 256], q_s[...]) * TAU_INV)
    for store in stores:
        store.wait()


def grads(k_near, k_far, e_own, mix, mix_far, row_in, col_in):
    return pl.pallas_call(
        grads_body,
        in_specs=[ANY] * 13 + [VMEM] * 8,
        out_specs=[ANY] * 8 + [VMEM],
        out_shape=[sds((256, EMB), BF)] * 8 + [sds((8, DOCS), F32)],
        scratch_shapes=[
            pltpu.VMEM((16 * DOCS, EMB), BF),
            pltpu.VMEM((16 * DOCS, EMB), BF),
            pltpu.VMEM((3, 8 * DOCS, 8 * DOCS), BF),
            pltpu.VMEM((8 * DOCS, 16 * DOCS), BF),
            pltpu.VMEM((16 * DOCS, 8 * DOCS), BF),
            pltpu.VMEM((8, 256, EMB), BF),
            pltpu.VMEM((32, DOCS), F32),
            pltpu.SemaphoreType.DMA((24,)),
            pltpu.SemaphoreType.DMA((8,)),
        ],
        compiler_params=params(),
    )(*k_near, *k_far, e_own, mix, mix_far, *row_in, *col_in)


def half_block(which):
    return pl.BlockSpec((DOCS, EMB), lambda i: (which, 0))


def pass_body(*refs):
    for ins, out in ((refs[0:4], refs[8]), (refs[4:8], refs[9])):
        out[...] = sum(ref[...].astype(F32) for ref in ins).astype(BF)


def pass_on(query_in, key_in):
    return pl.pallas_call(
        pass_body,
        grid=(1,),
        in_specs=[half_block(1)] * 8,
        out_specs=[half_block(0)] * 2,
        out_shape=[sds((DOCS, EMB), BF)] * 2,
        compiler_params=params(),
    )(*query_in, *key_in)


def keep_body(*refs):
    q_parts, k_parts = refs[0:4], refs[4:8]
    q_unit, paired, q_perm, pos, inv, q_out, k_out = refs[8:15]
    hot = one_hot(pos[...])
    same = eye()
    pair = paired[...].astype(F32)
    score = jnp.sum(q_unit[...].astype(F32) * pair, axis=1, keepdims=True) * TAU_INV
    expo = jnp.exp(score)
    inv_r = jnp.sum(same * inv[0:1, :], axis=1, keepdims=True)
    inv_c = jnp.sum(hot * inv[1:2, :], axis=1, keepdims=True)
    weight = expo * inv_r + expo * inv_c - 2.0
    weight_k = jnp.sum(same * jnp.sum(hot * weight, axis=0, keepdims=True), axis=1, keepdims=True)
    for parts, w, pair_rows, out in (
        (q_parts, weight, pair, q_out),
        (k_parts, weight_k, q_perm[...].astype(F32), k_out),
    ):
        out[...] = sum(ref[...].astype(F32) for ref in parts) + (w * TAU_INV) * pair_rows


def keep(query_in, key_in, q_unit, paired, q_perm, pos, inv):
    return pl.pallas_call(
        keep_body,
        grid=(1,),
        in_specs=[half_block(0)] * 11 + [VMEM] * 2,
        out_specs=[half_block(0)] * 2,
        out_shape=[sds((DOCS, EMB), F32)] * 2,
        compiler_params=params(),
    )(*query_in, *key_in, q_unit, paired, q_perm, pos, inv)


def back_body(q_keep, q_got, k_keep, k_got, q_raw, k_raw, out):
    for kept, got, raw, start in ((q_keep, q_got, q_raw, 0), (k_keep, k_got, k_raw, DOCS)):
        grad = kept[...] + got[...].astype(F32)
        exact, scale = unit_of(raw[...])
        inner = jnp.sum(exact * grad, axis=1, keepdims=True)
        out[start : start + DOCS, :] = (scale * (grad - exact * inner)).astype(BF)


def back(*args):
    return pl.pallas_call(
        back_body,
        in_specs=[VMEM] * 6,
        out_specs=VMEM,
        out_shape=sds((2 * DOCS, EMB), BF),
        compiler_params=params(),
    )(*args)


def contract_body(*refs):
    b_in, h_all, h_in, where, out = refs[0:4], refs[4], refs[5:8], refs[8], refs[9]
    h_s, b_s, o_s, sems, out_sems = refs[10:15]
    sources = (h_all.at[where[0]],) + tuple(h_in)
    loads = []
    for i in range(4):
        loads.append((b_in[i], b_s.at[pl.ds(i * 256, 256)]))
        loads.append((sources[i], h_s.at[:, pl.ds(i * 256, 256)]))
    loads = [pltpu.make_async_copy(s, d, sems.at[i]) for i, (s, d) in enumerate(loads)]
    for load in loads:
        load.start()
    for load in loads:
        load.wait()
    stores = []
    for m in range(4):
        rows = pl.ds(m * 256, 256)
        o_s[rows, :] = dot(h_s[rows, :], b_s[...]).astype(BF)
        stores.append(pltpu.make_async_copy(o_s.at[rows], out.at[rows], out_sems.at[m]))
        stores[-1].start()
    for store in stores:
        store.wait()


def contract(b_in, h_all, h_in, where):
    return pl.pallas_call(
        contract_body,
        in_specs=[ANY] * 8 + [SMEM],
        out_specs=ANY,
        out_shape=sds((1024, EMB), BF),
        scratch_shapes=[
            pltpu.VMEM((1024, 1024), BF),
            pltpu.VMEM((1024, EMB), BF),
            pltpu.VMEM((1024, EMB), BF),
            pltpu.SemaphoreType.DMA((8,)),
            pltpu.SemaphoreType.DMA((4,)),
        ],
        compiler_params=params(),
    )(*b_in, h_all, *h_in, where)


def flip_slots(value):
    return value[:, ::-1]


def to_owners(parts, move):
    return [parts[0]] + [move(parts[(4 - step) % 4], step, 0) for step in (1, 2, 3)]


def local(hid_query, hid_key, projection, tile_rows, tile_cols, tile_count, positive):
    row_index = lax.axis_index("row")
    col_index = lax.axis_index("col")
    core_index = lax.axis_index("dp")
    x, z_hi = row_index // 2, row_index % 2
    y, z_lo = col_index // 2, col_index % 2
    quarter = z_lo * 2 + core_index

    q_unit, k_unit, q_raw, k_raw = project(hid_query, hid_key, projection)
    k_flip = move_key(k_unit, 0, 1)
    q_flip = move_query(q_unit, 0, 1)

    pos = (positive - ((row_index * 8 + col_index) * 2 + core_index) * DOCS).reshape(DOCS, 1)
    paired, q_perm, pos_rows = pair_up(q_unit, k_unit, pos)
    turned = jnp.concatenate([hid_query, hid_key], axis=0).T.reshape(4, 2, 4, 2, 2, 32, 256)
    turned = turned.transpose(3, 4, 0, 1, 2, 5, 6).reshape(4, 1024, 256)
    h_flip = lax.dynamic_index_in_dim(turned, quarter ^ 2, 0, keepdims=False)
    h_both = lax.dynamic_index_in_dim(turned, quarter ^ 3, 0, keepdims=False)
    h_core = lax.dynamic_index_in_dim(turned, quarter ^ 1, 0, keepdims=False)
    entry_rows = tile_rows[0, 0]
    entry_cols = tile_cols[0, 0]
    used = jnp.arange(entry_rows.shape[0], dtype=jnp.int32) < tile_count[0, 0]
    slot_rows = ((y - entry_rows // 2) % 4) * 2 + (z_lo ^ (entry_rows % 2))
    slot_cols = ((x - entry_cols // 2) % 4) * 2 + (z_hi ^ (entry_cols % 2))
    eight = jnp.arange(8, dtype=jnp.int32)
    hit = (
        (slot_rows[:, None, None] == eight[None, :, None])
        & (slot_cols[:, None, None] == eight[None, None, :])
        & used[:, None, None]
    )
    mask = jnp.any(hit, axis=0).astype(F32)

    k_flip, q_flip, pos, paired, q_perm, pos_rows, turned, h_flip, h_both, h_core, mask = (
        lax.optimization_barrier(
            (k_flip, q_flip, pos, paired, q_perm, pos_rows, turned, h_flip, h_both, h_core, mask)
        )
    )
    k_pair = jnp.concatenate([k_unit, k_flip], axis=0)
    q_pair = jnp.concatenate([q_unit, q_flip], axis=0)
    k_pair, q_pair = lax.optimization_barrier((k_pair, q_pair))
    k1 = move_key(k_pair, 1, 0)
    q1 = move_query(q_pair, 1, 0)
    k3 = move_key(k_pair, 3, 0)
    q3 = move_query(q_pair, 3, 0)
    k_far = swap(k_pair)
    k1, q1, k3, q3, k_far = lax.optimization_barrier((k1, q1, k3, q3, k_far))
    k_own = [
        k_pair,
        k1,
        move_key(k1[:DOCS], 1, 0),
        move_key(k3[DOCS:], 3, 0),
        k3,
    ]
    q_own = [
        q_pair,
        q1,
        move_query(q1[:DOCS], 1, 0),
        move_query(q3[DOCS:], 3, 0),
        q3,
    ]
    k1_far = swap(k1)
    k1_far, k3_late = lax.optimization_barrier((k1_far, k3))
    k3_far = swap(k3_late)
    k_oth = [k_far, k1_far, swap(k_own[2]), swap(k_own[3]), k3_far]

    h_flip, *blocks = lax.optimization_barrier((h_flip, *q_own, *k_oth))
    q_own, k_oth = blocks[:5], blocks[5:]
    h_flip = move_query(h_flip, 0, 1)
    e_own, mix, sums = scores(q_own, k_own, k_oth, mask, pos_rows)
    far = swap(sums)
    far, mix, h_flip = lax.optimization_barrier((far, mix, h_flip))
    mix_far = swap(mix)
    row_part = jnp.concatenate([sums[:8], far[:8]], axis=0).reshape(8, 2, DOCS)
    col_part = sums[8:] + jnp.concatenate([far[16:], far[8:16]], axis=0)
    col_part = col_part.reshape(8, 2, DOCS)
    row_part = row_part + flip_slots(move_query(row_part, 0, 1))
    col_part = col_part + flip_slots(move_key(col_part, 0, 1))
    row_part = row_part.reshape(16, DOCS)
    col_part = col_part.reshape(16, DOCS)
    row_got = [row_part] + [move_query(row_part, step, 0) for step in (1, 2, 3)]
    col_got = [col_part] + [move_key(col_part, step, 0) for step in (1, 2, 3)]

    h_both, h_core, *got = lax.optimization_barrier((h_both, h_core, *row_got, *col_got))
    h_both = move_query(h_both, 0, 1)
    parts = grads(k_own, k_oth, e_own, mix, mix_far, got[:4], got[4:])
    inv = parts[8]
    query_in = to_owners(parts[:4], move_query)
    key_in = to_owners(parts[4:8], move_key)
    h_both, *query_in = lax.optimization_barrier((h_both, *query_in))
    q_send, k_send = pass_on(query_in, key_in)
    q_got = move_query(q_send, 0, 1)
    k_got = move_key(k_send, 0, 1)
    q_keep, k_keep = keep(query_in, key_in, q_unit, paired, q_perm, pos, inv)
    b_own = back(q_keep, q_got, k_keep, k_got, q_raw, k_raw)
    b_flip = move_query(b_own, 0, 1)
    out = contract(
        [b_own, swap(b_own), b_flip, swap(b_flip)],
        turned,
        [swap(h_core), h_flip, swap(h_both)],
        quarter.reshape(1).astype(jnp.int32),
    )
    out = lax.all_to_all(out, ("row", "col"), 0, 0, tiled=True, axis_index_groups=PLANES)
    return jnp.sum(out.reshape(32, 32, EMB).astype(F32), axis=0)


def solution(mesh):
    return jax.shard_map(
        local,
        mesh=mesh,
        in_specs=(
            P(("row", "col", "dp"), None),
            P(("row", "col", "dp"), None),
            P(),
            P("row", "col", None),
            P("row", "col", None),
            P("row", "col"),
            P(("row", "col", "dp")),
        ),
        out_specs=P(("row", "col", "dp"), None),
        check_vma=False,
    )
```
